32 devices in a mesh: fsdp: 4 (over y, x), ctx: 2 (over core), tp: 4 (over z).
Axes of the slice: x: 2, y: 2, z: 4, core: 2. Of those that a mesh axis runs over, the one named last changes fastest.
Arguments:
- tokens: bfloat16 [12288, 1024], P(('fsdp', 'ctx', 'tp')), may hold values from -6 to 6
- out_grad: bfloat16 [12288, 1024], P(('fsdp', 'ctx', 'tp')), may hold values from -6 to 6
- block_slot: int32 [4, 6], P('fsdp'), may hold values from 0 to 5, each once within a row
- attn_gain: float32 [1024], replicated, may hold values from 0.5 to 1.5
- ffn_gain: float32 [1024], replicated, may hold values from 0.5 to 1.5
- query_gain: float32 [128], replicated, may hold values from 1 to 2
- key_norm_gain: float32 [128], replicated, may hold values from 1 to 2
- w_query: bfloat16 [1024, 2048], P(('fsdp', 'ctx'), 'tp'), may hold values from -0.1875 to 0.1875
- key_weight: bfloat16 [1024, 1024], P(('fsdp', 'ctx'), 'tp'), may hold values from -0.1875 to 0.1875
- value_weight: bfloat16 [1024, 1024], P(('fsdp', 'ctx'), 'tp'), may hold values from -0.1875 to 0.1875
- w_out: bfloat16 [2048, 1024], P('tp', ('fsdp', 'ctx')), may hold values from -0.5 to 0.5
- w_gate: bfloat16 [1024, 3072], P(('fsdp', 'ctx'), 'tp'), may hold values from -0.1875 to 0.1875
- w_up: bfloat16 [1024, 3072], P(('fsdp', 'ctx'), 'tp'), may hold values from -0.1875 to 0.1875
- w_down: bfloat16 [3072, 1024], P('tp', ('fsdp', 'ctx')), may hold values from -0.21875 to 0.21875
Outputs:
- out: bfloat16 [12288, 1024], P(('fsdp', 'ctx', 'tp'))
- input_grad: float32 [12288, 1024], P(('fsdp', 'ctx', 'tp'))
- attn_gain_grad: float32 [1024], replicated
- ffn_gain_grad: float32 [1024], replicated
- query_gain_grad: float32 [128], replicated
- key_gain_grad: float32 [128], replicated
- w_query_grad: float32 [1024, 2048], P(('fsdp', 'ctx'), 'tp')
- w_key_grad: float32 [1024, 1024], P(('fsdp', 'ctx'), 'tp')
- w_value_grad: float32 [1024, 1024], P(('fsdp', 'ctx'), 'tp')
- w_out_grad: float32 [2048, 1024], P('tp', ('fsdp', 'ctx'))
- w_gate_grad: float32 [1024, 3072], P(('fsdp', 'ctx'), 'tp')
- w_up_grad: float32 [1024, 3072], P(('fsdp', 'ctx'), 'tp')
- w_down_grad: float32 [3072, 1024], P('tp', ('fsdp', 'ctx'))
The draws below stay inside these ranges and needn't reach their ends.
Inputs may be any that keep to these rules, and one draw needn't show every extreme that they name: `block_slot`: each row names every block of its group once; blocks under 4 are the prompt's in order, the others are continuations.
All inputs are finite; a program needn't handle non-finite values.
Results may differ from the reference program's by a relative error of at most 0.024.
Values may be sent and summed in bfloat16 or wider, within the bound.
A program may use at most 128 MiB of HBM per device.

```python
import jax
import jax.numpy as jnp
from jax import lax

MODEL_WIDTH = 1024
QUERY_HEADS = 16
KEY_VALUE_HEADS = 8
HEAD_WIDTH = 128
FF = 3072
BLOCK_TOKENS = 512
PROMPT = 2048
PBLOCKS = 4
BLOCKS = 6
GROUPS = 4
TOKENS = 12288


def block_levels(rng, shape, split, smallest, high):
    loudness, own = 1.0, jax.random.fold_in(rng, 6)
    for dim, parts in split:
        heights = jnp.exp(jax.random.uniform(jax.random.fold_in(own, dim), (parts,), jnp.float32, smallest / len(split), high / len(split)))
        loudness = loudness * jnp.repeat(heights, shape[dim] // parts).reshape([-1 if axis == dim else 1 for axis in range(len(shape))])
    return loudness


def normal_values(stream_key, extent, scale, bound, cuts=(), kind=jnp.bfloat16):
    entries = scale * jax.random.normal(stream_key, extent, jnp.float32)
    if cuts:
        entries = entries * block_levels(stream_key, extent, cuts, -0.22, 0.18)
    return jnp.clip(entries, -bound, bound).astype(kind)


def setup_inputs(seed: int = 0) -> dict:
    keys = jax.random.split(jax.random.key(seed), 15)
    tokens = normal_values(keys[0], (TOKENS, MODEL_WIDTH), 1.0, 6.0, ((0, 32),))
    out_grad = normal_values(keys[1], (TOKENS, MODEL_WIDTH), 1.0, 6.0, ((0, 32),))
    block_slot = jax.vmap(lambda own: jax.random.permutation(own, BLOCKS))(jax.random.split(keys[2], GROUPS)).reshape((GROUPS, BLOCKS)).astype(jnp.int32)
    attn_gain = jnp.clip(jax.random.uniform(keys[3], (MODEL_WIDTH,), jnp.float32, 0.5, 1.5), 0.5, 1.5)
    ffn_gain = jnp.clip(jax.random.uniform(keys[4], (MODEL_WIDTH,), jnp.float32, 0.5, 1.5), 0.5, 1.5)
    query_gain = jnp.clip(jax.random.uniform(keys[5], (HEAD_WIDTH,), jnp.float32, 1.0, 2.0), 1.0, 2.0)
    key_norm_gain = jnp.clip(jax.random.uniform(keys[6], (HEAD_WIDTH,), jnp.float32, 1.0, 2.0), 1.0, 2.0)
    w_query = normal_values(keys[7], (MODEL_WIDTH, QUERY_HEADS * HEAD_WIDTH), MODEL_WIDTH ** -0.5, 0.1875, ((0, 8), (1, 4)))
    key_weight = normal_values(keys[8], (MODEL_WIDTH, KEY_VALUE_HEADS * HEAD_WIDTH), MODEL_WIDTH ** -0.5, 0.1875, ((0, 8), (1, 4)))
    value_weight = normal_values(keys[9], (MODEL_WIDTH, KEY_VALUE_HEADS * HEAD_WIDTH), MODEL_WIDTH ** -0.5, 0.1875, ((0, 8), (1, 4)))
    w_out = normal_values(keys[10], (QUERY_HEADS * HEAD_WIDTH, MODEL_WIDTH), (QUERY_HEADS * HEAD_WIDTH // 16) ** -0.5, 0.5, ((0, 4), (1, 8)))
    w_gate = normal_values(keys[11], (MODEL_WIDTH, FF), MODEL_WIDTH ** -0.5, 0.1875, ((0, 8), (1, 4)))
    w_up = normal_values(keys[12], (MODEL_WIDTH, FF), MODEL_WIDTH ** -0.5, 0.1875, ((0, 8), (1, 4)))
    w_down = normal_values(keys[13], (FF, MODEL_WIDTH), (FF // 4) ** -0.5, 0.21875, ((0, 4), (1, 8)))
    return dict(tokens=tokens, out_grad=out_grad, block_slot=block_slot, attn_gain=attn_gain, ffn_gain=ffn_gain, query_gain=query_gain, key_norm_gain=key_norm_gain, w_query=w_query, key_weight=key_weight, value_weight=value_weight, w_out=w_out, w_gate=w_gate, w_up=w_up, w_down=w_down)


@jax.custom_vjp
def lowered(v):
    return lax.optimization_barrier(v.astype(jnp.bfloat16)).astype(jnp.float32)

@jax.custom_vjp
def low_back(v):
    return v

def low_keep(v):
    return (lowered(v), None)

def low_pass(kept, grad):
    return (grad,)

def back_keep(v):
    return (v, None)

def back_low(kept, grad):
    return (lowered(grad),)
lowered.defvjp(low_keep, low_pass)
low_back.defvjp(back_keep, back_low)
eps_norm = 1e-06
rope_base = 1000000.0
highest = lax.Precision.HIGHEST

def normed_rows(value):
    return value * lax.rsqrt(lax.optimization_barrier(jnp.mean(value * value, axis=-1, keepdims=True)) + eps_norm)

def rotate_half(value, cosine_table, sine_table):
    half = value.shape[-1] // 2
    turned = jnp.concatenate([-value[..., half:], value[..., :half]], axis=-1)
    return value * cosine_table + turned * sine_table

def rope_tables(places):
    freqs = rope_base ** (-(jnp.arange(0, HEAD_WIDTH, 2).astype(jnp.float32) / HEAD_WIDTH))
    angles = places.astype(jnp.float32)[:, None] * freqs[None, :]
    angles = jnp.concatenate([angles, angles], axis=-1)
    return (jnp.cos(angles)[:, None, :], jnp.sin(angles)[:, None, :])

def block_places(block_ids):
    offsets = jnp.arange(BLOCK_TOKENS, dtype=jnp.int32)
    in_prompt = block_ids < PBLOCKS
    start = jnp.where(in_prompt, block_ids * BLOCK_TOKENS, PROMPT).astype(jnp.int32)
    places = (start[:, None] + offsets[None, :]).reshape(-1)
    order = jnp.where(in_prompt, 0, block_ids - PBLOCKS + 1).astype(jnp.int32)
    groups = jnp.broadcast_to(order[:, None], (block_ids.shape[0], BLOCK_TOKENS)).reshape(-1)
    return (places, groups)

def attend(query_rows, key_rows, value_rows, q_pos, q_seq, k_pos, k_seq):
    grouped_rows = query_rows.reshape(BLOCK_TOKENS, KEY_VALUE_HEADS, QUERY_HEADS // KEY_VALUE_HEADS, HEAD_WIDTH)
    scores = jnp.einsum('qkrd,tkd->krqt', grouped_rows, key_rows, precision=highest) * HEAD_WIDTH ** (-0.5)
    scores = low_back(scores)
    allowed = (k_pos[None, :] <= q_pos[:, None]) & ((k_seq[None, :] == q_seq[:, None]) | (k_seq[None, :] == 0))
    scores = jnp.where(allowed, scores, -1e+30)
    peak = lax.optimization_barrier(jnp.max(scores, axis=-1, keepdims=True))
    weights = jnp.exp(scores - peak)
    probs = lowered(weights / lax.optimization_barrier(jnp.sum(weights, axis=-1, keepdims=True)))
    mixed = jnp.einsum('krqt,tkd->qkrd', probs, value_rows, precision=highest)
    return mixed.reshape(BLOCK_TOKENS, QUERY_HEADS * HEAD_WIDTH)

def layer(inputs, attn_gain, ffn_gain, query_gain, key_norm_gain, w_query, key_weight, value_weight, w_out, w_gate, w_up, w_down, places, groups):
    row_count = inputs.shape[0]
    normed = lowered(normed_rows(inputs) * attn_gain)
    query_rows = low_back(jnp.dot(normed, w_query, precision=highest))
    key_rows = low_back(jnp.dot(normed, key_weight, precision=highest))
    value_rows = lowered(low_back(jnp.dot(normed, value_weight, precision=highest)))
    cosine_table, sine_table = rope_tables(places)
    query_rows = lowered(rotate_half(normed_rows(query_rows.reshape(row_count, QUERY_HEADS, HEAD_WIDTH)) * query_gain, cosine_table, sine_table))
    key_rows = lowered(rotate_half(normed_rows(key_rows.reshape(row_count, KEY_VALUE_HEADS, HEAD_WIDTH)) * key_norm_gain, cosine_table, sine_table))
    value_rows = value_rows.reshape(row_count, KEY_VALUE_HEADS, HEAD_WIDTH)
    nblocks = row_count // BLOCK_TOKENS

    def one_block(item):
        return attend(item[0], key_rows, value_rows, item[1], item[2], places, groups)
    mixed = lax.map(jax.checkpoint(one_block), (query_rows.reshape(nblocks, BLOCK_TOKENS, QUERY_HEADS, HEAD_WIDTH), places.reshape(nblocks, BLOCK_TOKENS), groups.reshape(nblocks, BLOCK_TOKENS)))
    mixed = lowered(low_back(mixed.reshape(row_count, QUERY_HEADS * HEAD_WIDTH)))
    attn = low_back(jnp.dot(mixed, w_out, precision=highest))
    state = inputs + attn
    ffn_in = lowered(normed_rows(state) * ffn_gain)
    gate = low_back(jnp.dot(ffn_in, w_gate, precision=highest))
    up_val = low_back(jnp.dot(ffn_in, w_up, precision=highest))
    hidden = lowered(jax.nn.silu(gate) * up_val)
    ffn = low_back(jnp.dot(hidden, w_down, precision=highest))
    return state + ffn

def reference(tokens, out_grad, block_slot, attn_gain, ffn_gain, query_gain, key_norm_gain, w_query, key_weight, value_weight, w_out, w_gate, w_up, w_down):
    params = (attn_gain.astype(jnp.float32), ffn_gain.astype(jnp.float32), query_gain.astype(jnp.float32), key_norm_gain.astype(jnp.float32), w_query.astype(jnp.float32), key_weight.astype(jnp.float32), value_weight.astype(jnp.float32), w_out.astype(jnp.float32), w_gate.astype(jnp.float32), w_up.astype(jnp.float32), w_down.astype(jnp.float32))
    span = BLOCKS * BLOCK_TOKENS
    x_groups = tokens.astype(jnp.float32).reshape(GROUPS, span, MODEL_WIDTH)
    dy_groups = out_grad.astype(jnp.float32).reshape(GROUPS, span, MODEL_WIDTH)

    def one_group(totals, item):
        x_part, dy_part, block_ids = item
        places, groups = block_places(block_ids)

        def apply(x_in, *weights):
            return layer(x_in, *weights, places, groups)
        result, pull = jax.vjp(apply, x_part, *params)
        grads = pull(dy_part)
        totals = tuple((total + grad for total, grad in zip(totals, grads[1:])))
        return (totals, (result.astype(jnp.bfloat16), grads[0]))
    zeros = tuple((jnp.zeros_like(param) for param in params))
    totals, (results, input_grads) = lax.scan(one_group, zeros, (x_groups, dy_groups, block_slot))
    return (results.reshape(TOKENS, MODEL_WIDTH), input_grads.reshape(TOKENS, MODEL_WIDTH), totals[0], totals[1], totals[2], totals[3], totals[4], totals[5], totals[6], totals[7], totals[8], totals[9], totals[10])
```

```python
import math
import jax
import jax.numpy as jnp
from jax import lax
from jax.experimental import pallas as pl
from jax.experimental.pallas import tpu as pltpu
from jax.sharding import PartitionSpec as P

HEAD = 128
BLOCK = 512
PBLOCKS = 4
BLOCKS = 6
EPS = 1e-6
ROPE_BASE = 1e6
MESH = pl.DeviceIdType.MESH
F32, BF16 = jnp.float32, jnp.bfloat16
LOG2E = 1.4426950408889634
QSCALE = HEAD ** -0.5 * LOG2E
VMEM_SPEC = pl.BlockSpec(memory_space=pltpu.VMEM)
ANY_SPEC = pl.BlockSpec(memory_space=pl.ANY)
SMEM_SPEC = pl.BlockSpec(memory_space=pltpu.SMEM)
VMEM_LIMIT = 60 * 2**20


def dot(a, b, dims):
    return lax.dot_general(a, b, (dims, ((), ())), preferred_element_type=F32)


NN = ((1,), (0,))
NT = ((1,), (1,))
TN = ((0,), (0,))


def flip(f, mask):
    bit = 1
    while bit <= mask:
        if mask & bit:
            f = f + bit - 2 * bit * lax.rem(lax.div(f, bit), 2)
        bit *= 2
    return f


def remote(src, dst, send, recv, **where):
    return pltpu.make_async_remote_copy(
        src_ref=src, dst_ref=dst, send_sem=send, recv_sem=recv,
        device_id=where, device_id_type=MESH)


def pick(index, values):
    out = jnp.int32(values[-1])
    for k in range(len(values) - 1):
        out = jnp.where(index == k, jnp.int32(values[k]), out)
    return out


def near_order(n):
    return [sorted(range(n), key=lambda s: (abs(s - z), s)) for z in range(n)]


def bit_orders(fs):
    bits = [1 << b for b in range(fs.bit_length() - 1)]
    return bits, bits[::-1]


def combos(bits):
    out = [0]
    for b in bits:
        out = out + [m + b for m in out]
    return out


def plane_copies(half, stage, fs, f, view, ssem, rsem):
    order = bit_orders(fs)[half]
    partner = flip(f, order[stage])
    base = (1 << stage) - 1
    out = []
    for m, mask in enumerate(combos(order[:stage])):
        g = flip(f, mask)
        out.append(remote(view(g), view(g), ssem.at[base + m], rsem.at[base + m], fsdp=partner))
    return out
def head_norm_rope(pre, gain, cos, sins):
    n = pre * lax.rsqrt(jnp.mean(pre * pre, axis=-1, keepdims=True) + EPS) * gain
    return n * cos + pltpu.roll(n, HEAD // 2, 1) * sins


def gather_kernel(dims, x_ref, dy_ref, gain_ref, wqkv_ref, wz_ref, cos_ref, sin_ref, qg_ref, kg_ref,
                  a_ref, q_ref, k_ref, v_ref, pre_ref, wall_ref, w_ref, dyp_ref,
                  zs, zr, cs, cr, ws, wr, ms, mr, ps, pr, ls):
    fs, nc, nz = dims
    f, c, z = lax.axis_index("fsdp"), lax.axis_index("ctx"), lax.axis_index("tp")
    o = 1 - c
    me = f * nc + c
    others = [(df, dc) for df in range(fs) for dc in range(nc) if (df, dc) != (0, 0)]

    barrier = pltpu.get_barrier_semaphore()
    for df, dc in others:
        pl.semaphore_signal(barrier, inc=1, device_id={"fsdp": lax.rem(f + df, fs), "ctx": lax.rem(c + dc, nc)}, device_id_type=MESH)

    @pl.when(z > 0)
    def _():
        pl.semaphore_signal(barrier, inc=1, device_id={"tp": z - 1}, device_id_type=MESH)

    @pl.when(z < nz - 1)
    def _():
        pl.semaphore_signal(barrier, inc=1, device_id={"tp": z + 1}, device_id_type=MESH)
    own_w = pltpu.make_async_copy(wz_ref.at[c], w_ref.at[z, f, c], ls.at[0])
    own_w.start()
    own_dy = pltpu.make_async_copy(dy_ref, dyp_ref.at[c], ls.at[1])
    own_dy.start()
    x = x_ref[...].astype(F32)
    a_ref[c * nz + z] = (x * lax.rsqrt(jnp.mean(x * x, axis=-1, keepdims=True) + EPS) * gain_ref[...]).astype(BF16)
    wall_ref[me] = wqkv_ref[c]
    pl.semaphore_wait(barrier, len(others) + jnp.where(z > 0, 1, 0) + jnp.where(z < nz - 1, 1, 0))

    row = a_ref.at[c * nz + z]
    up = remote(row, row, zs.at[z], zr.at[z], tp=jnp.minimum(z + 1, nz - 1))
    down = remote(row, row, zs.at[nz], zr.at[z], tp=jnp.maximum(z - 1, 0))
    pl.when(z < nz - 1)(up.start)
    pl.when(z > 0)(down.start)
    across = remote(row, row, cs.at[z], cr.at[z], ctx=o)
    across.start()
    for i, (df, dc) in enumerate(others):
        tf, tc = lax.rem(f + df, fs), lax.rem(c + dc, nc)
        remote(wqkv_ref.at[tc], wall_ref.at[me], ws.at[i], wr.at[me], fsdp=tf, ctx=tc).start()
    half = remote(wz_ref.at[o], w_ref.at[z, f, c], ms.at[0], mr.at[0], ctx=o)
    half.start()
    dyc = remote(dy_ref, dyp_ref.at[c], ms.at[1], mr.at[1], ctx=o)
    dyc.start()

    def plane(half_index, stage):
        return plane_copies(half_index, stage, fs, f, lambda g: w_ref.at[z, g, half_index], ps.at[half_index], pr.at[half_index])
    stages = fs.bit_length() - 1

    own_w.wait()
    remote(wz_ref.at[0], w_ref.at[z, f, o], ms.at[0], mr.at[0], ctx=o).wait_recv()
    for hi in range(2):
        for cp in plane(hi, 0):
            cp.start()
    q_cols = q_ref.shape[-1]

    def project(s):
        y = dot(a_ref[s], wall_ref[...].reshape(-1, wall_ref.shape[2]), NN)
        pre_ref[s] = y[:, :q_cols + HEAD].astype(BF16)
        cos, sins = cos_ref[s], sin_ref[s]
        for h in range(q_cols // HEAD):
            q_ref[s, :, h * HEAD:(h + 1) * HEAD] = (head_norm_rope(y[:, h * HEAD:(h + 1) * HEAD], qg_ref[...], cos, sins) * QSCALE).astype(BF16)
        k_ref[s] = head_norm_rope(y[:, q_cols:q_cols + HEAD], kg_ref[...], cos, sins).astype(BF16)
        v_ref[s, :, :HEAD] = y[:, q_cols + HEAD:].astype(BF16)
        v_ref[s, :, HEAD:] = jnp.ones_like(v_ref[s, :, HEAD:])

    def take(hop):
        @pl.loop(0, 2 if hop == 0 else 4)
        def _(i):
            across_, way = (i, 0) if hop == 0 else (lax.rem(i, 2), lax.div(i, 2))
            src = z + (2 * way - 1) * hop

            @pl.when((src >= 0) & (src < nz))
            def _():
                s = jnp.where(across_ == 0, c, o) * nz + src

                @pl.when(across_ == 1)
                def _():
                    remote(a_ref.at[s], a_ref.at[s], cs.at[src], cr.at[src], ctx=o).wait_recv()
                project(s)

    for hop in range(1, nz):
        for way in range(2):
            src = z + (2 * way - 1) * hop

            @pl.when((src >= 0) & (src < nz))
            def _():
                part = a_ref.at[c * nz + src]
                remote(part, part, zs.at[src], zr.at[src], ctx=o).wait_recv()
                if way == 0:
                    pl.when(z < nz - 1)(remote(part, part, zs.at[src], zr.at[src], tp=jnp.minimum(z + 1, nz - 1)).start)
                else:
                    pl.when(z > 0)(remote(part, part, zs.at[src], zr.at[src], tp=jnp.maximum(z - 1, 0)).start)
                remote(part, part, cs.at[src], cr.at[src], ctx=o).start()
        if hop == 1:
            for i, (df, dc) in enumerate(others):
                src = lax.rem(f + df, fs) * nc + lax.rem(c + dc, nc)
                remote(wqkv_ref.at[0], wall_ref.at[src], ws.at[i], wr.at[src], ctx=o).wait_recv()
        take(hop - 1)
        stage = hop - 1
        if stage < stages:
            for hi in range(2):
                for cp in plane(hi, stage):
                    cp.wait_recv()
                if stage + 1 < stages:
                    for cp in plane(hi, stage + 1):
                        cp.start()
    take(nz - 1)
    for stage in range(nz - 1, stages):
        for hi in range(2):
            for cp in plane(hi, stage):
                cp.wait_recv()
            if stage + 1 < stages:
                for cp in plane(hi, stage + 1):
                    cp.start()
    for stage in range(stages):
        for hi in range(2):
            for cp in plane(hi, stage):
                cp.wait_send()
    for src in range(nz):
        @pl.when(((src <= z) & (z < nz - 1)) | ((src > z) & (z > 0)))
        def _():
            remote(row, row, zs.at[src], zr.at[src], ctx=o).wait_send()
        remote(row, row, cs.at[src], cr.at[src], ctx=o).wait_send()

    @pl.when(z > 0)
    def _():
        remote(row, row, zs.at[nz], zr.at[0], ctx=o).wait_send()
    for i in range(len(others)):
        remote(wqkv_ref.at[0], wall_ref.at[0], ws.at[i], wr.at[0], ctx=o).wait_send()
    half.wait_send()
    dyc.wait_send()
    own_dy.wait()
    remote(dy_ref, dyp_ref.at[o], ms.at[1], mr.at[1], ctx=o).wait_recv()


def gather_call(dims, x, dy, gain, wqkv, wz, cos, sin, qg, kg):
    fs, nc, nz = dims
    rows, width = x.shape
    ns = nc * nz
    cols = wqkv.shape[2]
    q_cols = cols - 2 * HEAD
    DMA = pltpu.SemaphoreType.DMA
    return pl.pallas_call(
        lambda *refs: gather_kernel(dims, *refs),
        out_shape=(
            jax.ShapeDtypeStruct((ns, rows, width), BF16),
            jax.ShapeDtypeStruct((ns, rows, q_cols), BF16),
            jax.ShapeDtypeStruct((ns, rows, HEAD), BF16),
            jax.ShapeDtypeStruct((ns, rows, 2 * HEAD), BF16),
            jax.ShapeDtypeStruct((ns, rows, q_cols + HEAD), BF16),
            jax.ShapeDtypeStruct((fs * nc,) + wqkv.shape[1:], BF16),
            jax.ShapeDtypeStruct((nz, fs, nc) + wz.shape[1:], BF16),
            jax.ShapeDtypeStruct((nc, rows, width), BF16),
        ),
        in_specs=[VMEM_SPEC, ANY_SPEC, VMEM_SPEC, VMEM_SPEC, ANY_SPEC] + [VMEM_SPEC] * 4,
        out_specs=(VMEM_SPEC,) * 6 + (ANY_SPEC, ANY_SPEC),
        scratch_shapes=[
            DMA((nz + 1,)), DMA((nz,)), DMA((nz,)), DMA((nz,)),
            DMA((fs * nc - 1,)), DMA((fs * nc,)), DMA((2,)), DMA((2,)),
            DMA((2, fs - 1)), DMA((2, fs - 1)), DMA((2,)),
        ],
        compiler_params=pltpu.CompilerParams(collective_id=0, has_side_effects=True, vmem_limit_bytes=VMEM_LIMIT),
        cost_estimate=pl.CostEstimate(flops=2 * ns * rows * width * cols, bytes_accessed=30 * 2**20, transcendentals=0),
    )(x, dy, gain, wqkv, wz, cos, sin, qg, kg)
def full_keys(qb):
    return min(qb, PBLOCKS)


def stack_heads(rows):
    return jnp.concatenate([rows[:, h * HEAD:(h + 1) * HEAD] for h in range(rows.shape[1] // HEAD)], axis=0)


def attend_kernel(dims, slot_ref, block_ref, q_ref, k_ref, v_ref, wi_ref, w_ref, or_ref, o_ref, l_ref,
                  ob, zs, zr, ps, pr, xs, xr):
    fs, nc, nz = dims
    f, c, z = lax.axis_index("fsdp"), lax.axis_index("ctx"), lax.axis_index("tp")
    rows = or_ref.shape[2]
    barrier = pltpu.get_barrier_semaphore()
    bits = bit_orders(fs)[0]
    for bit in bits:
        pl.semaphore_signal(barrier, inc=1, device_id={"fsdp": flip(f, bit)}, device_id_type=MESH)
    for dz in range(1, nz):
        pl.semaphore_signal(barrier, inc=1, device_id={"tp": lax.rem(z + dz, nz)}, device_id_type=MESH)
    pl.semaphore_wait(barrier, len(bits) + nz - 1)

    def up(src, sem):
        part = w_ref.at[src, f]
        return remote(part, part, zs.at[sem], zr.at[src], tp=jnp.minimum(z + 1, nz - 1))

    def down(src, sem):
        part = w_ref.at[src, f]
        return remote(part, part, zs.at[sem], zr.at[src], tp=jnp.maximum(z - 1, 0))
    pl.when(z < nz - 1)(up(z, z).start)
    pl.when(z > 0)(down(z, nz).start)
    stages = fs.bit_length() - 1

    def plane(src, hi, stage):
        return plane_copies(hi, stage, fs, f, lambda g: w_ref.at[src, g, hi], ps.at[src, hi], pr.at[src, hi])

    def each(hop, act):
        for way in range(2):
            src = z + (2 * way - 1) * hop

            @pl.when((src >= 0) & (src < nz))
            def _():
                act(way, src)

    def arrive(hop):
        def act(way, src):
            up(src, src).wait_recv()
            if way == 0:
                pl.when(z < nz - 1)(up(src, src).start)
            else:
                pl.when(z > 0)(down(src, src).start)
            for hi in range(2):
                for cp in plane(src, hi, 0):
                    cp.start()
        each(hop, act)

    def spread(hop, stage):
        def act(way, src):
            for hi in range(2):
                for cp in plane(src, hi, stage):
                    cp.wait_recv()
                if stage + 1 < stages:
                    for cp in plane(src, hi, stage + 1):
                        cp.start()
        each(hop, act)

    tri = lax.broadcasted_iota(jnp.int32, (BLOCK, BLOCK), 0) >= lax.broadcasted_iota(jnp.int32, (BLOCK, BLOCK), 1)
    heads = q_ref.shape[2] // HEAD
    for qb in range(BLOCKS):
        q2 = stack_heads(q_ref[slot_ref[qb]])

        def step(kb, acc):
            k = k_ref[slot_ref[kb]]
            v = v_ref[slot_ref[kb]]
            return acc + dot(jnp.exp2(dot(q2, k, NT)).astype(BF16), v, NN)
        acc = jnp.zeros((heads * BLOCK, 2 * HEAD), F32)
        if full_keys(qb):
            acc = lax.fori_loop(0, full_keys(qb), step, acc)
        k = k_ref[slot_ref[qb]]
        v = v_ref[slot_ref[qb]]
        s = dot(q2, k, NT)
        for h in range(heads):
            part = slice(h * BLOCK, (h + 1) * BLOCK)
            p = jnp.where(tri, jnp.exp2(s[part]), 0.0).astype(BF16)
            a = acc[part] + dot(p, v, NN)
            ob[qb, :, h * HEAD:(h + 1) * HEAD] = (a[:, :HEAD] / a[:, HEAD:]).astype(BF16)
            l_ref[qb, :, part] = jnp.log2(a[:, HEAD:]).T[0:8]
    for s in range(BLOCKS):
        o_ref[s * BLOCK:(s + 1) * BLOCK] = ob[block_ref[s]]

    def part_rows(side, zz):
        return pl.ds(pl.multiple_of((side * nz + zz) * rows, 128), rows)
    for dz in range(1, nz):
        to = lax.rem(z + dz, nz)
        for side in range(nc):
            remote(o_ref.at[part_rows(side, to)], or_ref.at[z, side], xs.at[dz, side], xr.at[z, side], tp=to).start()
    for side in range(nc):
        or_ref[z, side] = o_ref[part_rows(side, z)]
    arrive(1)
    for hop in range(1, nz):
        for stage in range(stages):
            if stage == 1 and hop + 1 < nz:
                arrive(hop + 1)
            spread(hop, stage)
        if stages < 2 and hop + 1 < nz:
            arrive(hop + 1)
    for dz in range(1, nz):
        src = lax.rem(z + dz, nz)
        for side in range(nc):
            cp = remote(o_ref.at[part_rows(side, 0)], or_ref.at[src, side], xs.at[dz, side], xr.at[src, side], tp=src)
            cp.wait_recv()
            cp.wait_send()
    for hop in range(1, nz):
        def left(way, src):
            if way == 0:
                pl.when(z < nz - 1)(up(src, src).wait_send)
            else:
                pl.when(z > 0)(down(src, src).wait_send)
            for hi in range(2):
                for stage in range(stages):
                    for cp in plane(src, hi, stage):
                        cp.wait_send()
        each(hop, left)
    pl.when(z < nz - 1)(up(z, z).wait_send)
    pl.when(z > 0)(down(z, nz).wait_send)


def attend_call(dims, slot, block, q, k, v, w, rows):
    fs, nc, nz = dims
    q_cols = q.shape[2]
    span = BLOCKS * BLOCK
    heads = q_cols // HEAD
    DMA = pltpu.SemaphoreType.DMA
    return pl.pallas_call(
        lambda *refs: attend_kernel(dims, *refs),
        out_shape=(
            jax.ShapeDtypeStruct(w.shape, BF16),
            jax.ShapeDtypeStruct((nz, nc, rows, q_cols), BF16),
            jax.ShapeDtypeStruct((span, q_cols), BF16),
            jax.ShapeDtypeStruct((BLOCKS, 8, heads * BLOCK), F32),
        ),
        in_specs=[SMEM_SPEC, SMEM_SPEC] + [VMEM_SPEC] * 3 + [ANY_SPEC],
        out_specs=(ANY_SPEC, VMEM_SPEC, VMEM_SPEC, VMEM_SPEC),
        scratch_shapes=[
            pltpu.VMEM((BLOCKS, BLOCK, q_cols), BF16),
            DMA((nz + 1,)), DMA((nz,)), DMA((nz, 2, fs - 1)), DMA((nz, 2, fs - 1)), DMA((nz, nc)), DMA((nz, nc)),
        ],
        input_output_aliases={5: 0},
        compiler_params=pltpu.CompilerParams(collective_id=1, has_side_effects=True, vmem_limit_bytes=VMEM_LIMIT),
        cost_estimate=pl.CostEstimate(flops=2 * 20 * BLOCK * BLOCK * heads * 3 * HEAD, bytes_accessed=30 * 2**20, transcendentals=0),
    )(slot, block, q, k, v, w)
def reduce_order(fs, hi):
    return bit_orders(fs)[hi][::-1]


def reduce_masks(fs, hi):
    return combos(reduce_order(fs, hi)[1:][::-1])


def first_copies(hi, fs, f, view, land, ssem, rsem):
    bit = reduce_order(fs, hi)[0]
    return [remote(view(flip(flip(f, m), bit)), land(i), ssem.at[i], rsem.at[i], fsdp=flip(f, bit))
            for i, m in enumerate(reduce_masks(fs, hi))]


def later_copies(hi, stage, fs, f, held, land, ssem, rsem):
    bit = reduce_order(fs, hi)[stage]
    keep = fs >> (stage + 1)
    base = fs // 2 - (fs >> stage)
    return [remote(held(keep + i), land(base + i), ssem.at[base + i], rsem.at[base + i], fsdp=flip(f, bit)) for i in range(keep)]


def add_low(a, b):
    return (a.astype(F32) + b.astype(F32)).astype(BF16)


def early_parts(nz):
    return (nz - 1, 0) if nz > 1 else (0,)


def late_parts(nz):
    return tuple(t for t in range(nz - 2, 0, -1))


def rope_norm_back(g, pre, gain, cos, sins):
    c = g * cos + pltpu.roll(g * sins, HEAD // 2, 1)
    inv = lax.rsqrt(jnp.mean(pre * pre, axis=-1, keepdims=True) + EPS)
    n = pre * inv
    sc = c * gain
    return inv * (sc - n * jnp.mean(sc * n, axis=-1, keepdims=True)), c * n


def attend_back_kernel(dims, slot_ref, block_ref, q_ref, k_ref, v_ref, o_ref, l_ref, do_ref, pre_ref, cos_ref, sin_ref,
                       qg_ref, kg_ref, re_ref, g_ref, d_ref, te_ref, tl_ref, qgg_ref, kgg_ref,
                       dq, dk, dv, dl, held, rl, rn, ls, fss, fsr, nss, nsr):
    fs, nc, nz = dims
    f = lax.axis_index("fsdp")
    heads = q_ref.shape[2] // HEAD
    early, late = early_parts(nz), late_parts(nz)
    stages = fs.bit_length() - 1
    barrier = pltpu.get_barrier_semaphore()
    bits = bit_orders(fs)[0]
    for bit in bits:
        pl.semaphore_signal(barrier, inc=1, device_id={"fsdp": flip(f, bit)}, device_id_type=MESH)
    own = []
    for e, t in enumerate(early + late):
        for hi in range(2):
            for i, m in enumerate(reduce_masks(fs, hi)):
                own.append(pltpu.make_async_copy(g_ref.at[t, flip(f, m), hi], held.at[e, hi, i], ls.at[e, hi, i]))
    for cp in own:
        cp.start()
    pl.semaphore_wait(barrier, len(bits))

    def first(j, hi):
        return first_copies(hi, fs, f, lambda g: g_ref.at[late[j], g, hi], lambda i: rl.at[j, hi, i], fss.at[j, hi], fsr.at[j, hi])

    def later(e, hi, stage):
        return later_copies(hi, stage, fs, f, lambda i: held.at[e, hi, i], lambda i: rn.at[e, hi, i], nss.at[e, hi], nsr.at[e, hi])
    for cp in own:
        cp.wait()
    for e in range(len(early)):
        for hi in range(2):
            held[e, hi] = add_low(held[e, hi], re_ref[e, hi])
            if stages > 1:
                for cp in later(e, hi, 1):
                    cp.start()
    for j in range(len(late)):
        for hi in range(2):
            for cp in first(j, hi):
                cp.start()

    key_at = lax.broadcasted_iota(jnp.int32, (BLOCK, BLOCK), 0)
    tri = key_at <= lax.broadcasted_iota(jnp.int32, (BLOCK, BLOCK), 1)
    dk[...] = jnp.zeros_like(dk)
    dv[...] = jnp.zeros_like(dv)
    for qb in range(BLOCKS):
        at = slot_ref[qb]
        q2, g2 = stack_heads(q_ref[at]), stack_heads(do_ref[at])
        dl[...] = jnp.broadcast_to(jnp.sum((g2.astype(F32) * stack_heads(o_ref[at]).astype(F32)).T, axis=0, keepdims=True), dl.shape)

        def pair(kb, diagonal):
            k = k_ref[slot_ref[kb]]
            v = v_ref[slot_ref[kb], :, :HEAD]
            p = jnp.exp2(dot(k, q2, NT) - l_ref[qb, 0:1])
            if diagonal:
                p = jnp.concatenate([jnp.where(tri, p[:, h * BLOCK:(h + 1) * BLOCK], 0.0) for h in range(heads)], axis=1)
            ds = (p * (dot(v, g2, NT) - dl[0:1])).astype(BF16)
            dv[kb] += dot(p.astype(BF16), g2, NN)
            dk[kb] += dot(ds, q2, NN)
            return dot(ds, k, TN)
        total = pair(qb, True)
        if full_keys(qb):
            total = lax.fori_loop(0, full_keys(qb), lambda kb, t: t + pair(kb, False), total)
        dq[qb] = total

    qgg_ref[...] = jnp.zeros_like(qgg_ref)
    kgg_ref[...] = jnp.zeros_like(kgg_ref)

    @pl.loop(0, BLOCKS)
    def _(s):
        b = block_ref[s]
        at = s
        cos, sins = cos_ref[at], sin_ref[at]
        qs = dq[b]
        for h in range(heads):
            back, part = rope_norm_back(qs[h * BLOCK:(h + 1) * BLOCK] * HEAD ** -0.5, pre_ref[at, :, h * HEAD:(h + 1) * HEAD].astype(F32), qg_ref[...], cos, sins)
            d_ref[at, :, h * HEAD:(h + 1) * HEAD] = back.astype(BF16)
            qgg_ref[...] += jnp.sum(part, axis=0, keepdims=True)
        back, part = rope_norm_back(dk[b] * (1.0 / LOG2E), pre_ref[at, :, heads * HEAD:].astype(F32), kg_ref[...], cos, sins)
        d_ref[at, :, heads * HEAD:(heads + 1) * HEAD] = back.astype(BF16)
        kgg_ref[...] += jnp.sum(part, axis=0, keepdims=True)
        d_ref[at, :, (heads + 1) * HEAD:] = dv[b].astype(BF16)

    for stage in range(1, stages):
        keep = fs >> (stage + 1)
        base = fs // 2 - (fs >> stage)
        for e in range(len(early)):
            for hi in range(2):
                for cp in later(e, hi, stage):
                    cp.wait_recv()
                held[e, hi, :keep] = add_low(held[e, hi, :keep], rn[e, hi, base:base + keep])
                if stage + 1 < stages:
                    for cp in later(e, hi, stage + 1):
                        cp.start()
    for e in range(len(early)):
        te_ref[e] = held[e, :, 0]
    for j in range(len(late)):
        for hi in range(2):
            for cp in first(j, hi):
                cp.wait_recv()
            tl_ref[j, hi] = add_low(held[len(early) + j, hi], rl[j, hi])
    for j in range(len(late)):
        for hi in range(2):
            for cp in first(j, hi):
                cp.wait_send()
    for e in range(len(early)):
        for hi in range(2):
            for stage in range(1, stages):
                for cp in later(e, hi, stage):
                    cp.wait_send()


def attend_back_call(dims, slot, block, q, k, v, o, l, do, pre, cos, sin, qg, kg, re, g):
    fs, nc, nz = dims
    q_cols = q.shape[2]
    heads = q_cols // HEAD
    early, late = len(early_parts(nz)), len(late_parts(nz))
    shard, cols = g.shape[3:]
    DMA = pltpu.SemaphoreType.DMA
    V = pltpu.VMEM
    return pl.pallas_call(
        lambda *refs: attend_back_kernel(dims, *refs),
        out_shape=(
            jax.ShapeDtypeStruct((BLOCKS, BLOCK, q_cols + 2 * HEAD), BF16),
            jax.ShapeDtypeStruct((early, 2, shard, cols), BF16),
            jax.ShapeDtypeStruct((late, 2, fs // 2, shard, cols), BF16),
            jax.ShapeDtypeStruct((1, HEAD), F32),
            jax.ShapeDtypeStruct((1, HEAD), F32),
        ),
        in_specs=[SMEM_SPEC, SMEM_SPEC] + [VMEM_SPEC] * 12 + [ANY_SPEC],
        out_specs=(VMEM_SPEC,) * 5,
        scratch_shapes=[
            V((BLOCKS, heads * BLOCK, HEAD), F32), V((BLOCKS, BLOCK, HEAD), F32), V((BLOCKS, BLOCK, HEAD), F32),
            V((8, heads * BLOCK), F32),
            V((nz, 2, fs // 2, shard, cols), BF16), V((late, 2, fs // 2, shard, cols), BF16),
            V((early, 2, max(fs // 2 - 1, 1), shard, cols), BF16),
            DMA((nz, 2, fs // 2)), DMA((late, 2, fs // 2)), DMA((late, 2, fs // 2)),
            DMA((early, 2, max(fs // 2 - 1, 1))), DMA((early, 2, max(fs // 2 - 1, 1))),
        ],
        compiler_params=pltpu.CompilerParams(collective_id=3, has_side_effects=True, vmem_limit_bytes=VMEM_LIMIT),
        cost_estimate=pl.CostEstimate(flops=2 * 20 * BLOCK * BLOCK * heads * 5 * HEAD, bytes_accessed=40 * 2**20, transcendentals=0),
    )(slot, block, q, k, v, o, l, do, pre, cos, sin, qg, kg, re, g)
def column_parts(dims, hidden, q_cols):
    return (0, hidden, 2 * hidden, 3 * hidden, 3 * hidden + q_cols)


def feed_kernel(dims, x_ref, dy_ref, o_ref, w_ref, gain_ref, out_ref, dh_ref, fg_ref, do_ref, g_ref, re_ref,
                wb, hs, b_ref, da_ref, dgu, u_ref, acc, dacc, snd, rcv, dos, bt, yt, at,
                ls, gs, ss, sr, xs, xr, fss, fsr):
    fs, nc, nz = dims
    f, c, z = lax.axis_index("fsdp"), lax.axis_index("ctx"), lax.axis_index("tp")
    o = 1 - c
    rows, width = x_ref.shape
    q_cols = o_ref.shape[3]
    hidden = (w_ref.shape[2] - q_cols) // 3
    gate, up_, down_, out_, end = column_parts(dims, hidden, q_cols)
    loads = [pltpu.make_async_copy(w_ref.at[zz], wb.at[zz], ls.at[zz]) for zz in range(nz)]
    for cp in loads:
        cp.start()
    barrier = pltpu.get_barrier_semaphore()
    pl.semaphore_signal(barrier, inc=1, device_id={"ctx": o}, device_id_type=MESH)
    for dz in range(1, nz):
        pl.semaphore_signal(barrier, inc=1, device_id={"tp": lax.rem(z + dz, nz)}, device_id_type=MESH)
    bit_first = sorted({reduce_order(fs, hi)[0] for hi in range(2)}) if fs > 1 else []
    for bit in bit_first:
        pl.semaphore_signal(barrier, inc=1, device_id={"fsdp": flip(f, bit)}, device_id_type=MESH)
    pl.semaphore_wait(barrier, nz + len(bit_first))
    early = early_parts(nz)
    shard = width // (fs * nc)

    def first(e, hi):
        def view(g):
            return wb.at[early[e], pl.ds(pl.multiple_of((g * nc + hi) * shard, shard), shard)]
        return first_copies(hi, fs, f, view, lambda i: re_ref.at[e, hi, i], fss.at[e, hi], fsr.at[e, hi])

    def cross(i, src, dst):
        return remote(src, dst, ss.at[i], sr.at[i], ctx=o)
    for cp in loads:
        cp.wait()

    def project(side):
        total = dot(o_ref[0, side], wb[0, :, out_:end], NT)
        for zz in range(1, nz):
            total += dot(o_ref[zz, side], wb[zz, :, out_:end], NT)
        return total
    snd[0] = project(o).astype(BF16)
    cross(0, snd.at[0], rcv.at[0]).start()
    own = project(c)
    cross(0, snd.at[0], rcv.at[0]).wait_recv()
    h = x_ref[...].astype(F32) + own + rcv[0].astype(F32)
    hs[...] = h
    b_ref[c] = (h * lax.rsqrt(jnp.mean(h * h, axis=-1, keepdims=True) + EPS) * gain_ref[...]).astype(BF16)
    cross(1, b_ref.at[c], b_ref.at[c]).start()
    yt[...] = dy_ref[...].reshape(nc * rows, width).T
    cross(1, b_ref.at[c], b_ref.at[o]).wait_recv()

    @pl.loop(0, nz)
    def _(zz):
        both = b_ref[...].reshape(nc * rows, width)
        gu = dot(both, wb[zz, :, gate:down_], NN)
        du = dot(dy_ref[...].reshape(nc * rows, width), wb[zz, :, down_:out_], NN)
        gt, uv = gu[:, :hidden], gu[:, hidden:]
        sig = 1.0 / (1.0 + jnp.exp(-gt))
        silu = gt * sig
        hid = (silu * uv).astype(BF16)
        u_ref[zz] = hid
        dgu[zz, :, :hidden] = (du * uv * sig * (1.0 + gt * (1.0 - sig))).astype(BF16)
        dgu[zz, :, hidden:] = (du * silu).astype(BF16)

        @pl.when(zz == 0)
        def _():
            acc[...] = dot(hid, wb[zz, :, down_:out_], NT)
            dacc[...] = dot(dgu[zz], wb[zz, :, gate:down_], NT)

        @pl.when(zz > 0)
        def _():
            acc[...] += dot(hid, wb[zz, :, down_:out_], NT)
            dacc[...] += dot(dgu[zz], wb[zz, :, gate:down_], NT)

    def side_rows(side):
        return pl.ds(pl.multiple_of(side * rows, 128), rows)
    snd[1] = dacc[side_rows(o)].astype(BF16)
    cross(2, snd.at[1], rcv.at[1]).start()
    snd[2] = acc[side_rows(o)].astype(BF16)
    cross(3, snd.at[2], rcv.at[2]).start()
    bt[...] = b_ref[...].reshape(nc * rows, width).T
    cross(2, snd.at[1], rcv.at[1]).wait_recv()
    db = dacc[side_rows(c)] + rcv[1].astype(F32)
    h = hs[...]
    inv = lax.rsqrt(jnp.mean(h * h, axis=-1, keepdims=True) + EPS)
    n = h * inv
    sc = db * gain_ref[...]
    dh = dy_ref[c].astype(F32) + inv * (sc - n * jnp.mean(sc * n, axis=-1, keepdims=True))
    fg_ref[...] = jnp.sum(db * n, axis=0, keepdims=True)
    dh_ref[...] = dh
    da_ref[c] = dh.astype(BF16)
    cross(4, da_ref.at[c], da_ref.at[c]).start()
    cross(3, snd.at[2], rcv.at[2]).wait_recv()
    out_ref[...] = (hs[...] + acc[side_rows(c)] + rcv[2].astype(F32)).astype(BF16)
    cross(4, da_ref.at[c], da_ref.at[o]).wait_recv()

    @pl.loop(1, nz + 1)
    def _(dz):
        to = lax.rem(z + dz, nz)
        dos[to] = dot(da_ref[...].reshape(nc * rows, width), wb[to, :, out_:end], NN).astype(BF16).reshape(nc, rows, q_cols)

        @pl.when(dz < nz)
        def _():
            for side in range(nc):
                remote(dos.at[to, side], do_ref.at[side, z], xs.at[dz, side], xr.at[z, side], tp=to).start()
    for side in range(nc):
        do_ref[side, z] = dos[z, side]
    at[...] = da_ref[...].reshape(nc * rows, width).T

    for zz in early + late_parts(nz):
        wb[zz, :, gate:down_] = dot(bt[...], dgu[zz], NN).astype(BF16)
        wb[zz, :, down_:out_] = dot(yt[...], u_ref[zz], NN).astype(BF16)
        wb[zz, :, out_:end] = dot(at[...], o_ref[zz].reshape(nc * rows, q_cols), NN).astype(BF16)
        pltpu.make_async_copy(wb.at[zz], g_ref.at[zz], gs.at[zz]).start()
        if zz in early:
            for hi in range(2):
                for cp in first(early.index(zz), hi):
                    cp.start()
    for zz in range(nz):
        pltpu.make_async_copy(wb.at[zz], g_ref.at[zz], gs.at[zz]).wait()
    for dz in range(1, nz):
        src = lax.rem(z + dz, nz)
        for side in range(nc):
            cp = remote(dos.at[0, side], do_ref.at[side, src], xs.at[dz, side], xr.at[src, side], tp=src)
            cp.wait_recv()
            cp.wait_send()
    for e in range(len(early)):
        for hi in range(2):
            for cp in first(e, hi):
                cp.wait_recv()
                cp.wait_send()
    for i, part in enumerate((snd.at[0], b_ref.at[c], snd.at[1], snd.at[2], da_ref.at[c])):
        cross(i, part, part).wait_send()


def feed_call(dims, x, dyp, o, w, gain):
    fs, nc, nz = dims
    rows, width = x.shape
    q_cols = o.shape[3]
    cols = w.shape[2]
    hidden = (cols - q_cols) // 3
    early = len(early_parts(nz))
    DMA = pltpu.SemaphoreType.DMA
    V = pltpu.VMEM
    return pl.pallas_call(
        lambda *refs: feed_kernel(dims, *refs),
        out_shape=(
            jax.ShapeDtypeStruct((rows, width), BF16),
            jax.ShapeDtypeStruct((rows, width), F32),
            jax.ShapeDtypeStruct((1, width), F32),
            jax.ShapeDtypeStruct((nc, nz, rows, q_cols), BF16),
            jax.ShapeDtypeStruct(w.shape, BF16),
            jax.ShapeDtypeStruct((early, 2, fs // 2, width // (fs * nc), cols), BF16),
        ),
        in_specs=[VMEM_SPEC] * 3 + [ANY_SPEC, VMEM_SPEC],
        out_specs=(VMEM_SPEC,) * 4 + (ANY_SPEC, ANY_SPEC),
        scratch_shapes=[
            V(w.shape, BF16), V((rows, width), F32), V((nc, rows, width), BF16), V((nc, rows, width), BF16),
            V((nz, nc * rows, 2 * hidden), BF16), V((nz, nc * rows, hidden), BF16),
            V((nc * rows, width), F32), V((nc * rows, width), F32),
            V((3, rows, width), BF16), V((3, rows, width), BF16), V((nz, nc, rows, q_cols), BF16),
            V((width, nc * rows), BF16), V((width, nc * rows), BF16), V((width, nc * rows), BF16),
            DMA((nz,)), DMA((nz,)), DMA((5,)), DMA((5,)), DMA((nz, nc)), DMA((nz, nc)),
            DMA((early, 2, fs // 2)), DMA((early, 2, fs // 2)),
        ],
        compiler_params=pltpu.CompilerParams(collective_id=2, has_side_effects=True, vmem_limit_bytes=VMEM_LIMIT),
        cost_estimate=pl.CostEstimate(flops=2 * 13 * 2**30, bytes_accessed=40 * 2**20, transcendentals=0),
    )(x, dyp, o, w, gain)
def line_events(nz):
    out = []
    for z in range(nz):
        events = [(z + nz - 1 - t, 0, t) for t in range(z + 1, nz)] + [(nz - 1 - z + t, 1, t) for t in range(z)]
        out.append([(way, t) for _, way, t in sorted(events)])
    return out


def at_place(z, rows):
    return pick(z, rows)


def finish_kernel(dims, d_ref, wall_ref, a_ref, x_ref, dh_ref, gain_ref, te_ref, tl_ref, fg_ref, qgg_ref, kgg_ref,
                  ig_ref, dwq_ref, dwz_ref, gains_ref,
                  pa, sib, ru, sa, snd, rq, wq, rw, sw, tw, rn, fin, share, sc_, gx, gy,
                  bs, br, us, ur, qs, qr, vs, vr, ns, nr, cs, cr, hs, hr):
    fs, nc, nz = dims
    f, c, z = lax.axis_index("fsdp"), lax.axis_index("ctx"), lax.axis_index("tp")
    o = 1 - c
    me = f * nc + c
    rows, width = x_ref.shape
    shard = dwq_ref.shape[1]
    early, late = early_parts(nz), late_parts(nz)
    stages = fs.bit_length() - 1
    others = [(df, dc) for df in range(fs) for dc in range(nc) if (df, dc) != (0, 0)]
    barrier = pltpu.get_barrier_semaphore()
    for df, dc in others:
        pl.semaphore_signal(barrier, inc=1, device_id={"fsdp": lax.rem(f + df, fs), "ctx": lax.rem(c + dc, nc)}, device_id_type=MESH)
    for dz in range(1, nz):
        pl.semaphore_signal(barrier, inc=1, device_id={"tp": lax.rem(z + dz, nz)}, device_id_type=MESH)
    pl.semaphore_wait(barrier, len(others) + nz - 1)

    def later(j, hi, stage):
        return later_copies(hi, stage, fs, f, lambda i: tl_ref.at[j, hi, i], lambda i: rn.at[j, hi, i], ns.at[j, hi], nr.at[j, hi])
    for j in range(len(late)):
        for hi in range(2):
            if stages > 1:
                for cp in later(j, hi, 1):
                    cp.start()

    order = sorted(range(nz), key=lambda t: (min(t, nz - 1 - t), -t))

    def cross(t):
        return remote(snd.at[t], sib.at[t], bs.at[t], br.at[t], ctx=o)

    @pl.loop(0, nz)
    def _(i):
        t = pick(i, order)
        snd[t] = dot(d_ref[o * nz + t], wall_ref[...], NT).astype(BF16)
        cross(t).start()
        pa[t] = dot(d_ref[c * nz + t], wall_ref[...], NT)

    @pl.loop(0, nz)
    def _(i):
        t = pick(i, order)
        cross(t).wait_recv()
        pa[t] += sib[t].astype(F32)

    events = line_events(nz)

    def event(i):
        way = at_place(z, [events[zz][i][0] for zz in range(nz)])
        t = at_place(z, [events[zz][i][1] for zz in range(nz)])
        arrives = jnp.where(way == 0, z > 0, z < nz - 1)
        to = jnp.where(way == 0, jnp.minimum(z + 1, nz - 1), jnp.maximum(z - 1, 0))
        slot = jnp.where((way == 1) & (t == to), nz, t)
        return t, arrives, to, slot

    def rows_copy(i):
        _, _, to, slot = event(i)
        return remote(sa.at[i], ru.at[slot], us.at[i], ur.at[slot], tp=to)

    def rows_event(i):
        t, arrives, _, _ = event(i)

        @pl.when(arrives)
        def _():
            remote(sa.at[i], ru.at[t], us.at[i], ur.at[t], ctx=o).wait_recv()
            sa[i] = (pa[t] + ru[t].astype(F32)).astype(BF16)

        @pl.when(jnp.logical_not(arrives))
        def _():
            sa[i] = pa[t].astype(BF16)
        rows_copy(i).start()

    def weights(r):
        return pl.ds(pl.multiple_of(r * shard, shard), shard)

    rows_event(0)
    wq[...] = jnp.zeros_like(wq)

    @pl.loop(0, nc * nz)
    def _(s):
        wq[...] += dot(a_ref[s], d_ref[s], TN)
    rq[me] = wq[weights(me)].astype(BF16)
    for i, (df, dc) in enumerate(others):
        tf, tc = lax.rem(f + df, fs), lax.rem(c + dc, nc)
        sc_[i] = wq[weights(tf * nc + tc)].astype(BF16)
        remote(sc_.at[i], rq.at[me], qs.at[i], qr.at[me], fsdp=tf, ctx=tc).start()
    for e in range(len(early)):
        tw[early[e]] = te_ref[e]
    for stage in range(1, stages):
        keep = fs >> (stage + 1)
        base = fs // 2 - (fs >> stage)
        for j in range(len(late)):
            for hi in range(2):
                for cp in later(j, hi, stage):
                    cp.wait_recv()
                if stage + 1 == stages:
                    tw[late[j], hi] = add_low(tl_ref[j, hi, 0], rn[j, hi, base])
                else:
                    tl_ref[j, hi, :keep] = add_low(tl_ref[j, hi, :keep], rn[j, hi, base:base + keep])
                    for cp in later(j, hi, stage + 1):
                        cp.start()
    for i in range(1, nz - 1):
        rows_event(i)

    def grads_copy(i):
        _, _, to, slot = event(i)
        return remote(sw.at[i], rw.at[slot], vs.at[i], vr.at[slot], tp=to)

    def grads_event(i):
        t, arrives, _, _ = event(i)

        @pl.when(arrives)
        def _():
            remote(sw.at[i], rw.at[t], vs.at[i], vr.at[t], ctx=o).wait_recv()
            sw[i] = add_low(tw[t], rw[t])

        @pl.when(jnp.logical_not(arrives))
        def _():
            sw[i] = tw[t]
        grads_copy(i).start()
    grads_event(0)

    def rows_arrival(way):
        slot = nz if way else z
        return remote(sa.at[0], ru.at[slot], us.at[0], ur.at[slot], ctx=o)

    @pl.when(z > 0)
    def _():
        rows_arrival(0).wait_recv()
        pa[z] += ru[z].astype(F32)

    @pl.when(z < nz - 1)
    def _():
        rows_arrival(1).wait_recv()
        pa[z] += ru[nz].astype(F32)
    da = pa[z]
    x = x_ref[...].astype(F32)
    inv = lax.rsqrt(jnp.mean(x * x, axis=-1, keepdims=True) + EPS)
    n = x * inv
    sc = da * gain_ref[...]
    ig_ref[...] = dh_ref[...] + inv * (sc - n * jnp.mean(sc * n, axis=-1, keepdims=True))
    gx[z, 0:1] = jnp.sum(da * n, axis=0, keepdims=True)
    gx[z, 1:2] = fg_ref[...]
    gx[z, 2:3] = jnp.concatenate([qgg_ref[...], kgg_ref[...]] + [jnp.zeros((1, width - 2 * HEAD), F32)], axis=1)
    gx[z, 3:] = jnp.zeros_like(gx[z, 3:])
    for dz in range(1, nz):
        to = lax.rem(z + dz, nz)
        remote(gx.at[z], gx.at[z], hs.at[dz - 1], hr.at[z], tp=to).start()
    for i in range(1, nz - 1):
        grads_event(i)

    for i, (df, dc) in enumerate(others):
        src = lax.rem(f + df, fs) * nc + lax.rem(c + dc, nc)
        remote(sc_.at[0], rq.at[src], qs.at[i], qr.at[src], ctx=o).wait_recv()
    for cc in range(nc):
        total = rq[cc].astype(F32)
        for ff in range(1, fs):
            total += rq[ff * nc + cc].astype(F32)
        dwq_ref[cc] = total

    def grads_arrival(way):
        slot = nz if way else z
        return remote(sw.at[0], rw.at[slot], vs.at[0], vr.at[slot], ctx=o)

    for dz in range(1, nz):
        src = lax.rem(z + dz, nz)
        remote(gx.at[src], gx.at[src], hs.at[dz - 1], hr.at[src], tp=src).wait_recv()
    total = gx[0]
    for zz in range(1, nz):
        total += gx[zz]
    gy[me] = total
    for i, (df, dc) in enumerate(others):
        remote(gy.at[me], gy.at[me], hs.at[nz - 1 + i], hr.at[nz + me], fsdp=lax.rem(f + df, fs), ctx=lax.rem(c + dc, nc)).start()

    fin[...] = tw[z].astype(F32)

    @pl.when(z > 0)
    def _():
        grads_arrival(0).wait_recv()
        fin[...] += rw[z].astype(F32)

    @pl.when(z < nz - 1)
    def _():
        grads_arrival(1).wait_recv()
        fin[...] += rw[nz].astype(F32)
    share[0] = fin[o].astype(BF16)
    swap = remote(share.at[0], share.at[1], cs.at[0], cr.at[0], ctx=o)
    swap.start()
    dwz_ref[c] = fin[c]

    for i, (df, dc) in enumerate(others):
        src = lax.rem(f + df, fs) * nc + lax.rem(c + dc, nc)
        remote(gy.at[src], gy.at[src], hs.at[nz - 1 + i], hr.at[nz + src], ctx=o).wait_recv()
    total = gy[0]
    for r in range(1, fs * nc):
        total += gy[r]
    gains_ref[...] = total
    swap.wait_recv()
    dwz_ref[o] = share[1].astype(F32)

    swap.wait_send()
    for i in range(nz - 1):
        rows_copy(i).wait_send()
        grads_copy(i).wait_send()
    for t in range(nz):
        cross(t).wait_send()
    for i in range(nz - 1):
        remote(gx.at[0], gx.at[0], hs.at[i], hr.at[0], ctx=o).wait_send()
    for i in range(len(others)):
        remote(sc_.at[0], rq.at[0], qs.at[i], qr.at[0], ctx=o).wait_send()
        remote(gy.at[0], gy.at[0], hs.at[nz - 1 + i], hr.at[nz], ctx=o).wait_send()
    for j in range(len(late)):
        for hi in range(2):
            for stage in range(1, stages):
                for cp in later(j, hi, stage):
                    cp.wait_send()


def finish_call(dims, d, wall, a, x, dh, gain, te, tl, fg, qgg, kgg):
    fs, nc, nz = dims
    rows, width = x.shape
    shard, cols = te.shape[2:]
    proj = wall.shape[1]
    late = len(late_parts(nz))
    n = fs * nc
    DMA = pltpu.SemaphoreType.DMA
    V = pltpu.VMEM
    return pl.pallas_call(
        lambda *refs: finish_kernel(dims, *refs),
        out_shape=(
            jax.ShapeDtypeStruct((rows, width), F32),
            jax.ShapeDtypeStruct((nc, width // n, proj), F32),
            jax.ShapeDtypeStruct((nc, shard, cols), F32),
            jax.ShapeDtypeStruct((8, width), F32),
        ),
        in_specs=[VMEM_SPEC] * 11,
        out_specs=(VMEM_SPEC,) * 4,
        scratch_shapes=[
            V((nz, rows, width), F32), V((nz, rows, width), BF16), V((nz + 1, rows, width), BF16),
            V((nz - 1, rows, width), BF16), V((nz, rows, width), BF16),
            V((n, width // n, proj), BF16), V((width, proj), F32),
            V((nz + 1, 2, shard, cols), BF16), V((nz - 1, 2, shard, cols), BF16), V((nz, 2, shard, cols), BF16),
            V((late, 2, max(fs // 2 - 1, 1), shard, cols), BF16),
            V((2, shard, cols), F32), V((2, shard, cols), BF16),
            V((n - 1, width // n, proj), BF16), V((nz, 8, width), F32), V((n, 8, width), F32),
            DMA((nz,)), DMA((nz,)), DMA((nz - 1,)), DMA((nz + 1,)),
            DMA((n - 1,)), DMA((n,)), DMA((nz - 1,)), DMA((nz + 1,)),
            DMA((late, 2, max(fs // 2 - 1, 1))), DMA((late, 2, max(fs // 2 - 1, 1))),
            DMA((1,)), DMA((1,)), DMA((nz - 1 + n - 1,)), DMA((nz + n,)),
        ],
        compiler_params=pltpu.CompilerParams(collective_id=4, has_side_effects=True, vmem_limit_bytes=VMEM_LIMIT),
        cost_estimate=pl.CostEstimate(flops=2 * 4 * 2**30, bytes_accessed=40 * 2**20, transcendentals=0),
    )(d, wall, a, x, dh, gain, te, tl, fg, qgg, kgg)
def on_device(dims, tokens, out_grad, block_slot, attn_gain, ffn_gain, query_gain, key_norm_gain,
              w_query, key_weight, value_weight, w_out, w_gate, w_up, w_down):
    fs, nc, nz = dims
    rows, width = tokens.shape
    shard = w_query.shape[0]
    block_ids = block_slot[0]
    slots = jnp.zeros((BLOCKS,), jnp.int32).at[block_ids].set(jnp.arange(BLOCKS, dtype=jnp.int32))
    start = jnp.minimum(block_ids, PBLOCKS) * BLOCK
    places = (start[:, None] + jnp.arange(BLOCK, dtype=jnp.int32)[None, :]).reshape(-1).astype(F32)
    freqs = ROPE_BASE ** (-(jnp.arange(0, HEAD, 2).astype(F32) / HEAD))
    angles = places[:, None] * freqs[None, :]
    cos, sin = jnp.cos(angles), jnp.sin(angles)
    cos = jnp.concatenate([cos, cos], axis=1)
    sins = jnp.concatenate([-sin, sin], axis=1)

    def halves(w):
        return jnp.stack(jnp.split(w, nc, axis=1))
    wqkv = jnp.concatenate([halves(w_query), halves(key_weight), halves(value_weight)], axis=2)
    wz = jnp.concatenate([halves(w_gate), halves(w_up), halves(w_down.T), halves(w_out.T)], axis=2)
    hidden, q_cols = w_gate.shape[1] // nc, w_query.shape[1] // nc
    ag, fg = attn_gain[None], ffn_gain[None]
    qg, kg = query_gain[None], key_norm_gain[None]

    a, q, k, v, pre, wall, w, dyp = gather_call(
        dims, tokens, out_grad, ag, wqkv, wz, cos.reshape(-1, rows, HEAD), sins.reshape(-1, rows, HEAD), qg, kg)
    blocks = lambda t: t.reshape(BLOCKS, BLOCK, -1)
    q, k, v, pre = blocks(q), blocks(k), blocks(v), blocks(pre)
    w, mixed, o, logs = attend_call(dims, slots, block_ids, q, k, v, w, rows)
    cols = w.shape[4]
    result, dh, ffn_part, do, g, re = feed_call(dims, tokens, dyp, mixed, w.reshape(nz, width, cols), fg)
    d, te, tl, q_part, k_part = attend_back_call(
        dims, slots, block_ids, q, k, v, blocks(o), logs, blocks(do), pre, blocks(cos), blocks(sins), qg, kg,
        re, g.reshape(nz, fs, nc, shard, cols))
    input_grad, dwq, dwz, gains = finish_call(
        dims, d.reshape(nc * nz, rows, -1), wall.reshape(width, -1), a, tokens, dh, ag, te, tl, ffn_part, q_part, k_part)

    def whole(g, at, n):
        return jnp.concatenate([g[i, :, at:at + n] for i in range(nc)], axis=1)
    return (
        result, input_grad, gains[0], gains[1], gains[2, :HEAD], gains[2, HEAD:2 * HEAD],
        whole(dwq, 0, q_cols), whole(dwq, q_cols, HEAD), whole(dwq, q_cols + HEAD, HEAD),
        whole(dwz, 3 * hidden, q_cols).T, whole(dwz, 0, hidden), whole(dwz, hidden, hidden), whole(dwz, 2 * hidden, hidden).T,
    )


def solution(mesh):
    dims = (mesh.shape["fsdp"], mesh.shape["ctx"], mesh.shape["tp"])
    everything, weights = ("fsdp", "ctx", "tp"), ("fsdp", "ctx")
    split, turned = P(weights, "tp"), P("tp", weights)
    return jax.shard_map(
        lambda *args: on_device(dims, *args),
        mesh=mesh,
        in_specs=(P(everything, None), P(everything, None), P("fsdp", None), P(), P(), P(), P(), split, split, split, turned, split, split, turned),
        out_specs=(P(everything, None), P(everything, None), P(), P(), P(), P(), split, split, split, turned, split, split, turned),
        check_vma=False,
    )
```

```python
import numpy as np
import jax
import jax.numpy as jnp
from jax import lax
from jax.experimental import pallas as pl
from jax.experimental.pallas import tpu as pltpu
from jax.sharding import PartitionSpec as P

HEAD = 128
BLOCK = 512
PBLOCKS = 4
BLOCKS = 6
EPS = 1e-6
ROPE_BASE = 1e6
MESH = pl.DeviceIdType.MESH
F32, BF16 = jnp.float32, jnp.bfloat16
LOG2E = 1.4426950408889634
QSCALE = HEAD ** -0.5 * LOG2E
VMEM_SPEC = pl.BlockSpec(memory_space=pltpu.VMEM)
ANY_SPEC = pl.BlockSpec(memory_space=pl.ANY)
SMEM_SPEC = pl.BlockSpec(memory_space=pltpu.SMEM)
VMEM_LIMIT = 60 * 2**20


def dot(a, b, dims):
    return lax.dot_general(a, b, (dims, ((), ())), preferred_element_type=F32)


NN = ((1,), (0,))
NT = ((1,), (1,))
TN = ((0,), (0,))


def flip(f, mask):
    bit = 1
    while bit <= mask:
        if mask & bit:
            f = f + bit - 2 * bit * lax.rem(lax.div(f, bit), 2)
        bit *= 2
    return f


def remote(src, dst, send, recv, **where):
    return pltpu.make_async_remote_copy(
        src_ref=src, dst_ref=dst, send_sem=send, recv_sem=recv,
        device_id=where, device_id_type=MESH)


def pick(index, values):
    out = jnp.int32(values[-1])
    for k in range(len(values) - 1):
        out = jnp.where(index == k, jnp.int32(values[k]), out)
    return out


def near_order(n):
    return [sorted(range(n), key=lambda s: (abs(s - z), s)) for z in range(n)]


def bit_orders(fs):
    bits = [1 << b for b in range(fs.bit_length() - 1)]
    return bits, bits[::-1]


def combos(bits):
    out = [0]
    for b in bits:
        out = out + [m + b for m in out]
    return out


def plane_copies(half, stage, fs, f, view, ssem, rsem):
    order = bit_orders(fs)[half]
    partner = flip(f, order[stage])
    base = (1 << stage) - 1
    out = []
    for m, mask in enumerate(combos(order[:stage])):
        g = flip(f, mask)
        out.append(remote(view(g), view(g), ssem.at[base + m], rsem.at[base + m], fsdp=partner))
    return out


UNIT = 128


def rope_tables():
    freqs = np.float32(ROPE_BASE) ** (-(np.arange(0, HEAD, 2, dtype=np.float32) / np.float32(HEAD)))
    places = np.arange((PBLOCKS + 1) * BLOCK, dtype=np.float32)
    angles = (places[:, None] * freqs[None, :].astype(np.float32)).astype(np.float64)
    cos, sin = np.cos(angles), np.sin(angles)
    shape = (-1, UNIT, HEAD)
    return (np.concatenate([cos, cos], axis=1).astype(np.float32).reshape(shape),
            np.concatenate([-sin, sin], axis=1).astype(np.float32).reshape(shape))


def rope_rows(table_ref, block_ref, first, count):
    per = BLOCK // UNIT
    out = []
    for i in range(count):
        unit = first + i
        out.append(table_ref[jnp.minimum(block_ref[lax.div(unit, per)], PBLOCKS) * per + lax.rem(unit, per)])
    return jnp.concatenate(out, axis=0)


def head_norm_rope(pre, gain, cos, sins):
    n = pre * lax.rsqrt(jnp.mean(pre * pre, axis=-1, keepdims=True) + EPS) * gain
    return n * cos + pltpu.roll(n, HEAD // 2, 1) * sins


def gather_kernel(dims, block_ref, x_ref, dy_ref, gain_ref, wq_in, wk_in, wv_in, wg_in, wu_in, wd_in, wo_in,
                  cos_ref, sin_ref, qg_ref, kg_ref,
                  a_ref, q_ref, k_ref, v_ref, pre_ref, wall_ref, w_ref, dyp_ref,
                  wqkv_ref, wz_ref, zs, zr, cs, cr, ws, wr, ms, mr, ps, pr, ls):
    fs, nc, nz = dims
    f, c, z = lax.axis_index("fsdp"), lax.axis_index("ctx"), lax.axis_index("tp")
    o = 1 - c
    me = f * nc + c
    others = [(df, dc) for df in range(fs) for dc in range(nc) if (df, dc) != (0, 0)]

    barrier = pltpu.get_barrier_semaphore()
    for df, dc in others:
        pl.semaphore_signal(barrier, inc=1, device_id={"fsdp": lax.rem(f + df, fs), "ctx": lax.rem(c + dc, nc)}, device_id_type=MESH)

    @pl.when(z > 0)
    def _():
        pl.semaphore_signal(barrier, inc=1, device_id={"tp": z - 1}, device_id_type=MESH)

    @pl.when(z < nz - 1)
    def _():
        pl.semaphore_signal(barrier, inc=1, device_id={"tp": z + 1}, device_id_type=MESH)
    x = x_ref[...].astype(F32)
    a_ref[c * nz + z] = (x * lax.rsqrt(jnp.mean(x * x, axis=-1, keepdims=True) + EPS) * gain_ref[...]).astype(BF16)
    pl.semaphore_wait(barrier, len(others) + jnp.where(z > 0, 1, 0) + jnp.where(z < nz - 1, 1, 0))

    row = a_ref.at[c * nz + z]
    up = remote(row, row, zs.at[z], zr.at[z], tp=jnp.minimum(z + 1, nz - 1))
    down = remote(row, row, zs.at[nz], zr.at[z], tp=jnp.maximum(z - 1, 0))
    pl.when(z < nz - 1)(up.start)
    pl.when(z > 0)(down.start)
    across = remote(row, row, cs.at[z], cr.at[z], ctx=o)
    across.start()
    dyc = remote(dy_ref, dyp_ref.at[c], ms.at[1], mr.at[1], ctx=o)
    dyc.start()
    dyp_ref[c] = dy_ref[...]

    def pack(packed, parts):
        at = 0
        for ref, turned in parts:
            value = ref[...].T if turned else ref[...]
            step = value.shape[1] // nc
            for cc in range(nc):
                packed[cc, :, at:at + step] = value[:, cc * step:(cc + 1) * step]
            at += step
    pack(wqkv_ref, ((wq_in, False), (wk_in, False), (wv_in, False)))
    wall_ref[me] = wqkv_ref[c]
    pack(wz_ref, ((wg_in, False), (wu_in, False), (wd_in, True), (wo_in, True)))
    own_w = pltpu.make_async_copy(wz_ref.at[c], w_ref.at[z, f, c], ls.at[0])
    own_w.start()
    for i, (df, dc) in enumerate(others):
        tf, tc = lax.rem(f + df, fs), lax.rem(c + dc, nc)
        remote(wqkv_ref.at[tc], wall_ref.at[me], ws.at[i], wr.at[me], fsdp=tf, ctx=tc).start()
    half = remote(wz_ref.at[o], w_ref.at[z, f, c], ms.at[0], mr.at[0], ctx=o)
    half.start()

    def plane(half_index, stage):
        return plane_copies(half_index, stage, fs, f, lambda g: w_ref.at[z, g, half_index], ps.at[half_index], pr.at[half_index])
    stages = fs.bit_length() - 1

    own_w.wait()
    remote(wz_ref.at[0], w_ref.at[z, f, o], ms.at[0], mr.at[0], ctx=o).wait_recv()
    for hi in range(2):
        for cp in plane(hi, 0):
            cp.start()
    q_cols = q_ref.shape[-1]

    def project(s):
        y = dot(a_ref[s], wall_ref[...].reshape(-1, wall_ref.shape[2]), NN)
        pre_ref[s] = y[:, :q_cols + HEAD].astype(BF16)
        units = a_ref.shape[1] // UNIT
        cos, sins = rope_rows(cos_ref, block_ref, s * units, units), rope_rows(sin_ref, block_ref, s * units, units)
        for h in range(q_cols // HEAD):
            q_ref[s, :, h * HEAD:(h + 1) * HEAD] = (head_norm_rope(y[:, h * HEAD:(h + 1) * HEAD], qg_ref[...], cos, sins) * QSCALE).astype(BF16)
        k_ref[s] = head_norm_rope(y[:, q_cols:q_cols + HEAD], kg_ref[...], cos, sins).astype(BF16)
        v_ref[s, :, :HEAD] = y[:, q_cols + HEAD:].astype(BF16)
        v_ref[s, :, HEAD:] = jnp.ones_like(v_ref[s, :, HEAD:])

    def take(hop):
        @pl.loop(0, 2 if hop == 0 else 4)
        def _(i):
            across_, way = (i, 0) if hop == 0 else (lax.rem(i, 2), lax.div(i, 2))
            src = z + (2 * way - 1) * hop

            @pl.when((src >= 0) & (src < nz))
            def _():
                s = jnp.where(across_ == 0, c, o) * nz + src

                @pl.when(across_ == 1)
                def _():
                    remote(a_ref.at[s], a_ref.at[s], cs.at[src], cr.at[src], ctx=o).wait_recv()
                project(s)

    for hop in range(1, nz):
        for way in range(2):
            src = z + (2 * way - 1) * hop

            @pl.when((src >= 0) & (src < nz))
            def _():
                part = a_ref.at[c * nz + src]
                remote(part, part, zs.at[src], zr.at[src], ctx=o).wait_recv()
                if way == 0:
                    pl.when(z < nz - 1)(remote(part, part, zs.at[src], zr.at[src], tp=jnp.minimum(z + 1, nz - 1)).start)
                else:
                    pl.when(z > 0)(remote(part, part, zs.at[src], zr.at[src], tp=jnp.maximum(z - 1, 0)).start)
                remote(part, part, cs.at[src], cr.at[src], ctx=o).start()
        if hop == 1:
            for i, (df, dc) in enumerate(others):
                src = lax.rem(f + df, fs) * nc + lax.rem(c + dc, nc)
                remote(wqkv_ref.at[0], wall_ref.at[src], ws.at[i], wr.at[src], ctx=o).wait_recv()
        take(hop - 1)
        stage = hop - 1
        if stage < stages:
            for hi in range(2):
                for cp in plane(hi, stage):
                    cp.wait_recv()
                if stage + 1 < stages:
                    for cp in plane(hi, stage + 1):
                        cp.start()
    take(nz - 1)
    for stage in range(nz - 1, stages):
        for hi in range(2):
            for cp in plane(hi, stage):
                cp.wait_recv()
            if stage + 1 < stages:
                for cp in plane(hi, stage + 1):
                    cp.start()
    for stage in range(stages):
        for hi in range(2):
            for cp in plane(hi, stage):
                cp.wait_send()
    for src in range(nz):
        @pl.when(((src <= z) & (z < nz - 1)) | ((src > z) & (z > 0)))
        def _():
            remote(row, row, zs.at[src], zr.at[src], ctx=o).wait_send()
        remote(row, row, cs.at[src], cr.at[src], ctx=o).wait_send()

    @pl.when(z > 0)
    def _():
        remote(row, row, zs.at[nz], zr.at[0], ctx=o).wait_send()
    for i in range(len(others)):
        remote(wqkv_ref.at[0], wall_ref.at[0], ws.at[i], wr.at[0], ctx=o).wait_send()
    half.wait_send()
    dyc.wait_send()
    remote(dy_ref, dyp_ref.at[o], ms.at[1], mr.at[1], ctx=o).wait_recv()


def gather_call(dims, block, x, dy, gain, weights, cos, sin, qg, kg):
    fs, nc, nz = dims
    rows, width = x.shape
    ns = nc * nz
    shard = weights[0].shape[0]
    q_cols = weights[0].shape[1] // nc
    cols = q_cols + 2 * HEAD
    wcols = 3 * (weights[3].shape[1] // nc) + q_cols
    DMA = pltpu.SemaphoreType.DMA
    return pl.pallas_call(
        lambda *refs: gather_kernel(dims, *refs),
        out_shape=(
            jax.ShapeDtypeStruct((ns, rows, width), BF16),
            jax.ShapeDtypeStruct((ns, rows, q_cols), BF16),
            jax.ShapeDtypeStruct((ns, rows, HEAD), BF16),
            jax.ShapeDtypeStruct((ns, rows, 2 * HEAD), BF16),
            jax.ShapeDtypeStruct((ns, rows, q_cols + HEAD), BF16),
            jax.ShapeDtypeStruct((fs * nc, shard, cols), BF16),
            jax.ShapeDtypeStruct((nz, fs, nc, shard, wcols), BF16),
            jax.ShapeDtypeStruct((nc, rows, width), BF16),
        ),
        in_specs=[SMEM_SPEC] + [VMEM_SPEC] * 14,
        out_specs=(VMEM_SPEC,) * 6 + (ANY_SPEC, VMEM_SPEC),
        scratch_shapes=[
            pltpu.VMEM((nc, shard, cols), BF16), pltpu.VMEM((nc, shard, wcols), BF16),
            DMA((nz + 1,)), DMA((nz,)), DMA((nz,)), DMA((nz,)),
            DMA((fs * nc - 1,)), DMA((fs * nc,)), DMA((2,)), DMA((2,)),
            DMA((2, fs - 1)), DMA((2, fs - 1)), DMA((2,)),
        ],
        compiler_params=pltpu.CompilerParams(collective_id=0, has_side_effects=True, vmem_limit_bytes=VMEM_LIMIT),
        cost_estimate=pl.CostEstimate(flops=2 * ns * rows * width * cols, bytes_accessed=30 * 2**20, transcendentals=0),
    )(block, x, dy, gain, *weights, cos, sin, qg, kg)
def full_keys(qb):
    return min(qb, PBLOCKS)


def stack_heads(rows):
    return jnp.concatenate([rows[:, h * HEAD:(h + 1) * HEAD] for h in range(rows.shape[1] // HEAD)], axis=0)


def slot_of(block_ref, b):
    out = jnp.int32(0)
    for s in range(1, BLOCKS):
        out = jnp.where(block_ref[s] == b, jnp.int32(s), out)
    return out


def attend_kernel(dims, keep, block_ref, q_ref, k_ref, v_ref, wi_ref, w_ref, or_ref, o_ref, l_ref,
                  ob, zs, zr, ps, pr, xs, xr):
    fs, nc, nz = dims
    f, c, z = lax.axis_index("fsdp"), lax.axis_index("ctx"), lax.axis_index("tp")
    rows = or_ref.shape[2]
    barrier = pltpu.get_barrier_semaphore()
    bits = bit_orders(fs)[0]
    for bit in bits:
        pl.semaphore_signal(barrier, inc=1, device_id={"fsdp": flip(f, bit)}, device_id_type=MESH)
    for dz in range(1, nz):
        pl.semaphore_signal(barrier, inc=1, device_id={"tp": lax.rem(z + dz, nz)}, device_id_type=MESH)
    pl.semaphore_wait(barrier, len(bits) + nz - 1)

    def piece(ref, hop):
        return ref.at[:, :, pl.ds(keep, ref.shape[-1] - keep)] if hop == nz - 1 else ref

    def up(src, sem, hop):
        part = piece(w_ref.at[src, f], hop)
        return remote(part, part, zs.at[sem], zr.at[src], tp=jnp.minimum(z + 1, nz - 1))

    def down(src, sem, hop):
        part = piece(w_ref.at[src, f], hop)
        return remote(part, part, zs.at[sem], zr.at[src], tp=jnp.maximum(z - 1, 0))
    pl.when(z < nz - 1)(up(z, z, 1).start)
    pl.when(z > 0)(down(z, nz, 1).start)
    stages = fs.bit_length() - 1

    def plane(src, hi, stage, hop):
        def view(g):
            ref = w_ref.at[src, g, hi]
            return ref.at[:, pl.ds(keep, ref.shape[-1] - keep)] if hop == nz - 1 else ref
        return plane_copies(hi, stage, fs, f, view, ps.at[src, hi], pr.at[src, hi])

    def each(hop, act):
        for way in range(2):
            src = z + (2 * way - 1) * hop

            @pl.when((src >= 0) & (src < nz))
            def _():
                act(way, src)

    def arrive(hop):
        def act(way, src):
            up(src, src, hop).wait_recv()
            if way == 0:
                pl.when(z < nz - 1)(up(src, src, hop + 1).start)
            else:
                pl.when(z > 0)(down(src, src, hop + 1).start)
            for hi in range(2):
                for cp in plane(src, hi, 0, hop):
                    cp.start()
        each(hop, act)

    def spread(hop, stage):
        def act(way, src):
            for hi in range(2):
                for cp in plane(src, hi, stage, hop):
                    cp.wait_recv()
                if stage + 1 < stages:
                    for cp in plane(src, hi, stage + 1, hop):
                        cp.start()
        each(hop, act)

    tri = lax.broadcasted_iota(jnp.int32, (BLOCK, BLOCK), 0) >= lax.broadcasted_iota(jnp.int32, (BLOCK, BLOCK), 1)
    heads = q_ref.shape[2] // HEAD
    for qb in range(BLOCKS):
        if qb == BLOCKS - 1:
            arrive(1)
        q2 = stack_heads(q_ref[slot_of(block_ref, qb)])

        def step(kb, acc):
            k = k_ref[slot_of(block_ref, kb)]
            v = v_ref[slot_of(block_ref, kb)]
            return acc + dot(jnp.exp2(dot(q2, k, NT)).astype(BF16), v, NN)
        acc = jnp.zeros((heads * BLOCK, 2 * HEAD), F32)
        if full_keys(qb):
            acc = lax.fori_loop(0, full_keys(qb), step, acc)
        k = k_ref[slot_of(block_ref, qb)]
        v = v_ref[slot_of(block_ref, qb)]
        s = dot(q2, k, NT)
        for h in range(heads):
            part = slice(h * BLOCK, (h + 1) * BLOCK)
            p = jnp.where(tri, jnp.exp2(s[part]), 0.0).astype(BF16)
            a = acc[part] + dot(p, v, NN)
            ob[qb, :, h * HEAD:(h + 1) * HEAD] = (a[:, :HEAD] / a[:, HEAD:]).astype(BF16)
            l_ref[qb, :, part] = jnp.log2(a[:, HEAD:]).T[0:8]
    for s in range(BLOCKS):
        o_ref[s * BLOCK:(s + 1) * BLOCK] = ob[block_ref[s]]

    def part_rows(side, zz):
        return pl.ds(pl.multiple_of((side * nz + zz) * rows, 128), rows)
    for hop in range(2, nz - 1):
        arrive(hop)
    for dz in range(1, nz):
        to = lax.rem(z + dz, nz)
        for side in range(nc):
            remote(o_ref.at[part_rows(side, to)], or_ref.at[z, side], xs.at[dz, side], xr.at[z, side], tp=to).start()
    for side in range(nc):
        or_ref[z, side] = o_ref[part_rows(side, z)]
    for hop in range(1, nz):
        for stage in range(stages):
            spread(hop, stage)
            if hop == nz - 2 and stage == 0:
                arrive(nz - 1)
    for dz in range(1, nz):
        src = lax.rem(z + dz, nz)
        for side in range(nc):
            cp = remote(o_ref.at[part_rows(side, 0)], or_ref.at[src, side], xs.at[dz, side], xr.at[src, side], tp=src)
            cp.wait_recv()
            cp.wait_send()
    for hop in range(1, nz):
        def left(way, src):
            if way == 0:
                pl.when(z < nz - 1)(up(src, src, hop + 1).wait_send)
            else:
                pl.when(z > 0)(down(src, src, hop + 1).wait_send)
            for hi in range(2):
                for stage in range(stages):
                    for cp in plane(src, hi, stage, hop):
                        cp.wait_send()
        each(hop, left)
    pl.when(z < nz - 1)(up(z, z, 1).wait_send)
    pl.when(z > 0)(down(z, nz, 1).wait_send)


def attend_call(dims, keep, block, q, k, v, w, rows):
    fs, nc, nz = dims
    q_cols = q.shape[2]
    span = BLOCKS * BLOCK
    heads = q_cols // HEAD
    DMA = pltpu.SemaphoreType.DMA
    return pl.pallas_call(
        lambda *refs: attend_kernel(dims, keep, *refs),
        out_shape=(
            jax.ShapeDtypeStruct(w.shape, BF16),
            jax.ShapeDtypeStruct((nz, nc, rows, q_cols), BF16),
            jax.ShapeDtypeStruct((span, q_cols), BF16),
            jax.ShapeDtypeStruct((BLOCKS, 8, heads * BLOCK), F32),
        ),
        in_specs=[SMEM_SPEC] + [VMEM_SPEC] * 3 + [ANY_SPEC],
        out_specs=(ANY_SPEC, VMEM_SPEC, VMEM_SPEC, VMEM_SPEC),
        scratch_shapes=[
            pltpu.VMEM((BLOCKS, BLOCK, q_cols), BF16),
            DMA((nz + 1,)), DMA((nz,)), DMA((nz, 2, fs - 1)), DMA((nz, 2, fs - 1)), DMA((nz, nc)), DMA((nz, nc)),
        ],
        input_output_aliases={4: 0},
        compiler_params=pltpu.CompilerParams(collective_id=1, has_side_effects=True, vmem_limit_bytes=VMEM_LIMIT),
        cost_estimate=pl.CostEstimate(flops=2 * 20 * BLOCK * BLOCK * heads * 3 * HEAD, bytes_accessed=30 * 2**20, transcendentals=0),
    )(block, q, k, v, w)
def reduce_order(fs, hi):
    return bit_orders(fs)[hi][::-1]


def reduce_masks(fs, hi):
    return combos(reduce_order(fs, hi)[1:][::-1])


def first_copies(hi, fs, f, view, land, ssem, rsem):
    bit = reduce_order(fs, hi)[0]
    return [remote(view(flip(flip(f, m), bit)), land(i), ssem.at[i], rsem.at[i], fsdp=flip(f, bit))
            for i, m in enumerate(reduce_masks(fs, hi))]


def later_copies(hi, stage, fs, f, held, land, ssem, rsem):
    bit = reduce_order(fs, hi)[stage]
    keep = fs >> (stage + 1)
    base = fs // 2 - (fs >> stage)
    return [remote(held(keep + i), land(base + i), ssem.at[base + i], rsem.at[base + i], fsdp=flip(f, bit)) for i in range(keep)]


def add_low(a, b):
    return (a.astype(F32) + b.astype(F32)).astype(BF16)


def early_parts(nz):
    return (nz - 1, 0) if nz > 1 else (0,)


def late_parts(nz):
    return tuple(t for t in range(nz - 2, 0, -1))


def rope_norm_back(g, pre, gain, cos, sins):
    c = g * cos + pltpu.roll(g * sins, HEAD // 2, 1)
    inv = lax.rsqrt(jnp.mean(pre * pre, axis=-1, keepdims=True) + EPS)
    n = pre * inv
    sc = c * gain
    return inv * (sc - n * jnp.mean(sc * n, axis=-1, keepdims=True)), c * n


def attend_back_kernel(dims, cut, block_ref, q_ref, k_ref, v_ref, o_ref, l_ref, do_ref, pre_ref, cos_ref, sin_ref,
                       qg_ref, kg_ref, re_ref, dr_ref, g_ref, d_ref, te_ref, to_ref, tl_ref, ch_ref, qgg_ref, kgg_ref,
                       dr, dq, dk, dv, he, ho, hl, ro, rl, rn, le, lo, ll, os, orr, fss, fsr, nss, nsr, xs, xr, hs, hr):
    fs, nc, nz = dims
    f, z = lax.axis_index("fsdp"), lax.axis_index("tp")
    heads = q_ref.shape[2] // HEAD
    early, late = early_parts(nz), late_parts(nz)[:-1]
    stages = fs.bit_length() - 1
    rest = pl.ds(cut, g_ref.shape[-1] - cut)
    barrier = pltpu.get_barrier_semaphore()
    bits = bit_orders(fs)[0]
    for bit in bits:
        pl.semaphore_signal(barrier, inc=1, device_id={"fsdp": flip(f, bit)}, device_id_type=MESH)
    for dz in range(1, nz):
        pl.semaphore_signal(barrier, inc=1, device_id={"tp": lax.rem(z + dz, nz)}, device_id_type=MESH)
    own = []
    for hi in range(2):
        for i, m in enumerate(reduce_masks(fs, hi)):
            for e, t in enumerate(early):
                own.append(pltpu.make_async_copy(g_ref.at[t, flip(f, m), hi, :, pl.ds(0, cut)], he.at[e, hi, i], le.at[e, hi, i]))
                own.append(pltpu.make_async_copy(g_ref.at[t, flip(f, m), hi, :, rest], ho.at[e, hi, i], lo.at[e, hi, i]))
            for j, t in enumerate(late):
                own.append(pltpu.make_async_copy(g_ref.at[t, flip(f, m), hi], hl.at[j, hi, i], ll.at[j, hi, i]))
    for cp in own:
        cp.start()
    pl.semaphore_wait(barrier, len(bits) + nz - 1)

    units = dr_ref.shape[2]
    def spot(side, zz):
        return pl.ds((side * nz + zz) * units, units)
    for dz in range(1, nz):
        to = lax.rem(z + dz, nz)
        for side in range(nc):
            remote(dr_ref.at[to, side], dr.at[spot(side, z)], xs.at[dz, side], xr.at[z, side], tp=to).start()
    for side in range(nc):
        dr[spot(side, z)] = dr_ref[z, side]

    def first_rest(e, hi):
        return first_copies(hi, fs, f, lambda g: g_ref.at[early[e], g, hi, :, rest], lambda i: ro.at[e, hi, i], os.at[e, hi], orr.at[e, hi])

    def first_late(j, hi):
        return first_copies(hi, fs, f, lambda g: g_ref.at[late[j], g, hi], lambda i: rl.at[j, hi, i], fss.at[j, hi], fsr.at[j, hi])

    def later(e, hi, stage):
        return later_copies(hi, stage, fs, f, lambda i: he.at[e, hi, i], lambda i: rn.at[e, hi, i], nss.at[e, hi], nsr.at[e, hi])
    for cp in own:
        cp.wait()
    for e in range(len(early)):
        for hi in range(2):
            he[e, hi] = add_low(he[e, hi], re_ref[e, hi])
            if stages > 1:
                for cp in later(e, hi, 1):
                    cp.start()

    def hop(e):
        return remote(te_ref.at[e], ch_ref, hs.at[e], hr.at[0], tp=jnp.minimum(z + 1, nz - 1) if e == 0 else jnp.maximum(z - 1, 0))

    def finish_early():
        for stage in range(1, stages):
            keep = fs >> (stage + 1)
            base = fs // 2 - (fs >> stage)
            for e in range(len(early)):
                for hi in range(2):
                    for cp in later(e, hi, stage):
                        cp.wait_recv()
                    he[e, hi, :keep] = add_low(he[e, hi, :keep], rn[e, hi, base:base + keep])
                    if stage + 1 < stages:
                        for cp in later(e, hi, stage + 1):
                            cp.start()
        for e in range(len(early)):
            te_ref[e] = he[e, :, 0]
        pl.when(z == 0)(hop(0).start)
        pl.when(z == nz - 1)(hop(1).start)
        for e in range(len(early)):
            for hi in range(2):
                for cp in first_rest(e, hi):
                    cp.start()
        for j in range(len(late)):
            for hi in range(2):
                for cp in first_late(j, hi):
                    cp.start()

    tri = lax.broadcasted_iota(jnp.int32, (BLOCK, BLOCK), 0) <= lax.broadcasted_iota(jnp.int32, (BLOCK, BLOCK), 1)
    dk[...] = jnp.zeros_like(dk)
    dv[...] = jnp.zeros_like(dv)
    per = BLOCK // UNIT
    for h in range(heads):
        cols, logs = slice(h * HEAD, (h + 1) * HEAD), slice(h * BLOCK, (h + 1) * BLOCK)
        if h == 1:
            for dz in range(1, nz):
                src = lax.rem(z + dz, nz)
                for side in range(nc):
                    remote(dr_ref.at[0, side], dr.at[spot(side, src)], xs.at[dz, side], xr.at[src, side], tp=src).wait_recv()
        for qb in range(BLOCKS):
            if h == 0 and qb == BLOCKS - 1:
                finish_early()
            at = slot_of(block_ref, qb)
            q = q_ref[at, :, cols]
            if h == 0:
                g = do_ref[at]
            else:
                g = jnp.concatenate([dr[at * per + i, :, (h - 1) * HEAD:h * HEAD] for i in range(per)], axis=0)
            delta = jnp.sum((g.astype(F32) * o_ref[at, :, cols].astype(F32)).T, axis=0, keepdims=True)
            log = l_ref[qb, 0:1, logs]

            def pair(kb, diagonal):
                k = k_ref[slot_of(block_ref, kb)]
                v = v_ref[slot_of(block_ref, kb), :, :HEAD]
                p = jnp.exp2(dot(k, q, NT) - log)
                if diagonal:
                    p = jnp.where(tri, p, 0.0)
                ds = (p * (dot(v, g, NT) - delta)).astype(BF16)
                dv[kb] += dot(p.astype(BF16), g, NN)
                dk[kb] += dot(ds, q, NN)
                return dot(k.T, ds, NN)
            total = pair(qb, True)
            for kb in range(full_keys(qb)):
                total = total + pair(kb, False)
            dq[qb, logs] = total.T

    qgg_ref[...] = jnp.zeros_like(qgg_ref)
    kgg_ref[...] = jnp.zeros_like(kgg_ref)

    @pl.loop(0, BLOCKS)
    def _(s):
        b = block_ref[s]
        cos, sins = rope_rows(cos_ref, block_ref, s * per, per), rope_rows(sin_ref, block_ref, s * per, per)
        qs = dq[b]
        for h in range(heads):
            back, part = rope_norm_back(qs[h * BLOCK:(h + 1) * BLOCK] * HEAD ** -0.5, pre_ref[s, :, h * HEAD:(h + 1) * HEAD].astype(F32), qg_ref[...], cos, sins)
            d_ref[s, :, h * HEAD:(h + 1) * HEAD] = back.astype(BF16)
            qgg_ref[...] += jnp.sum(part, axis=0, keepdims=True)
        back, part = rope_norm_back(dk[b] * (1.0 / LOG2E), pre_ref[s, :, heads * HEAD:].astype(F32), kg_ref[...], cos, sins)
        d_ref[s, :, heads * HEAD:(heads + 1) * HEAD] = back.astype(BF16)
        kgg_ref[...] += jnp.sum(part, axis=0, keepdims=True)
        d_ref[s, :, (heads + 1) * HEAD:] = dv[b].astype(BF16)

    for e in range(len(early)):
        for hi in range(2):
            for cp in first_rest(e, hi):
                cp.wait_recv()
            to_ref[e, hi] = add_low(ho[e, hi], ro[e, hi])
    for j in range(len(late)):
        for hi in range(2):
            for cp in first_late(j, hi):
                cp.wait_recv()
            tl_ref[j, hi] = add_low(hl[j, hi], rl[j, hi])
    pl.when((z == 1) | (z == nz - 2))(hop(0).wait_recv)
    pl.when(z == 0)(hop(0).wait_send)
    pl.when(z == nz - 1)(hop(1).wait_send)
    for dz in range(1, nz):
        for side in range(nc):
            remote(dr_ref.at[0, side], dr.at[spot(side, 0)], xs.at[dz, side], xr.at[0, side], tp=lax.rem(z + dz, nz)).wait_send()
    for hi in range(2):
        for j in range(len(late)):
            for cp in first_late(j, hi):
                cp.wait_send()
        for e in range(len(early)):
            for cp in first_rest(e, hi):
                cp.wait_send()
            for stage in range(1, stages):
                for cp in later(e, hi, stage):
                    cp.wait_send()


def attend_back_call(dims, block, q, k, v, o, l, do, pre, cos, sin, qg, kg, re, dr, g):
    fs, nc, nz = dims
    q_cols = q.shape[2]
    heads = q_cols // HEAD
    early, late = len(early_parts(nz)), len(late_parts(nz)) - 1
    shard, cols = g.shape[3:]
    cut = re.shape[4]
    half, more = fs // 2, max(fs // 2 - 1, 1)
    DMA = pltpu.SemaphoreType.DMA
    V = pltpu.VMEM
    return pl.pallas_call(
        lambda *refs: attend_back_kernel(dims, cut, *refs),
        out_shape=(
            jax.ShapeDtypeStruct((BLOCKS, BLOCK, q_cols + 2 * HEAD), BF16),
            jax.ShapeDtypeStruct((early, 2, shard, cut), BF16),
            jax.ShapeDtypeStruct((early, 2, half, shard, cols - cut), BF16),
            jax.ShapeDtypeStruct((late, 2, half, shard, cols), BF16),
            jax.ShapeDtypeStruct((2, shard, cut), BF16),
            jax.ShapeDtypeStruct((1, HEAD), F32),
            jax.ShapeDtypeStruct((1, HEAD), F32),
        ),
        in_specs=[SMEM_SPEC] + [VMEM_SPEC] * 13 + [ANY_SPEC],
        out_specs=(VMEM_SPEC,) * 7,
        scratch_shapes=[
            V((BLOCKS * BLOCK // UNIT, UNIT, q_cols - HEAD), BF16),
            V((BLOCKS, heads * BLOCK, HEAD), F32), V((BLOCKS, BLOCK, HEAD), F32), V((BLOCKS, BLOCK, HEAD), F32),
            V((early, 2, half, shard, cut), BF16), V((early, 2, half, shard, cols - cut), BF16), V((late, 2, half, shard, cols), BF16),
            V((early, 2, half, shard, cols - cut), BF16), V((late, 2, half, shard, cols), BF16), V((early, 2, more, shard, cut), BF16),
            DMA((early, 2, half)), DMA((early, 2, half)), DMA((late, 2, half)),
            DMA((early, 2, half)), DMA((early, 2, half)), DMA((late, 2, half)), DMA((late, 2, half)),
            DMA((early, 2, more)), DMA((early, 2, more)), DMA((nz, nc)), DMA((nz, nc)), DMA((2,)), DMA((1,)),
        ],
        compiler_params=pltpu.CompilerParams(collective_id=3, has_side_effects=True, vmem_limit_bytes=VMEM_LIMIT),
        cost_estimate=pl.CostEstimate(flops=2 * 20 * BLOCK * BLOCK * heads * 5 * HEAD, bytes_accessed=40 * 2**20, transcendentals=0),
    )(block, q, k, v, o, l, do, pre, cos, sin, qg, kg, re, dr, g)
def column_parts(dims, hidden, q_cols):
    return (0, hidden, 2 * hidden, 3 * hidden, 3 * hidden + q_cols)


def feed_kernel(dims, x_ref, dy_ref, o_ref, w_ref, gain_ref, out_ref, dh_ref, fg_ref, do_ref, dr_ref, g_ref, re_ref,
                wb, hs, b_ref, da_ref, dgu, u_ref, acc, dacc, snd, rcv, dos, bt, yt, at,
                ls, gs, ss, sr, xs, xr, fss, fsr, os, orr, ps, pr):
    fs, nc, nz = dims
    f, c, z = lax.axis_index("fsdp"), lax.axis_index("ctx"), lax.axis_index("tp")
    o = 1 - c
    rows, width = x_ref.shape
    q_cols = o_ref.shape[3]
    hidden = (w_ref.shape[2] - q_cols) // 3
    gate, up_, down_, out_, end = column_parts(dims, hidden, q_cols)
    edge = (z == 0) | (z == nz - 1)
    last = jnp.where(z == 0, nz - 1, 0)
    keep = down_
    rest = pl.ds(keep, end - keep)

    def loads(act):
        for zz in range(nz):
            here = edge & (last == zz)

            @pl.when(here)
            def _():
                act(pltpu.make_async_copy(w_ref.at[zz, :, rest], wb.at[zz, :, rest], ls.at[zz]))

            @pl.when(jnp.logical_not(here))
            def _():
                act(pltpu.make_async_copy(w_ref.at[zz], wb.at[zz], ls.at[zz]))
    loads(lambda cp: cp.start())
    barrier = pltpu.get_barrier_semaphore()
    pl.semaphore_signal(barrier, inc=1, device_id={"ctx": o}, device_id_type=MESH)
    for dz in range(1, nz):
        pl.semaphore_signal(barrier, inc=1, device_id={"tp": lax.rem(z + dz, nz)}, device_id_type=MESH)
    bits = bit_orders(fs)[0]
    stages = len(bits)
    for bit in bits:
        pl.semaphore_signal(barrier, inc=1, device_id={"fsdp": flip(f, bit)}, device_id_type=MESH)
    pl.semaphore_wait(barrier, nz + len(bits))
    early = early_parts(nz)
    shard = width // (fs * nc)

    def shard_rows(g, hi, n=1):
        return pl.ds(pl.multiple_of((g * nc + hi) * shard, shard), n * shard)

    def outward(way):
        part = 0 if way == 0 else nz - 1
        to = jnp.minimum(z + 1, nz - 1) if way == 0 else jnp.maximum(z - 1, 0)
        ref = shard_rows(f, 0, nc)
        return remote(w_ref.at[part, ref, pl.ds(0, keep)], wb.at[part, ref, pl.ds(0, keep)], os.at[way], orr.at[0], tp=to)
    pl.when(z == nz - 2)(outward(0).start)
    pl.when(z == 1)(outward(1).start)

    def late_plane(hi, stage):
        return plane_copies(hi, stage, fs, f, lambda g: wb.at[last, shard_rows(g, hi), pl.ds(0, keep)], ps.at[hi], pr.at[hi])

    def late_arrive():
        @pl.when(edge)
        def _():
            ref = shard_rows(f, 0, nc)
            remote(w_ref.at[0, ref, pl.ds(0, keep)], wb.at[last, ref, pl.ds(0, keep)], os.at[0], orr.at[0], ctx=o).wait_recv()
            for hi in range(2):
                for cp in late_plane(hi, 0):
                    cp.start()

    def late_spread(stage):
        @pl.when(edge)
        def _():
            for hi in range(2):
                for cp in late_plane(hi, stage):
                    cp.wait_recv()
                if stage + 1 < stages:
                    for cp in late_plane(hi, stage + 1):
                        cp.start()

    def first(e, hi):
        def view(g):
            return wb.at[early[e], shard_rows(g, hi), pl.ds(0, out_)]
        return first_copies(hi, fs, f, view, lambda i: re_ref.at[e, hi, i], fss.at[e, hi], fsr.at[e, hi])

    def cross(i, src, dst):
        return remote(src, dst, ss.at[i], sr.at[i], ctx=o)
    loads(lambda cp: cp.wait())

    def project(side):
        total = dot(o_ref[0, side], wb[0, :, out_:end], NT)
        for zz in range(1, nz):
            total += dot(o_ref[zz, side], wb[zz, :, out_:end], NT)
        return total
    snd[0] = project(o).astype(BF16)
    cross(0, snd.at[0], rcv.at[0]).start()
    own = project(c)
    cross(0, snd.at[0], rcv.at[0]).wait_recv()
    h = x_ref[...].astype(F32) + own + rcv[0].astype(F32)
    hs[...] = h
    b_ref[c] = (h * lax.rsqrt(jnp.mean(h * h, axis=-1, keepdims=True) + EPS) * gain_ref[...]).astype(BF16)
    cross(1, b_ref.at[c], b_ref.at[c]).start()
    yt[...] = dy_ref[...].reshape(nc * rows, width).T
    late_arrive()
    cross(1, b_ref.at[c], b_ref.at[o]).wait_recv()

    @pl.loop(0, nz)
    def _(i):
        zz = jnp.where(z == nz - 1, nz - 1 - i, i)

        @pl.when(i == 1)
        def _():
            late_spread(0)

        @pl.when(i == nz - 1)
        def _():
            for stage in range(1, stages):
                late_spread(stage)
        both = b_ref[...].reshape(nc * rows, width)
        gu = dot(both, wb[zz, :, gate:down_], NN)
        du = dot(dy_ref[...].reshape(nc * rows, width), wb[zz, :, down_:out_], NN)
        gt, uv = gu[:, :hidden], gu[:, hidden:]
        sig = 1.0 / (1.0 + jnp.exp(-gt))
        silu = gt * sig
        hid = (silu * uv).astype(BF16)
        u_ref[zz] = hid
        dgu[zz, :, :hidden] = (du * uv * sig * (1.0 + gt * (1.0 - sig))).astype(BF16)
        dgu[zz, :, hidden:] = (du * silu).astype(BF16)

        @pl.when(i == 0)
        def _():
            acc[...] = dot(hid, wb[zz, :, down_:out_], NT)
            dacc[...] = dot(dgu[zz], wb[zz, :, gate:down_], NT)

        @pl.when(i > 0)
        def _():
            acc[...] += dot(hid, wb[zz, :, down_:out_], NT)
            dacc[...] += dot(dgu[zz], wb[zz, :, gate:down_], NT)

    def side_rows(side):
        return pl.ds(pl.multiple_of(side * rows, 128), rows)
    snd[1] = dacc[side_rows(o)].astype(BF16)
    cross(2, snd.at[1], rcv.at[1]).start()
    snd[2] = acc[side_rows(o)].astype(BF16)
    cross(3, snd.at[2], rcv.at[2]).start()
    bt[...] = b_ref[...].reshape(nc * rows, width).T

    @pl.when(edge)
    def _():
        for hi in range(2):
            for stage in range(stages):
                for cp in late_plane(hi, stage):
                    cp.wait_send()

    def feed_grads(zz):
        wb[zz, :, gate:down_] = dot(bt[...], dgu[zz], NN).astype(BF16)
        wb[zz, :, down_:out_] = dot(yt[...], u_ref[zz], NN).astype(BF16)

    def early_grads(e):
        feed_grads(early[e])
        for hi in range(2):
            for cp in first(e, hi):
                cp.start()
    early_grads(0)
    cross(2, snd.at[1], rcv.at[1]).wait_recv()
    db = dacc[side_rows(c)] + rcv[1].astype(F32)
    h = hs[...]
    inv = lax.rsqrt(jnp.mean(h * h, axis=-1, keepdims=True) + EPS)
    n = h * inv
    sc = db * gain_ref[...]
    dh = dy_ref[c].astype(F32) + inv * (sc - n * jnp.mean(sc * n, axis=-1, keepdims=True))
    fg_ref[...] = jnp.sum(db * n, axis=0, keepdims=True)
    dh_ref[...] = dh
    da_ref[c] = dh.astype(BF16)
    cross(4, da_ref.at[c], da_ref.at[c]).start()
    for e in range(1, len(early)):
        early_grads(e)
    cross(3, snd.at[2], rcv.at[2]).wait_recv()
    out_ref[...] = (hs[...] + acc[side_rows(c)] + rcv[2].astype(F32)).astype(BF16)
    cross(4, da_ref.at[c], da_ref.at[o]).wait_recv()

    @pl.loop(1, nz + 1)
    def _(dz):
        to = lax.rem(z + dz, nz)
        both = dot(da_ref[...].reshape(nc * rows, width), wb[to, :, out_:end], NN).astype(BF16).reshape(nc, rows, q_cols)
        dos[to] = both[:, :, :HEAD]
        dr_ref[to] = both[:, :, HEAD:]

        @pl.when(dz < nz)
        def _():
            for side in range(nc):
                remote(dos.at[to, side], do_ref.at[side, z], xs.at[dz, side], xr.at[z, side], tp=to).start()
    for side in range(nc):
        do_ref[side, z] = dos[z, side]
    at[...] = da_ref[...].reshape(nc * rows, width).T
    for zz in early + late_parts(nz):
        wb[zz, :, out_:end] = dot(at[...], o_ref[zz].reshape(nc * rows, q_cols), NN).astype(BF16)
        if zz not in early:
            feed_grads(zz)
        pltpu.make_async_copy(wb.at[zz], g_ref.at[zz], gs.at[zz]).start()
    for zz in range(nz):
        pltpu.make_async_copy(wb.at[zz], g_ref.at[zz], gs.at[zz]).wait()
    for dz in range(1, nz):
        src = lax.rem(z + dz, nz)
        for side in range(nc):
            cp = remote(dos.at[0, side], do_ref.at[side, src], xs.at[dz, side], xr.at[src, side], tp=src)
            cp.wait_recv()
            cp.wait_send()
    pl.when(z == nz - 2)(outward(0).wait_send)
    pl.when(z == 1)(outward(1).wait_send)
    for e in range(len(early)):
        for hi in range(2):
            for cp in first(e, hi):
                cp.wait_recv()
                cp.wait_send()
    for i, part in enumerate((snd.at[0], b_ref.at[c], snd.at[1], snd.at[2], da_ref.at[c])):
        cross(i, part, part).wait_send()


def feed_call(dims, x, dyp, o, w, gain):
    fs, nc, nz = dims
    rows, width = x.shape
    q_cols = o.shape[3]
    cols = w.shape[2]
    hidden = (cols - q_cols) // 3
    early = len(early_parts(nz))
    DMA = pltpu.SemaphoreType.DMA
    V = pltpu.VMEM
    return pl.pallas_call(
        lambda *refs: feed_kernel(dims, *refs),
        out_shape=(
            jax.ShapeDtypeStruct((rows, width), BF16),
            jax.ShapeDtypeStruct((rows, width), F32),
            jax.ShapeDtypeStruct((1, width), F32),
            jax.ShapeDtypeStruct((nc, nz, rows, HEAD), BF16),
            jax.ShapeDtypeStruct((nz, nc, rows, q_cols - HEAD), BF16),
            jax.ShapeDtypeStruct(w.shape, BF16),
            jax.ShapeDtypeStruct((early, 2, fs // 2, width // (fs * nc), 3 * hidden), BF16),
        ),
        in_specs=[VMEM_SPEC] * 3 + [ANY_SPEC, VMEM_SPEC],
        out_specs=(VMEM_SPEC,) * 5 + (ANY_SPEC, ANY_SPEC),
        scratch_shapes=[
            V(w.shape, BF16), V((rows, width), F32), V((nc, rows, width), BF16), V((nc, rows, width), BF16),
            V((nz, nc * rows, 2 * hidden), BF16), V((nz, nc * rows, hidden), BF16),
            V((nc * rows, width), F32), V((nc * rows, width), F32),
            V((3, rows, width), BF16), V((3, rows, width), BF16), V((nz, nc, rows, HEAD), BF16),
            V((width, nc * rows), BF16), V((width, nc * rows), BF16), V((width, nc * rows), BF16),
            DMA((nz,)), DMA((nz,)), DMA((5,)), DMA((5,)), DMA((nz, nc)), DMA((nz, nc)),
            DMA((early, 2, fs // 2)), DMA((early, 2, fs // 2)),
            DMA((2,)), DMA((1,)), DMA((2, fs - 1)), DMA((2, fs - 1)),
        ],
        compiler_params=pltpu.CompilerParams(collective_id=2, has_side_effects=True, vmem_limit_bytes=VMEM_LIMIT),
        cost_estimate=pl.CostEstimate(flops=2 * 13 * 2**30, bytes_accessed=40 * 2**20, transcendentals=0),
    )(x, dyp, o, w, gain)
def line_events(nz):
    out = []
    for z in range(nz):
        events = [(z + nz - 1 - t, 0, t) for t in range(z + 1, nz)] + [(nz - 1 - z + t, 1, t) for t in range(z)]
        out.append([(way, t) for _, way, t in sorted(events)])
    return out


def at_place(z, rows):
    return pick(z, rows)


def finish_kernel(dims, cut, d_ref, wall_ref, a_ref, x_ref, dh_ref, gain_ref, te_ref, to_ref, tl_ref, ch_ref, fg_ref, qgg_ref, kgg_ref, g_ref,
                  ig_ref, dwq_ref, dwz_ref, gains_ref,
                  pa, sib, ru, snd, rq, wq, rw, tw, hx, rx, rno, rn, fin, share, sc_, gx, gy,
                  lx, xs, xr, os, orr, bs, br, us, ur, qs, qr, vs, vr, ns, nr, cs, cr, hs, hr):
    fs, nc, nz = dims
    f, c, z = lax.axis_index("fsdp"), lax.axis_index("ctx"), lax.axis_index("tp")
    o = 1 - c
    me = f * nc + c
    rows, width = x_ref.shape
    shard = dwq_ref.shape[1]
    early, late, final = early_parts(nz), late_parts(nz)[:-1], late_parts(nz)[-1]
    stages = fs.bit_length() - 1
    rest = pl.ds(cut, tw.shape[-1] - cut)
    others = [(df, dc) for df in range(fs) for dc in range(nc) if (df, dc) != (0, 0)]
    barrier = pltpu.get_barrier_semaphore()
    for df, dc in others:
        pl.semaphore_signal(barrier, inc=1, device_id={"fsdp": lax.rem(f + df, fs), "ctx": lax.rem(c + dc, nc)}, device_id_type=MESH)
    for dz in range(1, nz):
        pl.semaphore_signal(barrier, inc=1, device_id={"tp": lax.rem(z + dz, nz)}, device_id_type=MESH)
    own = []
    for hi in range(2):
        for i, m in enumerate(reduce_masks(fs, hi)):
            own.append(pltpu.make_async_copy(g_ref.at[final, flip(f, m), hi], hx.at[hi, i], lx.at[hi, i]))
    for cp in own:
        cp.start()
    pl.semaphore_wait(barrier, len(others) + nz - 1)

    def last(hi):
        return first_copies(hi, fs, f, lambda g: g_ref.at[final, g, hi], lambda i: rx.at[hi, i], xs.at[hi], xr.at[hi])

    def later_rest(e, hi, stage):
        return later_copies(hi, stage, fs, f, lambda i: to_ref.at[e, hi, i], lambda i: rno.at[e, hi, i], os.at[e, hi], orr.at[e, hi])

    def later(j, hi, stage):
        held = (lambda i: tl_ref.at[j, hi, i]) if j < len(late) else (lambda i: hx.at[hi, i])
        return later_copies(hi, stage, fs, f, held, lambda i: rn.at[j, hi, i], ns.at[j, hi], nr.at[j, hi])

    def begin(copies):
        for cp in copies:
            cp.start()
    for hi in range(2):
        begin(last(hi))
        if stages > 1:
            for e in range(len(early)):
                begin(later_rest(e, hi, 1))
            for j in range(len(late)):
                begin(later(j, hi, 1))

    def reduce_last():
        for cp in own:
            cp.wait()
        for hi in range(2):
            for cp in last(hi):
                cp.wait_recv()
            hx[hi] = add_low(hx[hi], rx[hi])
            if stages > 1:
                begin(later(len(late), hi, 1))

    def reduce_more(copies, held, got, done):
        for stage in range(1, stages):
            keep = fs >> (stage + 1)
            base = fs // 2 - (fs >> stage)
            for cp in copies(stage):
                cp.wait_recv()
            if stage + 1 == stages:
                done(add_low(held[0], got[base]))
            else:
                held[:keep] = add_low(held[:keep], got[base:base + keep])
                begin(copies(stage + 1))
        if stages == 1:
            done(held[0])

    def put(t, hi, where):
        def done(value):
            tw[t, hi, :, where] = value
        return done

    def reduce_rest():
        for hi in range(2):
            for e in range(len(early)):
                reduce_more(lambda stage: later_rest(e, hi, stage), to_ref.at[e, hi], rno.at[e, hi], put(early[e], hi, rest))
            for j, t in enumerate(late + (final,)):
                held = tl_ref.at[j, hi] if j < len(late) else hx.at[hi]
                reduce_more(lambda stage: later(j, hi, stage), held, rn.at[j, hi], put(t, hi, slice(None)))

    order = sorted(range(nz), key=lambda t: (min(t, nz - 1 - t), -t))

    def cross(t):
        return remote(snd.at[t], sib.at[t], bs.at[t], br.at[t], ctx=o)

    @pl.loop(0, nz)
    def _(i):
        t = pick(i, order)
        snd[t] = dot(d_ref[o * nz + t], wall_ref[...], NT).astype(BF16)
        cross(t).start()
        pa[t] = dot(d_ref[c * nz + t], wall_ref[...], NT)

    @pl.loop(0, nz)
    def _(i):
        t = pick(i, order)
        cross(t).wait_recv()
        pa[t] += sib[t].astype(F32)

    events = line_events(nz)

    def event(i):
        way = at_place(z, [events[zz][i][0] for zz in range(nz)])
        t = at_place(z, [events[zz][i][1] for zz in range(nz)])
        arrives = jnp.where(way == 0, z > 0, z < nz - 1)
        to = jnp.where(way == 0, jnp.minimum(z + 1, nz - 1), jnp.maximum(z - 1, 0))
        slot = jnp.where((way == 1) & (t == to), nz, t)
        return t, arrives, to, slot

    def rows_copy(i):
        t, _, to, slot = event(i)
        return remote(snd.at[t], ru.at[slot], us.at[i], ur.at[slot], tp=to)

    def rows_event(i):
        t, arrives, _, _ = event(i)
        cross(t).wait_send()

        @pl.when(arrives)
        def _():
            remote(snd.at[t], ru.at[t], us.at[i], ur.at[t], ctx=o).wait_recv()
            snd[t] = (pa[t] + ru[t].astype(F32)).astype(BF16)

        @pl.when(jnp.logical_not(arrives))
        def _():
            snd[t] = pa[t].astype(BF16)
        rows_copy(i).start()

    def weights(r):
        return pl.ds(pl.multiple_of(r * shard, shard), shard)

    rows_event(0)
    wq[...] = jnp.zeros_like(wq)

    @pl.loop(0, nc * nz)
    def _(s):
        wq[...] += dot(a_ref[s], d_ref[s], TN)
    rq[me] = wq[weights(me)].astype(BF16)
    for i, (df, dc) in enumerate(others):
        tf, tc = lax.rem(f + df, fs), lax.rem(c + dc, nc)
        sc_[i] = wq[weights(tf * nc + tc)].astype(BF16)
        remote(sc_.at[i], rq.at[me], qs.at[i], qr.at[me], fsdp=tf, ctx=tc).start()
    for e in range(len(early)):
        tw[early[e], :, :, :cut] = te_ref[e]

    @pl.when(z == 1)
    def _():
        rw[nz - 1, :, :, :cut] = ch_ref[...]

    @pl.when(z == nz - 2)
    def _():
        rw[0, :, :, :cut] = ch_ref[...]
    reduce_last()
    for i in range(1, nz - 1):
        rows_event(i)

    reduce_rest()
    firsts = ((z == 0), (z == nz - 1))

    def grads_copy(i, part=None):
        t, _, to, slot = event(i)
        src, dst = (tw.at[t], rw.at[slot]) if part is None else (tw.at[t, :, :, part], rw.at[slot, :, :, part])
        return remote(src, dst, vs.at[i], vr.at[slot], tp=to)

    def grads_came(i, t, part=None):
        src, dst = (tw.at[t], rw.at[t]) if part is None else (tw.at[t, :, :, part], rw.at[t, :, :, part])
        remote(src, dst, vs.at[i], vr.at[t], ctx=o).wait_recv()

    def leads(i):
        t = event(i)[0]
        return ((z == 0) & (t == nz - 1)) | ((z == nz - 1) & (t == 0))

    def follows(i):
        t = event(i)[0]
        return ((z == 1) & (t == nz - 1)) | ((z == nz - 2) & (t == 0))

    def grads_event(i):
        t, arrives, _, _ = event(i)

        @pl.when(arrives)
        def _():
            pl.when(follows(i))(lambda: grads_came(i, t, rest))
            pl.when(jnp.logical_not(follows(i)))(lambda: grads_came(i, t))
            tw[t] = add_low(tw[t], rw[t])
        pl.when(leads(i))(lambda: grads_copy(i, rest).start())
        pl.when(jnp.logical_not(leads(i)))(lambda: grads_copy(i).start())
    grads_event(0)

    def rows_arrival(way):
        slot = nz if way else z
        return remote(snd.at[0], ru.at[slot], us.at[0], ur.at[slot], ctx=o)

    @pl.when(z > 0)
    def _():
        rows_arrival(0).wait_recv()
        pa[z] += ru[z].astype(F32)

    @pl.when(z < nz - 1)
    def _():
        rows_arrival(1).wait_recv()
        pa[z] += ru[nz].astype(F32)
    da = pa[z]
    x = x_ref[...].astype(F32)
    inv = lax.rsqrt(jnp.mean(x * x, axis=-1, keepdims=True) + EPS)
    n = x * inv
    sc = da * gain_ref[...]
    ig_ref[...] = dh_ref[...] + inv * (sc - n * jnp.mean(sc * n, axis=-1, keepdims=True))
    gx[z, 0:1] = jnp.sum(da * n, axis=0, keepdims=True)
    gx[z, 1:2] = fg_ref[...]
    gx[z, 2:3] = jnp.concatenate([qgg_ref[...], kgg_ref[...]] + [jnp.zeros((1, width - 2 * HEAD), F32)], axis=1)
    gx[z, 3:] = jnp.zeros_like(gx[z, 3:])
    for dz in range(1, nz):
        to = lax.rem(z + dz, nz)
        remote(gx.at[z], gx.at[z], hs.at[dz - 1], hr.at[z], tp=to).start()
    for i in range(1, nz - 1):
        grads_event(i)

    for i, (df, dc) in enumerate(others):
        src = lax.rem(f + df, fs) * nc + lax.rem(c + dc, nc)
        remote(sc_.at[0], rq.at[src], qs.at[i], qr.at[src], ctx=o).wait_recv()
    for cc in range(nc):
        total = rq[cc].astype(F32)
        for ff in range(1, fs):
            total += rq[ff * nc + cc].astype(F32)
        dwq_ref[cc] = total

    def grads_arrival(way):
        slot = nz if way else z
        return remote(tw.at[0], rw.at[slot], vs.at[0], vr.at[slot], ctx=o)

    for dz in range(1, nz):
        src = lax.rem(z + dz, nz)
        remote(gx.at[src], gx.at[src], hs.at[dz - 1], hr.at[src], tp=src).wait_recv()
    total = gx[0]
    for zz in range(1, nz):
        total += gx[zz]
    gy[me] = total
    for i, (df, dc) in enumerate(others):
        remote(gy.at[me], gy.at[me], hs.at[nz - 1 + i], hr.at[nz + me], fsdp=lax.rem(f + df, fs), ctx=lax.rem(c + dc, nc)).start()

    fin[...] = tw[z].astype(F32)

    @pl.when(z > 0)
    def _():
        grads_arrival(0).wait_recv()
        fin[...] += rw[z].astype(F32)

    @pl.when(z < nz - 1)
    def _():
        grads_arrival(1).wait_recv()
        fin[...] += rw[nz].astype(F32)
    share[0] = fin[o].astype(BF16)
    swap = remote(share.at[0], share.at[1], cs.at[0], cr.at[0], ctx=o)
    swap.start()
    dwz_ref[c] = fin[c]

    for i, (df, dc) in enumerate(others):
        src = lax.rem(f + df, fs) * nc + lax.rem(c + dc, nc)
        remote(gy.at[src], gy.at[src], hs.at[nz - 1 + i], hr.at[nz + src], ctx=o).wait_recv()
    total = gy[0]
    for r in range(1, fs * nc):
        total += gy[r]
    gains_ref[...] = total
    swap.wait_recv()
    dwz_ref[o] = share[1].astype(F32)

    swap.wait_send()
    for i in range(nz - 1):
        rows_copy(i).wait_send()
        pl.when(leads(i))(lambda: grads_copy(i, rest).wait_send())
        pl.when(jnp.logical_not(leads(i)))(lambda: grads_copy(i).wait_send())
    cross(z).wait_send()
    for i in range(nz - 1):
        remote(gx.at[0], gx.at[0], hs.at[i], hr.at[0], ctx=o).wait_send()
    for i in range(len(others)):
        remote(sc_.at[0], rq.at[0], qs.at[i], qr.at[0], ctx=o).wait_send()
        remote(gy.at[0], gy.at[0], hs.at[nz - 1 + i], hr.at[nz], ctx=o).wait_send()
    for hi in range(2):
        for cp in last(hi):
            cp.wait_send()
        for stage in range(1, stages):
            for e in range(len(early)):
                for cp in later_rest(e, hi, stage):
                    cp.wait_send()
            for j in range(len(late) + 1):
                for cp in later(j, hi, stage):
                    cp.wait_send()


def finish_call(dims, d, wall, a, x, dh, gain, te, to, tl, ch, fg, qgg, kgg, g):
    fs, nc, nz = dims
    rows, width = x.shape
    shard, cols = g.shape[3:]
    cut = te.shape[3]
    early = te.shape[0]
    half, more = fs // 2, max(fs // 2 - 1, 1)
    proj = wall.shape[1]
    late = len(late_parts(nz))
    n = fs * nc
    DMA = pltpu.SemaphoreType.DMA
    V = pltpu.VMEM
    return pl.pallas_call(
        lambda *refs: finish_kernel(dims, cut, *refs),
        out_shape=(
            jax.ShapeDtypeStruct((rows, width), F32),
            jax.ShapeDtypeStruct((nc, width // n, proj), F32),
            jax.ShapeDtypeStruct((nc, shard, cols), F32),
            jax.ShapeDtypeStruct((8, width), F32),
        ),
        in_specs=[VMEM_SPEC] * 13 + [ANY_SPEC],
        out_specs=(VMEM_SPEC,) * 4,
        scratch_shapes=[
            V((nz, rows, width), F32), V((nz, rows, width), BF16), V((nz + 1, rows, width), BF16),
            V((nz, rows, width), BF16),
            V((n, width // n, proj), BF16), V((width, proj), F32),
            V((nz + 1, 2, shard, cols), BF16), V((nz, 2, shard, cols), BF16),
            V((2, half, shard, cols), BF16), V((2, half, shard, cols), BF16),
            V((early, 2, more, shard, cols - cut), BF16), V((late, 2, more, shard, cols), BF16),
            V((2, shard, cols), F32), V((2, shard, cols), BF16),
            V((n - 1, width // n, proj), BF16), V((nz, 8, width), F32), V((n, 8, width), F32),
            DMA((2, half)), DMA((2, half)), DMA((2, half)), DMA((early, 2, more)), DMA((early, 2, more)),
            DMA((nz,)), DMA((nz,)), DMA((nz - 1,)), DMA((nz + 1,)),
            DMA((n - 1,)), DMA((n,)), DMA((nz - 1,)), DMA((nz + 1,)),
            DMA((late, 2, max(fs // 2 - 1, 1))), DMA((late, 2, max(fs // 2 - 1, 1))),
            DMA((1,)), DMA((1,)), DMA((nz - 1 + n - 1,)), DMA((nz + n,)),
        ],
        compiler_params=pltpu.CompilerParams(collective_id=4, has_side_effects=True, vmem_limit_bytes=VMEM_LIMIT),
        cost_estimate=pl.CostEstimate(flops=2 * 4 * 2**30, bytes_accessed=40 * 2**20, transcendentals=0),
    )(d, wall, a, x, dh, gain, te, to, tl, ch, fg, qgg, kgg, g)
def unpack_kernel(parts, result_ref, ig_ref, gains_ref, dwq_ref, dwz_ref, *outs):
    outs[0][...] = result_ref[...]
    outs[1][...] = ig_ref[...]
    outs[2][...] = gains_ref[0:1]
    outs[3][...] = gains_ref[1:2]
    outs[4][...] = gains_ref[2:3, :HEAD]
    outs[5][...] = gains_ref[2:3, HEAD:2 * HEAD]
    for (which, at, step, turned), out in zip(parts, outs[6:]):
        ref = (dwq_ref, dwz_ref)[which]
        value = jnp.concatenate([ref[cc, :, at:at + step] for cc in range(ref.shape[0])], axis=1)
        out[...] = value.T if turned else value


def unpack_call(result, ig, gains, dwq, dwz, hidden, q_cols):
    nc, shard, _ = dwq.shape
    parts = ((0, 0, q_cols, False), (0, q_cols, HEAD, False), (0, q_cols + HEAD, HEAD, False),
             (1, 3 * hidden, q_cols, True), (1, 0, hidden, False), (1, hidden, hidden, False), (1, 2 * hidden, hidden, True))
    width = gains.shape[1]
    shapes = [(shard, nc * step)[::-1] if turned else (shard, nc * step) for _, _, step, turned in parts]
    return pl.pallas_call(
        lambda *refs: unpack_kernel(parts, *refs),
        out_shape=[jax.ShapeDtypeStruct(result.shape, BF16), jax.ShapeDtypeStruct(ig.shape, F32)]
        + [jax.ShapeDtypeStruct((1, n), F32) for n in (width, width, HEAD, HEAD)]
        + [jax.ShapeDtypeStruct(shape, F32) for shape in shapes],
        in_specs=[VMEM_SPEC] * 5,
        out_specs=[VMEM_SPEC] * 13,
        compiler_params=pltpu.CompilerParams(vmem_limit_bytes=VMEM_LIMIT),
    )(result, ig, gains, dwq, dwz)


def on_device(dims, tokens, out_grad, block_slot, attn_gain, ffn_gain, query_gain, key_norm_gain,
              w_query, key_weight, value_weight, w_out, w_gate, w_up, w_down):
    fs, nc, nz = dims
    rows, width = tokens.shape
    shard = w_query.shape[0]
    block_ids = block_slot[0]
    cos, sins = rope_tables()
    hidden, q_cols = w_gate.shape[1] // nc, w_query.shape[1] // nc
    ag, fg = attn_gain[None], ffn_gain[None]
    qg, kg = query_gain[None], key_norm_gain[None]
    weights = (w_query, key_weight, value_weight, w_gate, w_up, w_down, w_out)
    a, q, k, v, pre, wall, w, dyp = gather_call(dims, block_ids, tokens, out_grad, ag, weights, cos, sins, qg, kg)
    blocks = lambda t: t.reshape(BLOCKS, BLOCK, -1)
    q, k, v, pre = blocks(q), blocks(k), blocks(v), blocks(pre)
    w, mixed, o, logs = attend_call(dims, 2 * hidden, block_ids, q, k, v, w, rows)
    cols = w.shape[4]
    result, dh, ffn_part, do, dr, g, re = feed_call(dims, tokens, dyp, mixed, w.reshape(nz, width, cols), fg)
    g = g.reshape(nz, fs, nc, shard, cols)
    dr = dr.reshape(nz, nc, rows // UNIT, UNIT, q_cols - HEAD)
    d, te, to, tl, ch, q_part, k_part = attend_back_call(
        dims, block_ids, q, k, v, blocks(o), logs, blocks(do), pre, cos, sins, qg, kg, re, dr, g)
    input_grad, dwq, dwz, gains = finish_call(
        dims, d.reshape(nc * nz, rows, -1), wall.reshape(width, -1), a, tokens, dh, ag, te, to, tl, ch, ffn_part, q_part, k_part, g)
    outs = unpack_call(result, input_grad, gains, dwq, dwz, hidden, q_cols)
    return tuple(t[0] if 2 <= i < 6 else t for i, t in enumerate(outs))


def solution(mesh):
    dims = (mesh.shape["fsdp"], mesh.shape["ctx"], mesh.shape["tp"])
    everything, weights = ("fsdp", "ctx", "tp"), ("fsdp", "ctx")
    split, turned = P(weights, "tp"), P("tp", weights)
    return jax.shard_map(
        lambda *args: on_device(dims, *args),
        mesh=mesh,
        in_specs=(P(everything, None), P(everything, None), P("fsdp", None), P(), P(), P(), P(), split, split, split, turned, split, split, turned),
        out_specs=(P(everything, None), P(everything, None), P(), P(), P(), P(), split, split, split, turned, split, split, turned),
        check_vma=False,
    )
```

```python
import numpy as np
import jax
import jax.numpy as jnp
from jax import lax
from jax.experimental import pallas as pl
from jax.experimental.pallas import tpu as pltpu
from jax.sharding import PartitionSpec as P

HEAD = 128
BLOCK = 512
PBLOCKS = 4
BLOCKS = 6
EPS = 1e-6
ROPE_BASE = 1e6
MESH = pl.DeviceIdType.MESH
F32, BF16 = jnp.float32, jnp.bfloat16
LOG2E = 1.4426950408889634
QSCALE = HEAD ** -0.5 * LOG2E
VMEM_SPEC = pl.BlockSpec(memory_space=pltpu.VMEM)
ANY_SPEC = pl.BlockSpec(memory_space=pl.ANY)
SMEM_SPEC = pl.BlockSpec(memory_space=pltpu.SMEM)
VMEM_LIMIT = 60 * 2**20


def dot(a, b, dims):
    return lax.dot_general(a, b, (dims, ((), ())), preferred_element_type=F32)


NN = ((1,), (0,))
NT = ((1,), (1,))
TN = ((0,), (0,))


def flip(f, mask):
    bit = 1
    while bit <= mask:
        if mask & bit:
            f = f + bit - 2 * bit * lax.rem(lax.div(f, bit), 2)
        bit *= 2
    return f


def remote(src, dst, send, recv, **where):
    return pltpu.make_async_remote_copy(
        src_ref=src, dst_ref=dst, send_sem=send, recv_sem=recv,
        device_id=where, device_id_type=MESH)


def pick(index, values):
    out = jnp.int32(values[-1])
    for k in range(len(values) - 1):
        out = jnp.where(index == k, jnp.int32(values[k]), out)
    return out


def near_order(n):
    return [sorted(range(n), key=lambda s: (abs(s - z), s)) for z in range(n)]


def bit_orders(fs):
    bits = [1 << b for b in range(fs.bit_length() - 1)]
    return bits, bits[::-1]


def combos(bits):
    out = [0]
    for b in bits:
        out = out + [m + b for m in out]
    return out


def plane_copies(half, stage, fs, f, view, ssem, rsem):
    order = bit_orders(fs)[half]
    partner = flip(f, order[stage])
    base = (1 << stage) - 1
    out = []
    for m, mask in enumerate(combos(order[:stage])):
        g = flip(f, mask)
        out.append(remote(view(g), view(g), ssem.at[base + m], rsem.at[base + m], fsdp=partner))
    return out


UNIT = 128


def rope_tables():
    freqs = np.float32(ROPE_BASE) ** (-(np.arange(0, HEAD, 2, dtype=np.float32) / np.float32(HEAD)))
    places = np.arange((PBLOCKS + 1) * BLOCK, dtype=np.float32)
    angles = (places[:, None] * freqs[None, :].astype(np.float32)).astype(np.float64)
    cos, sin = np.cos(angles), np.sin(angles)
    shape = (-1, UNIT, HEAD)
    return (np.concatenate([cos, cos], axis=1).astype(np.float32).reshape(shape),
            np.concatenate([-sin, sin], axis=1).astype(np.float32).reshape(shape))


def rope_rows(table_ref, block_ref, first, count):
    per = BLOCK // UNIT
    out = []
    for i in range(count):
        unit = first + i
        out.append(table_ref[jnp.minimum(block_ref[lax.div(unit, per)], PBLOCKS) * per + lax.rem(unit, per)])
    return jnp.concatenate(out, axis=0)


def head_norm_rope(pre, gain, cos, sins):
    n = pre * lax.rsqrt(jnp.mean(pre * pre, axis=-1, keepdims=True) + EPS) * gain
    return n * cos + pltpu.roll(n, HEAD // 2, 1) * sins


def gather_kernel(dims, block_ref, x_ref, dy_ref, gain_ref, wq_in, wk_in, wv_in, wg_in, wu_in, wd_in, wo_in,
                  cos_ref, sin_ref, qg_ref, kg_ref,
                  a_ref, q_ref, k_ref, v_ref, pre_ref, wall_ref, w_ref, dyp_ref,
                  wqkv_ref, wz_ref, zs, zr, cs, cr, ws, wr, ms, mr, ps, pr, ls):
    fs, nc, nz = dims
    f, c, z = lax.axis_index("fsdp"), lax.axis_index("ctx"), lax.axis_index("tp")
    o = 1 - c
    me = f * nc + c
    others = [(df, dc) for df in range(fs) for dc in range(nc) if (df, dc) != (0, 0)]

    barrier = pltpu.get_barrier_semaphore()
    for df, dc in others:
        pl.semaphore_signal(barrier, inc=1, device_id={"fsdp": lax.rem(f + df, fs), "ctx": lax.rem(c + dc, nc)}, device_id_type=MESH)

    @pl.when(z > 0)
    def _():
        pl.semaphore_signal(barrier, inc=1, device_id={"tp": z - 1}, device_id_type=MESH)

    @pl.when(z < nz - 1)
    def _():
        pl.semaphore_signal(barrier, inc=1, device_id={"tp": z + 1}, device_id_type=MESH)
    x = x_ref[...].astype(F32)
    a_ref[c * nz + z] = (x * lax.rsqrt(jnp.mean(x * x, axis=-1, keepdims=True) + EPS) * gain_ref[...]).astype(BF16)
    pl.semaphore_wait(barrier, len(others) + jnp.where(z > 0, 1, 0) + jnp.where(z < nz - 1, 1, 0))

    row = a_ref.at[c * nz + z]
    up = remote(row, row, zs.at[z], zr.at[z], tp=jnp.minimum(z + 1, nz - 1))
    down = remote(row, row, zs.at[nz], zr.at[z], tp=jnp.maximum(z - 1, 0))
    pl.when(z < nz - 1)(up.start)
    pl.when(z > 0)(down.start)
    across = remote(row, row, cs.at[z], cr.at[z], ctx=o)
    across.start()
    dyc = remote(dy_ref, dyp_ref.at[c], ms.at[1], mr.at[1], ctx=o)
    dyc.start()
    dyp_ref[c] = dy_ref[...]

    def pack(packed, parts):
        at = 0
        for ref, turned in parts:
            value = ref[...].T if turned else ref[...]
            step = value.shape[1] // nc
            for cc in range(nc):
                packed[cc, :, at:at + step] = value[:, cc * step:(cc + 1) * step]
            at += step
    pack(wqkv_ref, ((wq_in, False), (wk_in, False), (wv_in, False)))
    wall_ref[me] = wqkv_ref[c]
    pack(wz_ref, ((wg_in, False), (wu_in, False), (wd_in, True), (wo_in, True)))
    own_w = pltpu.make_async_copy(wz_ref.at[c], w_ref.at[z, f, c], ls.at[0])
    own_w.start()
    for i, (df, dc) in enumerate(others):
        tf, tc = lax.rem(f + df, fs), lax.rem(c + dc, nc)
        remote(wqkv_ref.at[tc], wall_ref.at[me], ws.at[i], wr.at[me], fsdp=tf, ctx=tc).start()
    half = remote(wz_ref.at[o], w_ref.at[z, f, c], ms.at[0], mr.at[0], ctx=o)
    half.start()

    def plane(half_index, stage):
        return plane_copies(half_index, stage, fs, f, lambda g: w_ref.at[z, g, half_index], ps.at[half_index], pr.at[half_index])
    stages = fs.bit_length() - 1

    own_w.wait()
    remote(wz_ref.at[0], w_ref.at[z, f, o], ms.at[0], mr.at[0], ctx=o).wait_recv()
    for hi in range(2):
        for cp in plane(hi, 0):
            cp.start()
    q_cols = q_ref.shape[-1]

    def project(s):
        y = dot(a_ref[s], wall_ref[...].reshape(-1, wall_ref.shape[2]), NN)
        pre_ref[s] = y[:, :q_cols + HEAD].astype(BF16)
        units = a_ref.shape[1] // UNIT
        cos, sins = rope_rows(cos_ref, block_ref, s * units, units), rope_rows(sin_ref, block_ref, s * units, units)
        for h in range(q_cols // HEAD):
            q_ref[s, :, h * HEAD:(h + 1) * HEAD] = (head_norm_rope(y[:, h * HEAD:(h + 1) * HEAD], qg_ref[...], cos, sins) * QSCALE).astype(BF16)
        k_ref[s] = head_norm_rope(y[:, q_cols:q_cols + HEAD], kg_ref[...], cos, sins).astype(BF16)
        v_ref[s, :, :HEAD] = y[:, q_cols + HEAD:].astype(BF16)
        v_ref[s, :, HEAD:] = jnp.ones_like(v_ref[s, :, HEAD:])

    def take(hop):
        @pl.loop(0, 2 if hop == 0 else 4)
        def _(i):
            across_, way = (i, 0) if hop == 0 else (lax.rem(i, 2), lax.div(i, 2))
            src = z + (2 * way - 1) * hop

            @pl.when((src >= 0) & (src < nz))
            def _():
                s = jnp.where(across_ == 0, c, o) * nz + src

                @pl.when(across_ == 1)
                def _():
                    remote(a_ref.at[s], a_ref.at[s], cs.at[src], cr.at[src], ctx=o).wait_recv()
                project(s)

    for hop in range(1, nz):
        for way in range(2):
            src = z + (2 * way - 1) * hop

            @pl.when((src >= 0) & (src < nz))
            def _():
                part = a_ref.at[c * nz + src]
                remote(part, part, zs.at[src], zr.at[src], ctx=o).wait_recv()
                if way == 0:
                    pl.when(z < nz - 1)(remote(part, part, zs.at[src], zr.at[src], tp=jnp.minimum(z + 1, nz - 1)).start)
                else:
                    pl.when(z > 0)(remote(part, part, zs.at[src], zr.at[src], tp=jnp.maximum(z - 1, 0)).start)
                remote(part, part, cs.at[src], cr.at[src], ctx=o).start()
        if hop == 1:
            for i, (df, dc) in enumerate(others):
                src = lax.rem(f + df, fs) * nc + lax.rem(c + dc, nc)
                remote(wqkv_ref.at[0], wall_ref.at[src], ws.at[i], wr.at[src], ctx=o).wait_recv()
        take(hop - 1)
        stage = hop - 1
        if stage < stages:
            for hi in range(2):
                for cp in plane(hi, stage):
                    cp.wait_recv()
                if stage + 1 < stages:
                    for cp in plane(hi, stage + 1):
                        cp.start()
    take(nz - 1)
    for stage in range(nz - 1, stages):
        for hi in range(2):
            for cp in plane(hi, stage):
                cp.wait_recv()
            if stage + 1 < stages:
                for cp in plane(hi, stage + 1):
                    cp.start()
    for stage in range(stages):
        for hi in range(2):
            for cp in plane(hi, stage):
                cp.wait_send()
    for src in range(nz):
        @pl.when(((src <= z) & (z < nz - 1)) | ((src > z) & (z > 0)))
        def _():
            remote(row, row, zs.at[src], zr.at[src], ctx=o).wait_send()
        remote(row, row, cs.at[src], cr.at[src], ctx=o).wait_send()

    @pl.when(z > 0)
    def _():
        remote(row, row, zs.at[nz], zr.at[0], ctx=o).wait_send()
    for i in range(len(others)):
        remote(wqkv_ref.at[0], wall_ref.at[0], ws.at[i], wr.at[0], ctx=o).wait_send()
    half.wait_send()
    dyc.wait_send()
    remote(dy_ref, dyp_ref.at[o], ms.at[1], mr.at[1], ctx=o).wait_recv()


def gather_call(dims, block, x, dy, gain, weights, cos, sin, qg, kg):
    fs, nc, nz = dims
    rows, width = x.shape
    ns = nc * nz
    shard = weights[0].shape[0]
    q_cols = weights[0].shape[1] // nc
    cols = q_cols + 2 * HEAD
    wcols = 3 * (weights[3].shape[1] // nc) + q_cols
    DMA = pltpu.SemaphoreType.DMA
    return pl.pallas_call(
        lambda *refs: gather_kernel(dims, *refs),
        out_shape=(
            jax.ShapeDtypeStruct((ns, rows, width), BF16),
            jax.ShapeDtypeStruct((ns, rows, q_cols), BF16),
            jax.ShapeDtypeStruct((ns, rows, HEAD), BF16),
            jax.ShapeDtypeStruct((ns, rows, 2 * HEAD), BF16),
            jax.ShapeDtypeStruct((ns, rows, q_cols + HEAD), BF16),
            jax.ShapeDtypeStruct((fs * nc, shard, cols), BF16),
            jax.ShapeDtypeStruct((nz, fs, nc, shard, wcols), BF16),
            jax.ShapeDtypeStruct((nc, rows, width), BF16),
        ),
        in_specs=[SMEM_SPEC] + [VMEM_SPEC] * 14,
        out_specs=(VMEM_SPEC,) * 6 + (ANY_SPEC, VMEM_SPEC),
        scratch_shapes=[
            pltpu.VMEM((nc, shard, cols), BF16), pltpu.VMEM((nc, shard, wcols), BF16),
            DMA((nz + 1,)), DMA((nz,)), DMA((nz,)), DMA((nz,)),
            DMA((fs * nc - 1,)), DMA((fs * nc,)), DMA((2,)), DMA((2,)),
            DMA((2, fs - 1)), DMA((2, fs - 1)), DMA((2,)),
        ],
        compiler_params=pltpu.CompilerParams(collective_id=0, has_side_effects=True, vmem_limit_bytes=VMEM_LIMIT),
        cost_estimate=pl.CostEstimate(flops=2 * ns * rows * width * cols, bytes_accessed=30 * 2**20, transcendentals=0),
    )(block, x, dy, gain, *weights, cos, sin, qg, kg)
def full_keys(qb):
    return min(qb, PBLOCKS)


def stack_heads(rows):
    return jnp.concatenate([rows[:, h * HEAD:(h + 1) * HEAD] for h in range(rows.shape[1] // HEAD)], axis=0)


def slot_of(block_ref, b):
    out = jnp.int32(0)
    for s in range(1, BLOCKS):
        out = jnp.where(block_ref[s] == b, jnp.int32(s), out)
    return out


def attend_kernel(dims, keep, block_ref, q_ref, k_ref, v_ref, wi_ref, w_ref, or_ref, o_ref, l_ref,
                  ob, zs, zr, ps, pr, xs, xr):
    fs, nc, nz = dims
    f, c, z = lax.axis_index("fsdp"), lax.axis_index("ctx"), lax.axis_index("tp")
    rows = or_ref.shape[2]
    barrier = pltpu.get_barrier_semaphore()
    bits = bit_orders(fs)[0]
    for bit in bits:
        pl.semaphore_signal(barrier, inc=1, device_id={"fsdp": flip(f, bit)}, device_id_type=MESH)
    for dz in range(1, nz):
        pl.semaphore_signal(barrier, inc=1, device_id={"tp": lax.rem(z + dz, nz)}, device_id_type=MESH)
    pl.semaphore_wait(barrier, len(bits) + nz - 1)

    def piece(ref, hop):
        return ref.at[:, :, pl.ds(keep, ref.shape[-1] - keep)] if hop == nz - 1 else ref

    def up(src, sem, hop):
        part = piece(w_ref.at[src, f], hop)
        return remote(part, part, zs.at[sem], zr.at[src], tp=jnp.minimum(z + 1, nz - 1))

    def down(src, sem, hop):
        part = piece(w_ref.at[src, f], hop)
        return remote(part, part, zs.at[sem], zr.at[src], tp=jnp.maximum(z - 1, 0))
    pl.when(z < nz - 1)(up(z, z, 1).start)
    pl.when(z > 0)(down(z, nz, 1).start)
    stages = fs.bit_length() - 1

    def plane(src, hi, stage, hop):
        def view(g):
            ref = w_ref.at[src, g, hi]
            return ref.at[:, pl.ds(keep, ref.shape[-1] - keep)] if hop == nz - 1 else ref
        return plane_copies(hi, stage, fs, f, view, ps.at[src, hi], pr.at[src, hi])

    def each(hop, act):
        for way in range(2):
            src = z + (2 * way - 1) * hop

            @pl.when((src >= 0) & (src < nz))
            def _():
                act(way, src)

    def arrive(hop):
        def act(way, src):
            up(src, src, hop).wait_recv()
            if way == 0:
                pl.when(z < nz - 1)(up(src, src, hop + 1).start)
            else:
                pl.when(z > 0)(down(src, src, hop + 1).start)
            for hi in range(2):
                for cp in plane(src, hi, 0, hop):
                    cp.start()
        each(hop, act)

    def spread(hop, stage):
        def act(way, src):
            for hi in range(2):
                for cp in plane(src, hi, stage, hop):
                    cp.wait_recv()
                if stage + 1 < stages:
                    for cp in plane(src, hi, stage + 1, hop):
                        cp.start()
        each(hop, act)

    tri = lax.broadcasted_iota(jnp.int32, (BLOCK, BLOCK), 0) >= lax.broadcasted_iota(jnp.int32, (BLOCK, BLOCK), 1)
    heads = q_ref.shape[2] // HEAD
    for qb in range(BLOCKS):
        if qb == BLOCKS - 1:
            arrive(1)
        q2 = stack_heads(q_ref[slot_of(block_ref, qb)])

        def step(kb, acc):
            k = k_ref[slot_of(block_ref, kb)]
            v = v_ref[slot_of(block_ref, kb)]
            return acc + dot(jnp.exp2(dot(q2, k, NT)).astype(BF16), v, NN)
        acc = jnp.zeros((heads * BLOCK, 2 * HEAD), F32)
        if full_keys(qb):
            acc = lax.fori_loop(0, full_keys(qb), step, acc)
        k = k_ref[slot_of(block_ref, qb)]
        v = v_ref[slot_of(block_ref, qb)]
        s = dot(q2, k, NT)
        for h in range(heads):
            part = slice(h * BLOCK, (h + 1) * BLOCK)
            p = jnp.where(tri, jnp.exp2(s[part]), 0.0).astype(BF16)
            a = acc[part] + dot(p, v, NN)
            ob[qb, :, h * HEAD:(h + 1) * HEAD] = (a[:, :HEAD] / a[:, HEAD:]).astype(BF16)
            l_ref[qb, :, part] = jnp.log2(a[:, HEAD:]).T[0:8]
    for s in range(BLOCKS):
        o_ref[s * BLOCK:(s + 1) * BLOCK] = ob[block_ref[s]]

    def part_rows(side, zz):
        return pl.ds(pl.multiple_of((side * nz + zz) * rows, 128), rows)
    for hop in range(2, nz - 1):
        arrive(hop)
    for dz in range(1, nz):
        to = lax.rem(z + dz, nz)
        for side in range(nc):
            remote(o_ref.at[part_rows(side, to)], or_ref.at[z, side], xs.at[dz, side], xr.at[z, side], tp=to).start()
    for side in range(nc):
        or_ref[z, side] = o_ref[part_rows(side, z)]
    for hop in range(1, nz):
        for stage in range(stages):
            spread(hop, stage)
            if hop == nz - 2 and stage == 0:
                arrive(nz - 1)
    for dz in range(1, nz):
        src = lax.rem(z + dz, nz)
        for side in range(nc):
            cp = remote(o_ref.at[part_rows(side, 0)], or_ref.at[src, side], xs.at[dz, side], xr.at[src, side], tp=src)
            cp.wait_recv()
            cp.wait_send()
    for hop in range(1, nz):
        def left(way, src):
            if way == 0:
                pl.when(z < nz - 1)(up(src, src, hop + 1).wait_send)
            else:
                pl.when(z > 0)(down(src, src, hop + 1).wait_send)
            for hi in range(2):
                for stage in range(stages):
                    for cp in plane(src, hi, stage, hop):
                        cp.wait_send()
        each(hop, left)
    pl.when(z < nz - 1)(up(z, z, 1).wait_send)
    pl.when(z > 0)(down(z, nz, 1).wait_send)


def attend_call(dims, keep, block, q, k, v, w, rows):
    fs, nc, nz = dims
    q_cols = q.shape[2]
    span = BLOCKS * BLOCK
    heads = q_cols // HEAD
    DMA = pltpu.SemaphoreType.DMA
    return pl.pallas_call(
        lambda *refs: attend_kernel(dims, keep, *refs),
        out_shape=(
            jax.ShapeDtypeStruct(w.shape, BF16),
            jax.ShapeDtypeStruct((nz, nc, rows, q_cols), BF16),
            jax.ShapeDtypeStruct((span, q_cols), BF16),
            jax.ShapeDtypeStruct((BLOCKS, 8, heads * BLOCK), F32),
        ),
        in_specs=[SMEM_SPEC] + [VMEM_SPEC] * 3 + [ANY_SPEC],
        out_specs=(ANY_SPEC, VMEM_SPEC, VMEM_SPEC, VMEM_SPEC),
        scratch_shapes=[
            pltpu.VMEM((BLOCKS, BLOCK, q_cols), BF16),
            DMA((nz + 1,)), DMA((nz,)), DMA((nz, 2, fs - 1)), DMA((nz, 2, fs - 1)), DMA((nz, nc)), DMA((nz, nc)),
        ],
        input_output_aliases={4: 0},
        compiler_params=pltpu.CompilerParams(collective_id=1, has_side_effects=True, vmem_limit_bytes=VMEM_LIMIT),
        cost_estimate=pl.CostEstimate(flops=2 * 20 * BLOCK * BLOCK * heads * 3 * HEAD, bytes_accessed=30 * 2**20, transcendentals=0),
    )(block, q, k, v, w)
def reduce_order(fs, hi):
    return bit_orders(fs)[hi][::-1]


def reduce_masks(fs, hi):
    return combos(reduce_order(fs, hi)[1:][::-1])


def first_copies(hi, fs, f, view, land, ssem, rsem):
    bit = reduce_order(fs, hi)[0]
    return [remote(view(flip(flip(f, m), bit)), land(i), ssem.at[i], rsem.at[i], fsdp=flip(f, bit))
            for i, m in enumerate(reduce_masks(fs, hi))]


def later_copies(hi, stage, fs, f, held, land, ssem, rsem):
    bit = reduce_order(fs, hi)[stage]
    keep = fs >> (stage + 1)
    base = fs // 2 - (fs >> stage)
    return [remote(held(keep + i), land(base + i), ssem.at[base + i], rsem.at[base + i], fsdp=flip(f, bit)) for i in range(keep)]


def add_low(a, b):
    return (a.astype(F32) + b.astype(F32)).astype(BF16)


def early_parts(nz):
    return (nz - 1, 0) if nz > 1 else (0,)


def late_parts(nz):
    return tuple(t for t in range(nz - 2, 0, -1))


def rope_norm_back(g, pre, gain, cos, sins):
    c = g * cos + pltpu.roll(g * sins, HEAD // 2, 1)
    inv = lax.rsqrt(jnp.mean(pre * pre, axis=-1, keepdims=True) + EPS)
    n = pre * inv
    sc = c * gain
    return inv * (sc - n * jnp.mean(sc * n, axis=-1, keepdims=True)), c * n


def attend_back_kernel(dims, cut, block_ref, q_ref, k_ref, v_ref, o_ref, l_ref, do_ref, pre_hbm, cos_hbm, sin_hbm,
                       qg_ref, kg_ref, re_ref, dr_ref, g_ref, d_ref, te_ref, to_ref, tl_ref, ch_ref, qgg_ref, kgg_ref,
                       pre_ref, cos_ref, sin_ref, lp, dr, dq, dk, dv, he, ho, hl, ro, rl, rn, le, lo, ll, os, orr, fss, fsr, nss, nsr, xs, xr, hs, hr):
    fs, nc, nz = dims
    f, z = lax.axis_index("fsdp"), lax.axis_index("tp")
    heads = q_ref.shape[2] // HEAD
    early, late = early_parts(nz), late_parts(nz)[:-1]
    stages = fs.bit_length() - 1
    rest = pl.ds(cut, g_ref.shape[-1] - cut)
    barrier = pltpu.get_barrier_semaphore()
    bits = bit_orders(fs)[0]
    for bit in bits:
        pl.semaphore_signal(barrier, inc=1, device_id={"fsdp": flip(f, bit)}, device_id_type=MESH)
    for dz in range(1, nz):
        pl.semaphore_signal(barrier, inc=1, device_id={"tp": lax.rem(z + dz, nz)}, device_id_type=MESH)
    tables = [pltpu.make_async_copy(src, dst, lp.at[i]) for i, (src, dst) in enumerate(((pre_hbm, pre_ref), (cos_hbm, cos_ref), (sin_hbm, sin_ref)))]
    own = []
    for hi in range(2):
        for i, m in enumerate(reduce_masks(fs, hi)):
            for e, t in enumerate(early):
                own.append(pltpu.make_async_copy(g_ref.at[t, flip(f, m), hi, :, pl.ds(0, cut)], he.at[e, hi, i], le.at[e, hi, i]))
                own.append(pltpu.make_async_copy(g_ref.at[t, flip(f, m), hi, :, rest], ho.at[e, hi, i], lo.at[e, hi, i]))
            for j, t in enumerate(late):
                own.append(pltpu.make_async_copy(g_ref.at[t, flip(f, m), hi], hl.at[j, hi, i], ll.at[j, hi, i]))
    for cp in own + tables:
        cp.start()
    pl.semaphore_wait(barrier, len(bits) + nz - 1)

    units = dr_ref.shape[2]
    def spot(side, zz):
        return pl.ds((side * nz + zz) * units, units)
    for dz in range(1, nz):
        to = lax.rem(z + dz, nz)
        for side in range(nc):
            remote(dr_ref.at[to, side], dr.at[spot(side, z)], xs.at[dz, side], xr.at[z, side], tp=to).start()
    keep_own = [pltpu.make_async_copy(dr_ref.at[z, side], dr.at[spot(side, z)], lp.at[3 + side]) for side in range(nc)]
    for cp in keep_own:
        cp.start()

    def first_rest(e, hi):
        return first_copies(hi, fs, f, lambda g: g_ref.at[early[e], g, hi, :, rest], lambda i: ro.at[e, hi, i], os.at[e, hi], orr.at[e, hi])

    def first_late(j, hi):
        return first_copies(hi, fs, f, lambda g: g_ref.at[late[j], g, hi], lambda i: rl.at[j, hi, i], fss.at[j, hi], fsr.at[j, hi])

    def later(e, hi, stage):
        return later_copies(hi, stage, fs, f, lambda i: he.at[e, hi, i], lambda i: rn.at[e, hi, i], nss.at[e, hi], nsr.at[e, hi])
    for cp in own:
        cp.wait()
    for e in range(len(early)):
        for hi in range(2):
            he[e, hi] = add_low(he[e, hi], re_ref[e, hi])
            if stages > 1:
                for cp in later(e, hi, 1):
                    cp.start()

    def hop(e):
        return remote(te_ref.at[e], ch_ref, hs.at[e], hr.at[0], tp=jnp.minimum(z + 1, nz - 1) if e == 0 else jnp.maximum(z - 1, 0))

    def finish_early():
        for stage in range(1, stages):
            keep = fs >> (stage + 1)
            base = fs // 2 - (fs >> stage)
            for e in range(len(early)):
                for hi in range(2):
                    for cp in later(e, hi, stage):
                        cp.wait_recv()
                    he[e, hi, :keep] = add_low(he[e, hi, :keep], rn[e, hi, base:base + keep])
                    if stage + 1 < stages:
                        for cp in later(e, hi, stage + 1):
                            cp.start()
        for e in range(len(early)):
            te_ref[e] = he[e, :, 0]
        pl.when(z == 0)(hop(0).start)
        pl.when(z == nz - 1)(hop(1).start)
        for e in range(len(early)):
            for hi in range(2):
                for cp in first_rest(e, hi):
                    cp.start()
        for j in range(len(late)):
            for hi in range(2):
                for cp in first_late(j, hi):
                    cp.start()

    tri = lax.broadcasted_iota(jnp.int32, (BLOCK, BLOCK), 0) <= lax.broadcasted_iota(jnp.int32, (BLOCK, BLOCK), 1)
    dk[...] = jnp.zeros_like(dk)
    dv[...] = jnp.zeros_like(dv)
    per = BLOCK // UNIT
    for h in range(heads):
        cols, logs = slice(h * HEAD, (h + 1) * HEAD), slice(h * BLOCK, (h + 1) * BLOCK)
        if h == 1:
            for cp in keep_own:
                cp.wait()
            for dz in range(1, nz):
                src = lax.rem(z + dz, nz)
                for side in range(nc):
                    remote(dr_ref.at[0, side], dr.at[spot(side, src)], xs.at[dz, side], xr.at[src, side], tp=src).wait_recv()
        for qb in range(BLOCKS):
            if h == 0 and qb == BLOCKS - 1:
                finish_early()
            at = slot_of(block_ref, qb)
            q = q_ref[at, :, cols]
            if h == 0:
                g = do_ref[at]
            else:
                g = jnp.concatenate([dr[at * per + i, :, (h - 1) * HEAD:h * HEAD] for i in range(per)], axis=0)
            delta = jnp.sum((g.astype(F32) * o_ref[at, :, cols].astype(F32)).T, axis=0, keepdims=True)
            log = l_ref[qb, 0:1, logs]

            def pair(kb, diagonal):
                k = k_ref[slot_of(block_ref, kb)]
                v = v_ref[slot_of(block_ref, kb), :, :HEAD]
                p = jnp.exp2(dot(k, q, NT) - log)
                if diagonal:
                    p = jnp.where(tri, p, 0.0)
                ds = (p * (dot(v, g, NT) - delta)).astype(BF16)
                dv[kb] += dot(p.astype(BF16), g, NN)
                dk[kb] += dot(ds, q, NN)
                return dot(k.T, ds, NN)
            total = pair(qb, True)
            for kb in range(full_keys(qb)):
                total = total + pair(kb, False)
            dq[qb, logs] = total.T

    for cp in tables:
        cp.wait()
    qgg_ref[...] = jnp.zeros_like(qgg_ref)
    kgg_ref[...] = jnp.zeros_like(kgg_ref)

    @pl.loop(0, BLOCKS)
    def _(s):
        b = block_ref[s]
        cos, sins = rope_rows(cos_ref, block_ref, s * per, per), rope_rows(sin_ref, block_ref, s * per, per)
        qs = dq[b]
        for h in range(heads):
            back, part = rope_norm_back(qs[h * BLOCK:(h + 1) * BLOCK] * HEAD ** -0.5, pre_ref[s, :, h * HEAD:(h + 1) * HEAD].astype(F32), qg_ref[...], cos, sins)
            d_ref[s, :, h * HEAD:(h + 1) * HEAD] = back.astype(BF16)
            qgg_ref[...] += jnp.sum(part, axis=0, keepdims=True)
        back, part = rope_norm_back(dk[b] * (1.0 / LOG2E), pre_ref[s, :, heads * HEAD:].astype(F32), kg_ref[...], cos, sins)
        d_ref[s, :, heads * HEAD:(heads + 1) * HEAD] = back.astype(BF16)
        kgg_ref[...] += jnp.sum(part, axis=0, keepdims=True)
        d_ref[s, :, (heads + 1) * HEAD:] = dv[b].astype(BF16)

    for e in range(len(early)):
        for hi in range(2):
            for cp in first_rest(e, hi):
                cp.wait_recv()
            to_ref[e, hi] = add_low(ho[e, hi], ro[e, hi])
    for j in range(len(late)):
        for hi in range(2):
            for cp in first_late(j, hi):
                cp.wait_recv()
            tl_ref[j, hi] = add_low(hl[j, hi], rl[j, hi])
    pl.when((z == 1) | (z == nz - 2))(hop(0).wait_recv)
    pl.when(z == 0)(hop(0).wait_send)
    pl.when(z == nz - 1)(hop(1).wait_send)
    for dz in range(1, nz):
        for side in range(nc):
            remote(dr_ref.at[0, side], dr.at[spot(side, 0)], xs.at[dz, side], xr.at[0, side], tp=lax.rem(z + dz, nz)).wait_send()
    for hi in range(2):
        for j in range(len(late)):
            for cp in first_late(j, hi):
                cp.wait_send()
        for e in range(len(early)):
            for cp in first_rest(e, hi):
                cp.wait_send()
            for stage in range(1, stages):
                for cp in later(e, hi, stage):
                    cp.wait_send()


def attend_back_call(dims, block, q, k, v, o, l, do, pre, cos, sin, qg, kg, re, dr, g):
    fs, nc, nz = dims
    q_cols = q.shape[2]
    heads = q_cols // HEAD
    early, late = len(early_parts(nz)), len(late_parts(nz)) - 1
    shard, cols = g.shape[3:]
    cut = re.shape[4]
    half, more = fs // 2, max(fs // 2 - 1, 1)
    DMA = pltpu.SemaphoreType.DMA
    V = pltpu.VMEM
    return pl.pallas_call(
        lambda *refs: attend_back_kernel(dims, cut, *refs),
        out_shape=(
            jax.ShapeDtypeStruct((BLOCKS, BLOCK, q_cols + 2 * HEAD), BF16),
            jax.ShapeDtypeStruct((early, 2, shard, cut), BF16),
            jax.ShapeDtypeStruct((early, 2, half, shard, cols - cut), BF16),
            jax.ShapeDtypeStruct((late, 2, half, shard, cols), BF16),
            jax.ShapeDtypeStruct((2, shard, cut), BF16),
            jax.ShapeDtypeStruct((1, HEAD), F32),
            jax.ShapeDtypeStruct((1, HEAD), F32),
        ),
        in_specs=[SMEM_SPEC] + [VMEM_SPEC] * 6 + [ANY_SPEC] * 3 + [VMEM_SPEC] * 3 + [ANY_SPEC] * 2,
        out_specs=(VMEM_SPEC,) * 7,
        scratch_shapes=[
            V(pre.shape, BF16), V(cos.shape, F32), V(sin.shape, F32), DMA((3 + nc,)),
            V((BLOCKS * BLOCK // UNIT, UNIT, q_cols - HEAD), BF16),
            V((BLOCKS, heads * BLOCK, HEAD), F32), V((BLOCKS, BLOCK, HEAD), F32), V((BLOCKS, BLOCK, HEAD), F32),
            V((early, 2, half, shard, cut), BF16), V((early, 2, half, shard, cols - cut), BF16), V((late, 2, half, shard, cols), BF16),
            V((early, 2, half, shard, cols - cut), BF16), V((late, 2, half, shard, cols), BF16), V((early, 2, more, shard, cut), BF16),
            DMA((early, 2, half)), DMA((early, 2, half)), DMA((late, 2, half)),
            DMA((early, 2, half)), DMA((early, 2, half)), DMA((late, 2, half)), DMA((late, 2, half)),
            DMA((early, 2, more)), DMA((early, 2, more)), DMA((nz, nc)), DMA((nz, nc)), DMA((2,)), DMA((1,)),
        ],
        compiler_params=pltpu.CompilerParams(collective_id=3, has_side_effects=True, vmem_limit_bytes=VMEM_LIMIT),
        cost_estimate=pl.CostEstimate(flops=2 * 20 * BLOCK * BLOCK * heads * 5 * HEAD, bytes_accessed=40 * 2**20, transcendentals=0),
    )(block, q, k, v, o, l, do, pre, cos, sin, qg, kg, re, dr, g)
def column_parts(dims, hidden, q_cols):
    return (0, hidden, 2 * hidden, 3 * hidden, 3 * hidden + q_cols)


def feed_kernel(dims, x_ref, dy_ref, o_ref, w_ref, gain_ref, out_ref, dh_ref, fg_ref, do_ref, dr_ref, g_ref, re_ref,
                wb, ge, hs, b_ref, da_ref, dgu, u_ref, acc, snd, rcv, dos, bt, yt, at,
                ls, gs, ss, sr, xs, xr, fss, fsr, os, orr, ps, pr):
    fs, nc, nz = dims
    f, c, z = lax.axis_index("fsdp"), lax.axis_index("ctx"), lax.axis_index("tp")
    o = 1 - c
    rows, width = x_ref.shape
    q_cols = o_ref.shape[3]
    hidden = (w_ref.shape[2] - q_cols) // 3
    gate, up_, down_, out_, end = column_parts(dims, hidden, q_cols)
    edge = (z == 0) | (z == nz - 1)
    last = jnp.where(z == 0, nz - 1, 0)
    keep = down_

    def load_out(zz):
        part = pl.ds(out_, end - out_)
        return pltpu.make_async_copy(w_ref.at[zz, :, part], wb.at[zz, :, part], ls.at[0, zz])

    def loads(act):
        for zz in range(nz):
            here = edge & (last == zz)
            for late in range(2):
                part = pl.ds(keep if late else 0, out_ - (keep if late else 0))

                @pl.when(here if late else jnp.logical_not(here))
                def _():
                    act(pltpu.make_async_copy(w_ref.at[zz, :, part], wb.at[zz, :, part], ls.at[1, zz]))
    for zz in range(nz):
        load_out(zz).start()
    loads(lambda cp: cp.start())
    barrier = pltpu.get_barrier_semaphore()
    pl.semaphore_signal(barrier, inc=1, device_id={"ctx": o}, device_id_type=MESH)
    for dz in range(1, nz):
        pl.semaphore_signal(barrier, inc=1, device_id={"tp": lax.rem(z + dz, nz)}, device_id_type=MESH)
    bits = bit_orders(fs)[0]
    stages = len(bits)
    for bit in bits:
        pl.semaphore_signal(barrier, inc=1, device_id={"fsdp": flip(f, bit)}, device_id_type=MESH)
    pl.semaphore_wait(barrier, nz + len(bits))
    early = early_parts(nz)
    shard = width // (fs * nc)

    def shard_rows(g, hi, n=1):
        return pl.ds(pl.multiple_of((g * nc + hi) * shard, shard), n * shard)

    def chunk(k):
        return pl.ds(k * (keep // 2), keep // 2)

    def outward(way, k):
        part = 0 if way == 0 else nz - 1
        to = jnp.minimum(z + 1, nz - 1) if way == 0 else jnp.maximum(z - 1, 0)
        ref = shard_rows(f, 0, nc)
        return remote(w_ref.at[part, ref, chunk(k)], wb.at[part, ref, chunk(k)], os.at[way, k], orr.at[k], tp=to)

    def out_copies(act):
        for k in range(2):
            pl.when(z == nz - 2)(lambda: act(outward(0, k)))
            pl.when(z == 1)(lambda: act(outward(1, k)))
    out_copies(lambda cp: cp.start())

    def late_plane(hi, stage, k):
        return plane_copies(hi, stage, fs, f, lambda g: wb.at[last, shard_rows(g, hi), chunk(k)], ps.at[hi, k], pr.at[hi, k])

    def late_arrive(k):
        @pl.when(edge)
        def _():
            ref = shard_rows(f, 0, nc)
            remote(w_ref.at[0, ref, chunk(k)], wb.at[last, ref, chunk(k)], os.at[0, k], orr.at[k], ctx=o).wait_recv()
            for hi in range(2):
                for cp in late_plane(hi, 0, k):
                    cp.start()

    def late_spread(stage, k):
        @pl.when(edge)
        def _():
            for hi in range(2):
                for cp in late_plane(hi, stage, k):
                    cp.wait_recv()
                if stage + 1 < stages:
                    for cp in late_plane(hi, stage + 1, k):
                        cp.start()

    def first(e, hi):
        def view(g):
            return ge.at[e, shard_rows(g, hi)]
        return first_copies(hi, fs, f, view, lambda i: re_ref.at[e, hi, i], fss.at[e, hi], fsr.at[e, hi])

    def cross(i, src, dst):
        return remote(src, dst, ss.at[i], sr.at[i], ctx=o)
    for zz in range(nz):
        load_out(zz).wait()

    def project(side):
        total = dot(o_ref[0, side], wb[0, :, out_:end], NT)
        for zz in range(1, nz):
            total += dot(o_ref[zz, side], wb[zz, :, out_:end], NT)
        return total
    snd[0] = project(o).astype(BF16)
    cross(0, snd.at[0], rcv.at[0]).start()
    own = project(c)
    loads(lambda cp: cp.wait())

    @pl.loop(0, nz)
    def _(zz):
        dgu[zz, :, :hidden] = dot(dy_ref[...].reshape(nc * rows, width), wb[zz, :, down_:out_], NN).astype(BF16)
    late_arrive(0)
    cross(0, snd.at[0], rcv.at[0]).wait_recv()
    h = x_ref[...].astype(F32) + own + rcv[0].astype(F32)
    hs[...] = h
    b_ref[c] = (h * lax.rsqrt(jnp.mean(h * h, axis=-1, keepdims=True) + EPS) * gain_ref[...]).astype(BF16)
    cross(1, b_ref.at[c], b_ref.at[c]).start()
    yt[...] = dy_ref[...].reshape(nc * rows, width).T
    late_spread(0, 0)
    late_arrive(1)
    cross(1, b_ref.at[c], b_ref.at[o]).wait_recv()

    @pl.loop(0, nz)
    def _(i):
        zz = jnp.where(z == nz - 1, nz - 1 - i, i)

        @pl.when(i == 1)
        def _():
            late_spread(0, 1)

        @pl.when(i == nz - 1)
        def _():
            for stage in range(1, stages):
                for k in range(2):
                    late_spread(stage, k)
        both = b_ref[...].reshape(nc * rows, width)
        gu = dot(both, wb[zz, :, gate:down_], NN)
        du = dgu[zz, :, :hidden].astype(F32)
        gt, uv = gu[:, :hidden], gu[:, hidden:]
        sig = 1.0 / (1.0 + jnp.exp(-gt))
        silu = gt * sig
        hid = (silu * uv).astype(BF16)
        u_ref[zz] = hid
        dgu[zz, :, :hidden] = (du * uv * sig * (1.0 + gt * (1.0 - sig))).astype(BF16)
        dgu[zz, :, hidden:] = (du * silu).astype(BF16)

    def side_rows(side):
        return pl.ds(pl.multiple_of(side * rows, 128), rows)

    def feed_sum(side, left, start, stop):
        total = dot(left[0, side_rows(side)], wb[0, :, start:stop], NT)
        for zz in range(1, nz):
            total += dot(left[zz, side_rows(side)], wb[zz, :, start:stop], NT)
        return total
    snd[1] = feed_sum(o, dgu, gate, down_).astype(BF16)
    cross(2, snd.at[1], rcv.at[1]).start()
    acc[...] = feed_sum(c, dgu, gate, down_)
    bt[...] = b_ref[...].reshape(nc * rows, width).T

    def feed_grads(zz, into):
        into[:, gate:down_] = dot(bt[...], dgu[zz], NN).astype(BF16)
        into[:, down_:out_] = dot(yt[...], u_ref[zz], NN).astype(BF16)

    def early_grads(e):
        feed_grads(early[e], ge.at[e])
        for hi in range(2):
            for cp in first(e, hi):
                cp.start()
    early_grads(0)
    cross(2, snd.at[1], rcv.at[1]).wait_recv()
    db = acc[...] + rcv[1].astype(F32)
    h = hs[...]
    inv = lax.rsqrt(jnp.mean(h * h, axis=-1, keepdims=True) + EPS)
    n = h * inv
    sc = db * gain_ref[...]
    dh = dy_ref[c].astype(F32) + inv * (sc - n * jnp.mean(sc * n, axis=-1, keepdims=True))
    fg_ref[...] = jnp.sum(db * n, axis=0, keepdims=True)
    dh_ref[...] = dh
    da_ref[c] = dh.astype(BF16)
    cross(4, da_ref.at[c], da_ref.at[c]).start()
    for e in range(1, len(early)):
        early_grads(e)
    snd[2] = feed_sum(o, u_ref, down_, out_).astype(BF16)
    cross(3, snd.at[2], rcv.at[2]).start()
    acc[...] = feed_sum(c, u_ref, down_, out_)
    cross(4, da_ref.at[c], da_ref.at[o]).wait_recv()

    def stores(zz):
        if zz not in early:
            return [pltpu.make_async_copy(wb.at[zz], g_ref.at[zz], gs.at[0, zz])]
        lead, tail = pl.ds(0, out_), pl.ds(out_, end - out_)
        return [pltpu.make_async_copy(ge.at[early.index(zz)], g_ref.at[zz, :, lead], gs.at[0, zz]),
                pltpu.make_async_copy(wb.at[zz, :, tail], g_ref.at[zz, :, tail], gs.at[1, zz])]

    @pl.loop(1, nz + 1)
    def _(dz):
        to = lax.rem(z + dz, nz)
        both = dot(da_ref[...].reshape(nc * rows, width), wb[to, :, out_:end], NN).astype(BF16).reshape(nc, rows, q_cols)
        dos[to] = both[:, :, :HEAD]
        dr_ref[to] = both[:, :, HEAD:]

        @pl.when(dz < nz)
        def _():
            for side in range(nc):
                remote(dos.at[to, side], do_ref.at[side, z], xs.at[dz, side], xr.at[z, side], tp=to).start()
    for side in range(nc):
        do_ref[side, z] = dos[z, side]
    cross(3, snd.at[2], rcv.at[2]).wait_recv()
    out_ref[...] = (hs[...] + acc[...] + rcv[2].astype(F32)).astype(BF16)
    at[...] = da_ref[...].reshape(nc * rows, width).T
    for zz in early + late_parts(nz):
        wb[zz, :, out_:end] = dot(at[...], o_ref[zz].reshape(nc * rows, q_cols), NN).astype(BF16)
        if zz not in early:
            feed_grads(zz, wb.at[zz])
        for cp in stores(zz):
            cp.start()
    for zz in range(nz):
        for cp in stores(zz):
            cp.wait()

    @pl.when(edge)
    def _():
        for hi in range(2):
            for stage in range(stages):
                for k in range(2):
                    for cp in late_plane(hi, stage, k):
                        cp.wait_send()
    for dz in range(1, nz):
        src = lax.rem(z + dz, nz)
        for side in range(nc):
            cp = remote(dos.at[0, side], do_ref.at[side, src], xs.at[dz, side], xr.at[src, side], tp=src)
            cp.wait_recv()
            cp.wait_send()
    out_copies(lambda cp: cp.wait_send())
    for e in range(len(early)):
        for hi in range(2):
            for cp in first(e, hi):
                cp.wait_recv()
                cp.wait_send()
    for i, part in enumerate((snd.at[0], b_ref.at[c], snd.at[1], snd.at[2], da_ref.at[c])):
        cross(i, part, part).wait_send()


def feed_call(dims, x, dyp, o, w, gain):
    fs, nc, nz = dims
    rows, width = x.shape
    q_cols = o.shape[3]
    cols = w.shape[2]
    hidden = (cols - q_cols) // 3
    early = len(early_parts(nz))
    DMA = pltpu.SemaphoreType.DMA
    V = pltpu.VMEM
    return pl.pallas_call(
        lambda *refs: feed_kernel(dims, *refs),
        out_shape=(
            jax.ShapeDtypeStruct((rows, width), BF16),
            jax.ShapeDtypeStruct((rows, width), F32),
            jax.ShapeDtypeStruct((1, width), F32),
            jax.ShapeDtypeStruct((nc, nz, rows, HEAD), BF16),
            jax.ShapeDtypeStruct((nz, nc, rows, q_cols - HEAD), BF16),
            jax.ShapeDtypeStruct(w.shape, BF16),
            jax.ShapeDtypeStruct((early, 2, fs // 2, width // (fs * nc), 3 * hidden), BF16),
        ),
        in_specs=[VMEM_SPEC] * 3 + [ANY_SPEC, VMEM_SPEC],
        out_specs=(VMEM_SPEC,) * 5 + (ANY_SPEC, ANY_SPEC),
        scratch_shapes=[
            V(w.shape, BF16), V((early, width, 3 * hidden), BF16), V((rows, width), F32), V((nc, rows, width), BF16), V((nc, rows, width), BF16),
            V((nz, nc * rows, 2 * hidden), BF16), V((nz, nc * rows, hidden), BF16),
            V((rows, width), F32),
            V((3, rows, width), BF16), V((3, rows, width), BF16), V((nz, nc, rows, HEAD), BF16),
            V((width, nc * rows), BF16), V((width, nc * rows), BF16), V((width, nc * rows), BF16),
            DMA((2, nz)), DMA((2, nz)), DMA((5,)), DMA((5,)), DMA((nz, nc)), DMA((nz, nc)),
            DMA((early, 2, fs // 2)), DMA((early, 2, fs // 2)),
            DMA((2, 2)), DMA((2,)), DMA((2, 2, fs - 1)), DMA((2, 2, fs - 1)),
        ],
        compiler_params=pltpu.CompilerParams(collective_id=2, has_side_effects=True, vmem_limit_bytes=VMEM_LIMIT),
        cost_estimate=pl.CostEstimate(flops=2 * 13 * 2**30, bytes_accessed=40 * 2**20, transcendentals=0),
    )(x, dyp, o, w, gain)
def line_events(nz):
    out = []
    for z in range(nz):
        events = [(z + nz - 1 - t, 0, t) for t in range(z + 1, nz)] + [(nz - 1 - z + t, 1, t) for t in range(z)]
        out.append([(way, t) for _, way, t in sorted(events)])
    return out


def at_place(z, rows):
    return pick(z, rows)


def finish_kernel(dims, cut, d_ref, wall_ref, a_hbm, x_hbm, dh_hbm, gain_ref, te_hbm, to_hbm, tl_hbm, ch_hbm, fg_ref, qgg_ref, kgg_ref, g_ref,
                  ig_ref, dwq_ref, dwz_ref, gains_ref,
                  a_ref, x_ref, dh_ref, te_ref, to_ref, tl_ref, ch_ref, pa, sib, ru, snd, rq, wq, rw, tw, hx, rx, rno, rn, fin, share, sc_, gx, gy,
                  la, lx, xs, xr, os, orr, bs, br, us, ur, qs, qr, vs, vr, ns, nr, cs, cr, hs, hr):
    fs, nc, nz = dims
    f, c, z = lax.axis_index("fsdp"), lax.axis_index("ctx"), lax.axis_index("tp")
    o = 1 - c
    me = f * nc + c
    rows, width = ig_ref.shape
    shard = dwq_ref.shape[1]
    early, late, final = early_parts(nz), late_parts(nz)[:-1], late_parts(nz)[-1]
    stages = fs.bit_length() - 1
    rest = pl.ds(cut, tw.shape[-1] - cut)
    others = [(df, dc) for df in range(fs) for dc in range(nc) if (df, dc) != (0, 0)]
    barrier = pltpu.get_barrier_semaphore()
    for df, dc in others:
        pl.semaphore_signal(barrier, inc=1, device_id={"fsdp": lax.rem(f + df, fs), "ctx": lax.rem(c + dc, nc)}, device_id_type=MESH)
    for dz in range(1, nz):
        pl.semaphore_signal(barrier, inc=1, device_id={"tp": lax.rem(z + dz, nz)}, device_id_type=MESH)
    pairs = ((to_hbm, to_ref), (tl_hbm, tl_ref), (te_hbm, te_ref), (ch_hbm, ch_ref), (x_hbm, x_ref), (dh_hbm, dh_ref), (a_hbm, a_ref))
    fills = [pltpu.make_async_copy(src, dst, la.at[i]) for i, (src, dst) in enumerate(pairs)]
    for cp in fills:
        cp.start()
    own = []
    for hi in range(2):
        for i, m in enumerate(reduce_masks(fs, hi)):
            own.append(pltpu.make_async_copy(g_ref.at[final, flip(f, m), hi], hx.at[hi, i], lx.at[hi, i]))
    for cp in own:
        cp.start()
    pl.semaphore_wait(barrier, len(others) + nz - 1)

    def last(hi):
        return first_copies(hi, fs, f, lambda g: g_ref.at[final, g, hi], lambda i: rx.at[hi, i], xs.at[hi], xr.at[hi])

    def later_rest(e, hi, stage):
        return later_copies(hi, stage, fs, f, lambda i: to_ref.at[e, hi, i], lambda i: rno.at[e, hi, i], os.at[e, hi], orr.at[e, hi])

    def later(j, hi, stage):
        held = (lambda i: tl_ref.at[j, hi, i]) if j < len(late) else (lambda i: hx.at[hi, i])
        return later_copies(hi, stage, fs, f, held, lambda i: rn.at[j, hi, i], ns.at[j, hi], nr.at[j, hi])

    def begin(copies):
        for cp in copies:
            cp.start()
    def reduce_last():
        for cp in own:
            cp.wait()
        for hi in range(2):
            for cp in last(hi):
                cp.wait_recv()
            hx[hi] = add_low(hx[hi], rx[hi])
            if stages > 1:
                begin(later(len(late), hi, 1))

    def reduce_more(copies, held, got, done):
        for stage in range(1, stages):
            keep = fs >> (stage + 1)
            base = fs // 2 - (fs >> stage)
            for cp in copies(stage):
                cp.wait_recv()
            if stage + 1 == stages:
                done(add_low(held[0], got[base]))
            else:
                held[:keep] = add_low(held[:keep], got[base:base + keep])
                begin(copies(stage + 1))
        if stages == 1:
            done(held[0])

    def put(t, hi, where):
        def done(value):
            tw[t, hi, :, where] = value
        return done

    def reduce_rest():
        for hi in range(2):
            for e in range(len(early)):
                reduce_more(lambda stage: later_rest(e, hi, stage), to_ref.at[e, hi], rno.at[e, hi], put(early[e], hi, rest))
            for j, t in enumerate(late + (final,)):
                held = tl_ref.at[j, hi] if j < len(late) else hx.at[hi]
                reduce_more(lambda stage: later(j, hi, stage), held, rn.at[j, hi], put(t, hi, slice(None)))

    def cross(t):
        return remote(snd.at[t], sib.at[t], bs.at[t], br.at[t], ctx=o)
    events = line_events(nz)

    def event(i):
        way = at_place(z, [events[zz][i][0] for zz in range(nz)])
        t = at_place(z, [events[zz][i][1] for zz in range(nz)])
        arrives = jnp.where(way == 0, z > 0, z < nz - 1)
        to = jnp.where(way == 0, jnp.minimum(z + 1, nz - 1), jnp.maximum(z - 1, 0))
        slot = jnp.where((way == 1) & (t == to), nz, t)
        return t, arrives, to, slot

    def rows_copy(i):
        t, _, to, slot = event(i)
        return remote(snd.at[t], ru.at[slot], us.at[i], ur.at[slot], tp=to)

    def rows_event(i):
        t, arrives, _, _ = event(i)
        cross(t).wait()

        @pl.when(arrives)
        def _():
            remote(snd.at[t], ru.at[t], us.at[i], ur.at[t], ctx=o).wait_recv()
            snd[t] = (pa[t] + sib[t].astype(F32) + ru[t].astype(F32)).astype(BF16)

        @pl.when(jnp.logical_not(arrives))
        def _():
            snd[t] = (pa[t] + sib[t].astype(F32)).astype(BF16)
        rows_copy(i).start()

    def weights(r):
        return pl.ds(pl.multiple_of(r * shard, shard), shard)

    def project(t):
        snd[t] = dot(d_ref[o * nz + t], wall_ref[...], NT).astype(BF16)
        cross(t).start()
        pa[t] = dot(d_ref[c * nz + t], wall_ref[...], NT)

    @pl.loop(0, nz)
    def _(i):
        t = z
        for k in range(nz - 1):
            t = jnp.where(i == k, event(k)[0], t)
        project(t)

        @pl.when(i == 0)
        def _():
            for cp in fills[:2]:
                cp.wait()
            for hi in range(2):
                begin(last(hi))
                if stages > 1:
                    for e in range(len(early)):
                        begin(later_rest(e, hi, 1))
                    for j in range(len(late)):
                        begin(later(j, hi, 1))

        @pl.when(i == min(2, nz - 1))
        def _():
            rows_event(0)
    for cp in fills[2:]:
        cp.wait()
    wq[...] = jnp.zeros_like(wq)

    @pl.loop(0, nc * nz)
    def _(s):
        wq[...] += dot(a_ref[s], d_ref[s], TN)
    rq[me] = wq[weights(me)].astype(BF16)
    for i, (df, dc) in enumerate(others):
        tf, tc = lax.rem(f + df, fs), lax.rem(c + dc, nc)
        sc_[i] = wq[weights(tf * nc + tc)].astype(BF16)
        remote(sc_.at[i], rq.at[me], qs.at[i], qr.at[me], fsdp=tf, ctx=tc).start()
    for e in range(len(early)):
        tw[early[e], :, :, :cut] = te_ref[e]

    @pl.when(z == 1)
    def _():
        rw[nz - 1, :, :, :cut] = ch_ref[...]

    @pl.when(z == nz - 2)
    def _():
        rw[0, :, :, :cut] = ch_ref[...]
    reduce_last()
    for i in range(1, nz - 1):
        rows_event(i)

    reduce_rest()
    firsts = ((z == 0), (z == nz - 1))

    def grads_copy(i, part=None):
        t, _, to, slot = event(i)
        src, dst = (tw.at[t], rw.at[slot]) if part is None else (tw.at[t, :, :, part], rw.at[slot, :, :, part])
        return remote(src, dst, vs.at[i], vr.at[slot], tp=to)

    def grads_came(i, t, part=None):
        src, dst = (tw.at[t], rw.at[t]) if part is None else (tw.at[t, :, :, part], rw.at[t, :, :, part])
        remote(src, dst, vs.at[i], vr.at[t], ctx=o).wait_recv()

    def leads(i):
        t = event(i)[0]
        return ((z == 0) & (t == nz - 1)) | ((z == nz - 1) & (t == 0))

    def follows(i):
        t = event(i)[0]
        return ((z == 1) & (t == nz - 1)) | ((z == nz - 2) & (t == 0))

    def grads_event(i):
        t, arrives, _, _ = event(i)

        @pl.when(arrives)
        def _():
            pl.when(follows(i))(lambda: grads_came(i, t, rest))
            pl.when(jnp.logical_not(follows(i)))(lambda: grads_came(i, t))
            tw[t] = add_low(tw[t], rw[t])
        pl.when(leads(i))(lambda: grads_copy(i, rest).start())
        pl.when(jnp.logical_not(leads(i)))(lambda: grads_copy(i).start())
    grads_event(0)

    def rows_arrival(way):
        slot = nz if way else z
        return remote(snd.at[0], ru.at[slot], us.at[0], ur.at[slot], ctx=o)

    cross(z).wait()
    pa[z] += sib[z].astype(F32)

    @pl.when(z > 0)
    def _():
        rows_arrival(0).wait_recv()
        pa[z] += ru[z].astype(F32)

    @pl.when(z < nz - 1)
    def _():
        rows_arrival(1).wait_recv()
        pa[z] += ru[nz].astype(F32)
    da = pa[z]
    x = x_ref[...].astype(F32)
    inv = lax.rsqrt(jnp.mean(x * x, axis=-1, keepdims=True) + EPS)
    n = x * inv
    sc = da * gain_ref[...]
    ig_ref[...] = dh_ref[...] + inv * (sc - n * jnp.mean(sc * n, axis=-1, keepdims=True))
    gx[z, 0:1] = jnp.sum(da * n, axis=0, keepdims=True)
    gx[z, 1:2] = fg_ref[...]
    gx[z, 2:3] = jnp.concatenate([qgg_ref[...], kgg_ref[...]] + [jnp.zeros((1, width - 2 * HEAD), F32)], axis=1)
    gx[z, 3:] = jnp.zeros_like(gx[z, 3:])
    for dz in range(1, nz):
        to = lax.rem(z + dz, nz)
        remote(gx.at[z], gx.at[z], hs.at[dz - 1], hr.at[z], tp=to).start()
    for i in range(1, nz - 1):
        grads_event(i)

    for i, (df, dc) in enumerate(others):
        src = lax.rem(f + df, fs) * nc + lax.rem(c + dc, nc)
        remote(sc_.at[0], rq.at[src], qs.at[i], qr.at[src], ctx=o).wait_recv()
    for cc in range(nc):
        total = rq[cc].astype(F32)
        for ff in range(1, fs):
            total += rq[ff * nc + cc].astype(F32)
        dwq_ref[cc] = total

    def grads_arrival(way):
        slot = nz if way else z
        return remote(tw.at[0], rw.at[slot], vs.at[0], vr.at[slot], ctx=o)

    for dz in range(1, nz):
        src = lax.rem(z + dz, nz)
        remote(gx.at[src], gx.at[src], hs.at[dz - 1], hr.at[src], tp=src).wait_recv()
    total = gx[0]
    for zz in range(1, nz):
        total += gx[zz]
    gy[me] = total
    for i, (df, dc) in enumerate(others):
        remote(gy.at[me], gy.at[me], hs.at[nz - 1 + i], hr.at[nz + me], fsdp=lax.rem(f + df, fs), ctx=lax.rem(c + dc, nc)).start()

    fin[...] = tw[z].astype(F32)

    @pl.when(z > 0)
    def _():
        grads_arrival(0).wait_recv()
        fin[...] += rw[z].astype(F32)

    @pl.when(z < nz - 1)
    def _():
        grads_arrival(1).wait_recv()
        fin[...] += rw[nz].astype(F32)
    share[0] = fin[o].astype(BF16)
    swap = remote(share.at[0], share.at[1], cs.at[0], cr.at[0], ctx=o)
    swap.start()
    dwz_ref[c] = fin[c]

    for i, (df, dc) in enumerate(others):
        src = lax.rem(f + df, fs) * nc + lax.rem(c + dc, nc)
        remote(gy.at[src], gy.at[src], hs.at[nz - 1 + i], hr.at[nz + src], ctx=o).wait_recv()
    total = gy[0]
    for r in range(1, fs * nc):
        total += gy[r]
    gains_ref[...] = total
    swap.wait_recv()
    dwz_ref[o] = share[1].astype(F32)

    swap.wait_send()
    for i in range(nz - 1):
        rows_copy(i).wait_send()
        pl.when(leads(i))(lambda: grads_copy(i, rest).wait_send())
        pl.when(jnp.logical_not(leads(i)))(lambda: grads_copy(i).wait_send())
    for i in range(nz - 1):
        remote(gx.at[0], gx.at[0], hs.at[i], hr.at[0], ctx=o).wait_send()
    for i in range(len(others)):
        remote(sc_.at[0], rq.at[0], qs.at[i], qr.at[0], ctx=o).wait_send()
        remote(gy.at[0], gy.at[0], hs.at[nz - 1 + i], hr.at[nz], ctx=o).wait_send()
    for hi in range(2):
        for cp in last(hi):
            cp.wait_send()
        for stage in range(1, stages):
            for e in range(len(early)):
                for cp in later_rest(e, hi, stage):
                    cp.wait_send()
            for j in range(len(late) + 1):
                for cp in later(j, hi, stage):
                    cp.wait_send()


def finish_call(dims, d, wall, a, x, dh, gain, te, to, tl, ch, fg, qgg, kgg, g):
    fs, nc, nz = dims
    rows, width = x.shape
    shard, cols = g.shape[3:]
    cut = te.shape[3]
    early = te.shape[0]
    half, more = fs // 2, max(fs // 2 - 1, 1)
    proj = wall.shape[1]
    late = len(late_parts(nz))
    n = fs * nc
    DMA = pltpu.SemaphoreType.DMA
    V = pltpu.VMEM
    return pl.pallas_call(
        lambda *refs: finish_kernel(dims, cut, *refs),
        out_shape=(
            jax.ShapeDtypeStruct((rows, width), F32),
            jax.ShapeDtypeStruct((nc, width // n, proj), F32),
            jax.ShapeDtypeStruct((nc, shard, cols), F32),
            jax.ShapeDtypeStruct((8, width), F32),
        ),
        in_specs=[VMEM_SPEC] * 2 + [ANY_SPEC] * 3 + [VMEM_SPEC] + [ANY_SPEC] * 4 + [VMEM_SPEC] * 3 + [ANY_SPEC],
        out_specs=(VMEM_SPEC,) * 4,
        scratch_shapes=[
            V(a.shape, BF16), V(x.shape, BF16), V(dh.shape, F32), V(te.shape, BF16), V(to.shape, BF16), V(tl.shape, BF16), V(ch.shape, BF16),
            V((nz, rows, width), F32), V((nz, rows, width), BF16), V((nz + 1, rows, width), BF16),
            V((nz, rows, width), BF16),
            V((n, width // n, proj), BF16), V((width, proj), F32),
            V((nz + 1, 2, shard, cols), BF16), V((nz, 2, shard, cols), BF16),
            V((2, half, shard, cols), BF16), V((2, half, shard, cols), BF16),
            V((early, 2, more, shard, cols - cut), BF16), V((late, 2, more, shard, cols), BF16),
            V((2, shard, cols), F32), V((2, shard, cols), BF16),
            V((n - 1, width // n, proj), BF16), V((nz, 8, width), F32), V((n, 8, width), F32),
            DMA((7,)), DMA((2, half)), DMA((2, half)), DMA((2, half)), DMA((early, 2, more)), DMA((early, 2, more)),
            DMA((nz,)), DMA((nz,)), DMA((nz - 1,)), DMA((nz + 1,)),
            DMA((n - 1,)), DMA((n,)), DMA((nz - 1,)), DMA((nz + 1,)),
            DMA((late, 2, max(fs // 2 - 1, 1))), DMA((late, 2, max(fs // 2 - 1, 1))),
            DMA((1,)), DMA((1,)), DMA((nz - 1 + n - 1,)), DMA((nz + n,)),
        ],
        compiler_params=pltpu.CompilerParams(collective_id=4, has_side_effects=True, vmem_limit_bytes=VMEM_LIMIT),
        cost_estimate=pl.CostEstimate(flops=2 * 4 * 2**30, bytes_accessed=40 * 2**20, transcendentals=0),
    )(d, wall, a, x, dh, gain, te, to, tl, ch, fg, qgg, kgg, g)
def unpack_kernel(parts, result_ref, ig_ref, gains_ref, dwq_ref, dwz_ref, *outs):
    outs[0][...] = result_ref[...]
    outs[1][...] = ig_ref[...]
    outs[2][...] = gains_ref[0:1]
    outs[3][...] = gains_ref[1:2]
    outs[4][...] = gains_ref[2:3, :HEAD]
    outs[5][...] = gains_ref[2:3, HEAD:2 * HEAD]
    for (which, at, step, turned), out in zip(parts, outs[6:]):
        ref = (dwq_ref, dwz_ref)[which]
        value = jnp.concatenate([ref[cc, :, at:at + step] for cc in range(ref.shape[0])], axis=1)
        out[...] = value.T if turned else value


def unpack_call(result, ig, gains, dwq, dwz, hidden, q_cols):
    nc, shard, _ = dwq.shape
    parts = ((0, 0, q_cols, False), (0, q_cols, HEAD, False), (0, q_cols + HEAD, HEAD, False),
             (1, 3 * hidden, q_cols, True), (1, 0, hidden, False), (1, hidden, hidden, False), (1, 2 * hidden, hidden, True))
    width = gains.shape[1]
    shapes = [(shard, nc * step)[::-1] if turned else (shard, nc * step) for _, _, step, turned in parts]
    return pl.pallas_call(
        lambda *refs: unpack_kernel(parts, *refs),
        out_shape=[jax.ShapeDtypeStruct(result.shape, BF16), jax.ShapeDtypeStruct(ig.shape, F32)]
        + [jax.ShapeDtypeStruct((1, n), F32) for n in (width, width, HEAD, HEAD)]
        + [jax.ShapeDtypeStruct(shape, F32) for shape in shapes],
        in_specs=[VMEM_SPEC] * 5,
        out_specs=[VMEM_SPEC] * 13,
        compiler_params=pltpu.CompilerParams(vmem_limit_bytes=VMEM_LIMIT),
    )(result, ig, gains, dwq, dwz)


def on_device(dims, tokens, out_grad, block_slot, attn_gain, ffn_gain, query_gain, key_norm_gain,
              w_query, key_weight, value_weight, w_out, w_gate, w_up, w_down):
    fs, nc, nz = dims
    rows, width = tokens.shape
    shard = w_query.shape[0]
    block_ids = block_slot[0]
    cos, sins = rope_tables()
    hidden, q_cols = w_gate.shape[1] // nc, w_query.shape[1] // nc
    ag, fg = attn_gain[None], ffn_gain[None]
    qg, kg = query_gain[None], key_norm_gain[None]
    weights = (w_query, key_weight, value_weight, w_gate, w_up, w_down, w_out)
    a, q, k, v, pre, wall, w, dyp = gather_call(dims, block_ids, tokens, out_grad, ag, weights, cos, sins, qg, kg)
    blocks = lambda t: t.reshape(BLOCKS, BLOCK, -1)
    q, k, v, pre = blocks(q), blocks(k), blocks(v), blocks(pre)
    w, mixed, o, logs = attend_call(dims, 2 * hidden, block_ids, q, k, v, w, rows)
    cols = w.shape[4]
    result, dh, ffn_part, do, dr, g, re = feed_call(dims, tokens, dyp, mixed, w.reshape(nz, width, cols), fg)
    g = g.reshape(nz, fs, nc, shard, cols)
    dr = dr.reshape(nz, nc, rows // UNIT, UNIT, q_cols - HEAD)
    d, te, to, tl, ch, q_part, k_part = attend_back_call(
        dims, block_ids, q, k, v, blocks(o), logs, blocks(do), pre, cos, sins, qg, kg, re, dr, g)
    input_grad, dwq, dwz, gains = finish_call(
        dims, d.reshape(nc * nz, rows, -1), wall.reshape(width, -1), a, tokens, dh, ag, te, to, tl, ch, ffn_part, q_part, k_part, g)
    outs = unpack_call(result, input_grad, gains, dwq, dwz, hidden, q_cols)
    return tuple(t[0] if 2 <= i < 6 else t for i, t in enumerate(outs))


def solution(mesh):
    dims = (mesh.shape["fsdp"], mesh.shape["ctx"], mesh.shape["tp"])
    everything, weights = ("fsdp", "ctx", "tp"), ("fsdp", "ctx")
    split, turned = P(weights, "tp"), P("tp", weights)
    return jax.shard_map(
        lambda *args: on_device(dims, *args),
        mesh=mesh,
        in_specs=(P(everything, None), P(everything, None), P("fsdp", None), P(), P(), P(), P(), split, split, split, turned, split, split, turned),
        out_specs=(P(everything, None), P(everything, None), P(), P(), P(), P(), split, split, split, turned, split, split, turned),
        check_vma=False,
    )
```

```python
import numpy as np
import jax
import jax.numpy as jnp
from jax import lax
from jax.experimental import pallas as pl
from jax.experimental.pallas import tpu as pltpu
from jax.sharding import PartitionSpec as P

HEAD = 128
BLOCK = 512
PBLOCKS = 4
BLOCKS = 6
EPS = 1e-6
ROPE_BASE = 1e6
MESH = pl.DeviceIdType.MESH
F32, BF16 = jnp.float32, jnp.bfloat16
LOG2E = 1.4426950408889634
QSCALE = HEAD ** -0.5 * LOG2E
VMEM_SPEC = pl.BlockSpec(memory_space=pltpu.VMEM)
ANY_SPEC = pl.BlockSpec(memory_space=pl.ANY)
SMEM_SPEC = pl.BlockSpec(memory_space=pltpu.SMEM)
VMEM_LIMIT = 60 * 2**20


def dot(a, b, dims):
    return lax.dot_general(a, b, (dims, ((), ())), preferred_element_type=F32)


NN = ((1,), (0,))
NT = ((1,), (1,))
TN = ((0,), (0,))


def flip(f, mask):
    bit = 1
    while bit <= mask:
        if mask & bit:
            f = f + bit - 2 * bit * lax.rem(lax.div(f, bit), 2)
        bit *= 2
    return f


def remote(src, dst, send, recv, **where):
    return pltpu.make_async_remote_copy(
        src_ref=src, dst_ref=dst, send_sem=send, recv_sem=recv,
        device_id=where, device_id_type=MESH)


def pick(index, values):
    out = jnp.int32(values[-1])
    for k in range(len(values) - 1):
        out = jnp.where(index == k, jnp.int32(values[k]), out)
    return out


def near_order(n):
    return [sorted(range(n), key=lambda s: (abs(s - z), s)) for z in range(n)]


def bit_orders(fs):
    bits = [1 << b for b in range(fs.bit_length() - 1)]
    return bits, bits[::-1]


def combos(bits):
    out = [0]
    for b in bits:
        out = out + [m + b for m in out]
    return out


def plane_copies(half, stage, fs, f, view, ssem, rsem):
    order = bit_orders(fs)[half]
    partner = flip(f, order[stage])
    base = (1 << stage) - 1
    out = []
    for m, mask in enumerate(combos(order[:stage])):
        g = flip(f, mask)
        out.append(remote(view(g), view(g), ssem.at[base + m], rsem.at[base + m], fsdp=partner))
    return out


UNIT = 128


def head_means(*values):
    ones = jnp.full((HEAD, HEAD), 1.0 / HEAD, BF16)
    return [dot(v.astype(BF16), ones, NN) for v in values]


def rope_tables():
    freqs = np.float32(ROPE_BASE) ** (-(np.arange(0, HEAD, 2, dtype=np.float32) / np.float32(HEAD)))
    places = np.arange((PBLOCKS + 1) * BLOCK, dtype=np.float32)
    angles = (places[:, None] * freqs[None, :].astype(np.float32)).astype(np.float64)
    cos, sin = np.cos(angles), np.sin(angles)
    shape = (-1, UNIT, HEAD)
    return (np.concatenate([cos, cos], axis=1).astype(np.float32).reshape(shape),
            np.concatenate([-sin, sin], axis=1).astype(np.float32).reshape(shape))


def rope_rows(table_ref, block_ref, first, count):
    per = BLOCK // UNIT
    out = []
    for i in range(count):
        unit = first + i
        out.append(table_ref[jnp.minimum(block_ref[lax.div(unit, per)], PBLOCKS) * per + lax.rem(unit, per)])
    return jnp.concatenate(out, axis=0)


def head_norm_rope(pre, gain, cos, sins):
    n = pre * lax.rsqrt(jnp.mean(pre * pre, axis=-1, keepdims=True) + EPS) * gain
    return n * cos + pltpu.roll(n, HEAD // 2, 1) * sins


def gather_kernel(dims, block_ref, x_ref, dy_ref, gain_ref, wq_in, wk_in, wv_in, wg_in, wu_in, wd_in, wo_in,
                  cos_ref, sin_ref, qg_ref, kg_ref,
                  a_out, q_out, k_out, v_out, pre_out, wall_ref, w_ref, dyp_ref,
                  a_ref, q_ref, k_ref, v_ref, pre_ref, out_sems, wqkv_ref, wz_ref, zs, zr, cs, cr, ws, wr, ms, mr, ps, pr, ls):
    fs, nc, nz = dims
    f, c, z = lax.axis_index("fsdp"), lax.axis_index("ctx"), lax.axis_index("tp")
    o = 1 - c
    me = f * nc + c
    others = [(df, dc) for df in range(fs) for dc in range(nc) if (df, dc) != (0, 0)]

    barrier = pltpu.get_barrier_semaphore()
    for df, dc in others:
        pl.semaphore_signal(barrier, inc=1, device_id={"fsdp": lax.rem(f + df, fs), "ctx": lax.rem(c + dc, nc)}, device_id_type=MESH)

    @pl.when(z > 0)
    def _():
        pl.semaphore_signal(barrier, inc=1, device_id={"tp": z - 1}, device_id_type=MESH)

    @pl.when(z < nz - 1)
    def _():
        pl.semaphore_signal(barrier, inc=1, device_id={"tp": z + 1}, device_id_type=MESH)
    x = x_ref[...].astype(F32)
    a_ref[c * nz + z] = (x * lax.rsqrt(jnp.mean(x * x, axis=-1, keepdims=True) + EPS) * gain_ref[...]).astype(BF16)
    pl.semaphore_wait(barrier, len(others) + jnp.where(z > 0, 1, 0) + jnp.where(z < nz - 1, 1, 0))

    row = a_ref.at[c * nz + z]
    up = remote(row, row, zs.at[z], zr.at[z], tp=jnp.minimum(z + 1, nz - 1))
    down = remote(row, row, zs.at[nz], zr.at[z], tp=jnp.maximum(z - 1, 0))
    pl.when(z < nz - 1)(up.start)
    pl.when(z > 0)(down.start)
    across = remote(row, row, cs.at[z], cr.at[z], ctx=o)
    across.start()
    dyc = remote(dy_ref, dyp_ref.at[c], ms.at[1], mr.at[1], ctx=o)
    dyc.start()
    dyp_ref[c] = dy_ref[...]

    def pack(packed, parts):
        at = 0
        for ref, turned in parts:
            value = ref[...].T if turned else ref[...]
            step = value.shape[1] // nc
            for cc in range(nc):
                packed[cc, :, at:at + step] = value[:, cc * step:(cc + 1) * step]
            at += step
    pack(wqkv_ref, ((wq_in, False), (wk_in, False), (wv_in, False)))
    wall_ref[me] = wqkv_ref[c]
    pack(wz_ref, ((wg_in, False), (wu_in, False), (wd_in, True), (wo_in, True)))
    own_w = pltpu.make_async_copy(wz_ref.at[c], w_ref.at[z, f, c], ls.at[0])
    own_w.start()
    for i, (df, dc) in enumerate(others):
        tf, tc = lax.rem(f + df, fs), lax.rem(c + dc, nc)
        remote(wqkv_ref.at[tc], wall_ref.at[me], ws.at[i], wr.at[me], fsdp=tf, ctx=tc).start()
    half = remote(wz_ref.at[o], w_ref.at[z, f, c], ms.at[0], mr.at[0], ctx=o)
    half.start()

    def plane(half_index, stage):
        return plane_copies(half_index, stage, fs, f, lambda g: w_ref.at[z, g, half_index], ps.at[half_index], pr.at[half_index])
    stages = fs.bit_length() - 1

    own_w.wait()
    remote(wz_ref.at[0], w_ref.at[z, f, o], ms.at[0], mr.at[0], ctx=o).wait_recv()
    for hi in range(2):
        for cp in plane(hi, 0):
            cp.start()
    q_cols = q_ref.shape[-1]

    def project(s):
        y = dot(a_ref[s], wall_ref[...].reshape(-1, wall_ref.shape[2]), NN)
        pre_ref[s] = y[:, :q_cols + HEAD].astype(BF16)
        units = a_ref.shape[1] // UNIT
        cos, sins = rope_rows(cos_ref, block_ref, s * units, units), rope_rows(sin_ref, block_ref, s * units, units)
        for h in range(q_cols // HEAD):
            q_ref[s, :, h * HEAD:(h + 1) * HEAD] = (head_norm_rope(y[:, h * HEAD:(h + 1) * HEAD], qg_ref[...], cos, sins) * QSCALE).astype(BF16)
        k_ref[s] = head_norm_rope(y[:, q_cols:q_cols + HEAD], kg_ref[...], cos, sins).astype(BF16)
        v_ref[s, :, :HEAD] = y[:, q_cols + HEAD:].astype(BF16)
        v_ref[s, :, HEAD:] = jnp.ones_like(v_ref[s, :, HEAD:])

    def take(hop):
        @pl.loop(0, 2 if hop == 0 else 4)
        def _(i):
            across_, way = (i, 0) if hop == 0 else (lax.rem(i, 2), lax.div(i, 2))
            src = z + (2 * way - 1) * hop

            @pl.when((src >= 0) & (src < nz))
            def _():
                s = jnp.where(across_ == 0, c, o) * nz + src

                @pl.when(across_ == 1)
                def _():
                    remote(a_ref.at[s], a_ref.at[s], cs.at[src], cr.at[src], ctx=o).wait_recv()
                project(s)
                for cp in results(s):
                    cp.start()

    def results(s):
        pairs = ((a_ref, a_out), (q_ref, q_out), (k_ref, k_out), (v_ref, v_out), (pre_ref, pre_out))
        return [pltpu.make_async_copy(src.at[s], dst.at[s], out_sems.at[i, s]) for i, (src, dst) in enumerate(pairs)]

    for hop in range(1, nz):
        for way in range(2):
            src = z + (2 * way - 1) * hop

            @pl.when((src >= 0) & (src < nz))
            def _():
                part = a_ref.at[c * nz + src]
                remote(part, part, zs.at[src], zr.at[src], ctx=o).wait_recv()
                if way == 0:
                    pl.when(z < nz - 1)(remote(part, part, zs.at[src], zr.at[src], tp=jnp.minimum(z + 1, nz - 1)).start)
                else:
                    pl.when(z > 0)(remote(part, part, zs.at[src], zr.at[src], tp=jnp.maximum(z - 1, 0)).start)
                remote(part, part, cs.at[src], cr.at[src], ctx=o).start()
        if hop == 1:
            for i, (df, dc) in enumerate(others):
                src = lax.rem(f + df, fs) * nc + lax.rem(c + dc, nc)
                remote(wqkv_ref.at[0], wall_ref.at[src], ws.at[i], wr.at[src], ctx=o).wait_recv()
        take(hop - 1)
        stage = hop - 1
        if stage < stages:
            for hi in range(2):
                for cp in plane(hi, stage):
                    cp.wait_recv()
                if stage + 1 < stages:
                    for cp in plane(hi, stage + 1):
                        cp.start()
    take(nz - 1)
    for stage in range(nz - 1, stages):
        for hi in range(2):
            for cp in plane(hi, stage):
                cp.wait_recv()
            if stage + 1 < stages:
                for cp in plane(hi, stage + 1):
                    cp.start()
    for s in range(nc * nz):
        for cp in results(s):
            cp.wait()
    for stage in range(stages):
        for hi in range(2):
            for cp in plane(hi, stage):
                cp.wait_send()
    for src in range(nz):
        @pl.when(((src <= z) & (z < nz - 1)) | ((src > z) & (z > 0)))
        def _():
            remote(row, row, zs.at[src], zr.at[src], ctx=o).wait_send()
        remote(row, row, cs.at[src], cr.at[src], ctx=o).wait_send()

    @pl.when(z > 0)
    def _():
        remote(row, row, zs.at[nz], zr.at[0], ctx=o).wait_send()
    for i in range(len(others)):
        remote(wqkv_ref.at[0], wall_ref.at[0], ws.at[i], wr.at[0], ctx=o).wait_send()
    half.wait_send()
    dyc.wait_send()
    remote(dy_ref, dyp_ref.at[o], ms.at[1], mr.at[1], ctx=o).wait_recv()


def gather_call(dims, block, x, dy, gain, weights, cos, sin, qg, kg):
    fs, nc, nz = dims
    rows, width = x.shape
    ns = nc * nz
    shard = weights[0].shape[0]
    q_cols = weights[0].shape[1] // nc
    cols = q_cols + 2 * HEAD
    wcols = 3 * (weights[3].shape[1] // nc) + q_cols
    DMA = pltpu.SemaphoreType.DMA
    return pl.pallas_call(
        lambda *refs: gather_kernel(dims, *refs),
        out_shape=(
            jax.ShapeDtypeStruct((ns, rows, width), BF16),
            jax.ShapeDtypeStruct((ns, rows, q_cols), BF16),
            jax.ShapeDtypeStruct((ns, rows, HEAD), BF16),
            jax.ShapeDtypeStruct((ns, rows, 2 * HEAD), BF16),
            jax.ShapeDtypeStruct((ns, rows, q_cols + HEAD), BF16),
            jax.ShapeDtypeStruct((fs * nc, shard, cols), BF16),
            jax.ShapeDtypeStruct((nz, fs, nc, shard, wcols), BF16),
            jax.ShapeDtypeStruct((nc, rows, width), BF16),
        ),
        in_specs=[SMEM_SPEC] + [VMEM_SPEC] * 14,
        out_specs=(ANY_SPEC,) * 5 + (VMEM_SPEC, ANY_SPEC, VMEM_SPEC),
        scratch_shapes=[
            pltpu.VMEM((ns, rows, width), BF16), pltpu.VMEM((ns, rows, q_cols), BF16), pltpu.VMEM((ns, rows, HEAD), BF16),
            pltpu.VMEM((ns, rows, 2 * HEAD), BF16), pltpu.VMEM((ns, rows, q_cols + HEAD), BF16), DMA((5, ns)),
            pltpu.VMEM((nc, shard, cols), BF16), pltpu.VMEM((nc, shard, wcols), BF16),
            DMA((nz + 1,)), DMA((nz,)), DMA((nz,)), DMA((nz,)),
            DMA((fs * nc - 1,)), DMA((fs * nc,)), DMA((2,)), DMA((2,)),
            DMA((2, fs - 1)), DMA((2, fs - 1)), DMA((2,)),
        ],
        compiler_params=pltpu.CompilerParams(collective_id=0, has_side_effects=True, vmem_limit_bytes=VMEM_LIMIT),
        cost_estimate=pl.CostEstimate(flops=2 * ns * rows * width * cols, bytes_accessed=30 * 2**20, transcendentals=0),
    )(block, x, dy, gain, *weights, cos, sin, qg, kg)
HALF = BLOCK // 2


def full_keys(qb):
    return min(qb, PBLOCKS)


def stack_heads(rows):
    return jnp.concatenate([rows[:, h * HEAD:(h + 1) * HEAD] for h in range(rows.shape[1] // HEAD)], axis=0)


def slot_of(block_ref, b):
    out = jnp.int32(0)
    for s in range(1, BLOCKS):
        out = jnp.where(block_ref[s] == b, jnp.int32(s), out)
    return out


def attend_kernel(dims, keep, block_ref, q_ref, k_ref, v_ref, wi_ref, w_ref, or_ref, o_ref, l_ref,
                  ob, zs, zr, ps, pr, xs, xr):
    fs, nc, nz = dims
    f, c, z = lax.axis_index("fsdp"), lax.axis_index("ctx"), lax.axis_index("tp")
    rows = or_ref.shape[2]
    barrier = pltpu.get_barrier_semaphore()
    bits = bit_orders(fs)[0]
    for bit in bits:
        pl.semaphore_signal(barrier, inc=1, device_id={"fsdp": flip(f, bit)}, device_id_type=MESH)
    for dz in range(1, nz):
        pl.semaphore_signal(barrier, inc=1, device_id={"tp": lax.rem(z + dz, nz)}, device_id_type=MESH)
    pl.semaphore_wait(barrier, len(bits) + nz - 1)

    def piece(ref, hop):
        return ref.at[:, :, pl.ds(keep, ref.shape[-1] - keep)] if hop == nz - 1 else ref

    def up(src, sem, hop):
        part = piece(w_ref.at[src, f], hop)
        return remote(part, part, zs.at[sem], zr.at[src], tp=jnp.minimum(z + 1, nz - 1))

    def down(src, sem, hop):
        part = piece(w_ref.at[src, f], hop)
        return remote(part, part, zs.at[sem], zr.at[src], tp=jnp.maximum(z - 1, 0))
    pl.when(z < nz - 1)(up(z, z, 1).start)
    pl.when(z > 0)(down(z, nz, 1).start)
    stages = fs.bit_length() - 1

    def plane(src, hi, stage, cut):
        def view(g):
            ref = w_ref.at[src, g, hi]
            return ref.at[:, pl.ds(keep, ref.shape[-1] - keep)] if cut else ref
        return plane_copies(hi, stage, fs, f, view, ps.at[src, hi], pr.at[src, hi])

    edge = (z == 0) | (z == nz - 1)

    def planes(hop, act):
        if hop == nz - 2:
            pl.when(edge)(lambda: act(False))
            pl.when(jnp.logical_not(edge))(lambda: act(True))
        else:
            act(hop == nz - 1)

    def each(hop, act):
        for way in range(2):
            src = z + (2 * way - 1) * hop

            @pl.when((src >= 0) & (src < nz))
            def _():
                act(way, src)

    def arrive(hop):
        def act(way, src):
            up(src, src, hop).wait_recv()
            if way == 0:
                pl.when(z < nz - 1)(up(src, src, hop + 1).start)
            else:
                pl.when(z > 0)(down(src, src, hop + 1).start)

            def go(cut):
                for hi in range(2):
                    for cp in plane(src, hi, 0, cut):
                        cp.start()
            planes(hop, go)
        each(hop, act)

    def spread(hop, stage):
        def act(way, src):
            def go(cut):
                for hi in range(2):
                    for cp in plane(src, hi, stage, cut):
                        cp.wait_recv()
                    if stage + 1 < stages:
                        for cp in plane(src, hi, stage + 1, cut):
                            cp.start()
            planes(hop, go)
        each(hop, act)

    tri = lax.broadcasted_iota(jnp.int32, (HALF, HALF), 0) >= lax.broadcasted_iota(jnp.int32, (HALF, HALF), 1)
    heads = q_ref.shape[2] // HEAD
    for qb in range(BLOCKS):
        if qb == BLOCKS - 1:
            arrive(1)
        q2 = stack_heads(q_ref[slot_of(block_ref, qb)])

        def step(kb, acc):
            k = k_ref[slot_of(block_ref, kb)]
            v = v_ref[slot_of(block_ref, kb)]
            return acc + dot(jnp.exp2(dot(q2, k, NT)).astype(BF16), v, NN)
        acc = jnp.zeros((heads * BLOCK, 2 * HEAD), F32)
        if full_keys(qb):
            acc = lax.fori_loop(0, full_keys(qb), step, acc)
        k = k_ref[slot_of(block_ref, qb)]
        v = v_ref[slot_of(block_ref, qb)]
        for h in range(heads):
            part = slice(h * BLOCK, (h + 1) * BLOCK)
            first = slice(h * BLOCK, h * BLOCK + HALF)
            second = slice(h * BLOCK + HALF, (h + 1) * BLOCK)
            p0 = jnp.where(tri, jnp.exp2(dot(q2[first], k[:HALF], NT)), 0.0).astype(BF16)
            p1 = jnp.exp2(dot(q2[second], k, NT))
            p1 = jnp.concatenate([p1[:, :HALF], jnp.where(tri, p1[:, HALF:], 0.0)], axis=1).astype(BF16)
            a = acc[part] + jnp.concatenate([dot(p0, v[:HALF], NN), dot(p1, v, NN)], axis=0)
            ob[qb, :, h * HEAD:(h + 1) * HEAD] = (a[:, :HEAD] / a[:, HEAD:]).astype(BF16)
            l_ref[qb, :, part] = jnp.log2(a[:, HEAD:]).T[0:8]
    for s in range(BLOCKS):
        o_ref[s * BLOCK:(s + 1) * BLOCK] = ob[block_ref[s]]

    def part_rows(side, zz):
        return pl.ds(pl.multiple_of((side * nz + zz) * rows, 128), rows)
    for hop in range(2, nz - 1):
        arrive(hop)
    for dz in range(1, nz):
        to = lax.rem(z + dz, nz)
        for side in range(nc):
            remote(o_ref.at[part_rows(side, to)], or_ref.at[z, side], xs.at[dz, side], xr.at[z, side], tp=to).start()
    for side in range(nc):
        or_ref[z, side] = o_ref[part_rows(side, z)]
    for hop in range(1, nz):
        for stage in range(stages):
            spread(hop, stage)
            if hop == nz - 2 and stage == 0:
                arrive(nz - 1)
    for dz in range(1, nz):
        src = lax.rem(z + dz, nz)
        for side in range(nc):
            cp = remote(o_ref.at[part_rows(side, 0)], or_ref.at[src, side], xs.at[dz, side], xr.at[src, side], tp=src)
            cp.wait_recv()
            cp.wait_send()
    for hop in range(1, nz):
        def left(way, src):
            if way == 0:
                pl.when(z < nz - 1)(up(src, src, hop + 1).wait_send)
            else:
                pl.when(z > 0)(down(src, src, hop + 1).wait_send)

            def go(cut):
                for hi in range(2):
                    for stage in range(stages):
                        for cp in plane(src, hi, stage, cut):
                            cp.wait_send()
            planes(hop, go)
        each(hop, left)
    pl.when(z < nz - 1)(up(z, z, 1).wait_send)
    pl.when(z > 0)(down(z, nz, 1).wait_send)


def attend_call(dims, keep, block, q, k, v, w, rows):
    fs, nc, nz = dims
    q_cols = q.shape[2]
    span = BLOCKS * BLOCK
    heads = q_cols // HEAD
    DMA = pltpu.SemaphoreType.DMA
    return pl.pallas_call(
        lambda *refs: attend_kernel(dims, keep, *refs),
        out_shape=(
            jax.ShapeDtypeStruct(w.shape, BF16),
            jax.ShapeDtypeStruct((nz, nc, rows, q_cols), BF16),
            jax.ShapeDtypeStruct((span, q_cols), BF16),
            jax.ShapeDtypeStruct((BLOCKS, 8, heads * BLOCK), F32),
        ),
        in_specs=[SMEM_SPEC] + [VMEM_SPEC] * 3 + [ANY_SPEC],
        out_specs=(ANY_SPEC, VMEM_SPEC, VMEM_SPEC, VMEM_SPEC),
        scratch_shapes=[
            pltpu.VMEM((BLOCKS, BLOCK, q_cols), BF16),
            DMA((nz + 1,)), DMA((nz,)), DMA((nz, 2, fs - 1)), DMA((nz, 2, fs - 1)), DMA((nz, nc)), DMA((nz, nc)),
        ],
        input_output_aliases={4: 0},
        compiler_params=pltpu.CompilerParams(collective_id=1, has_side_effects=True, vmem_limit_bytes=VMEM_LIMIT),
        cost_estimate=pl.CostEstimate(flops=2 * 20 * BLOCK * BLOCK * heads * 3 * HEAD, bytes_accessed=30 * 2**20, transcendentals=0),
    )(block, q, k, v, w)
def reduce_order(fs, hi):
    return bit_orders(fs)[hi][::-1]


def reduce_masks(fs, hi):
    return combos(reduce_order(fs, hi)[1:][::-1])


def first_copies(hi, fs, f, view, land, ssem, rsem):
    bit = reduce_order(fs, hi)[0]
    return [remote(view(flip(flip(f, m), bit)), land(i), ssem.at[i], rsem.at[i], fsdp=flip(f, bit))
            for i, m in enumerate(reduce_masks(fs, hi))]


def later_copies(hi, stage, fs, f, held, land, ssem, rsem):
    bit = reduce_order(fs, hi)[stage]
    keep = fs >> (stage + 1)
    base = fs // 2 - (fs >> stage)
    return [remote(held(keep + i), land(base + i), ssem.at[base + i], rsem.at[base + i], fsdp=flip(f, bit)) for i in range(keep)]


def add_low(a, b):
    return (a.astype(F32) + b.astype(F32)).astype(BF16)


def early_parts(nz):
    return (nz - 1, 0) if nz > 1 else (0,)


def late_parts(nz):
    return tuple(t for t in range(nz - 2, 0, -1))


def rope_norm_back(g, pre, gain, cos, sins):
    c = g * cos + pltpu.roll(g * sins, HEAD // 2, 1)
    sc = c * gain
    square, mixed = head_means(pre * pre, sc * pre)
    inv = lax.rsqrt(square + EPS)
    n = pre * inv
    return inv * (sc - n * (inv * mixed)), c * n


def attend_back_kernel(dims, cut, block_ref, q_ref, k_ref, v_ref, o_ref, l_ref, do_ref, pre_hbm, cos_hbm, sin_hbm,
                       qg_ref, kg_ref, re_ref, dr_ref, g_ref, d_ref, te_ref, to_ref, tl_ref, ch_ref, qgg_ref, kgg_ref,
                       pre_ref, cos_ref, sin_ref, lp, dr, dq, dk, dv, he, ho, hl, ro, rl, rn, le, lo, ll, os, orr, fss, fsr, nss, nsr, xs, xr, hs, hr):
    fs, nc, nz = dims
    f, z = lax.axis_index("fsdp"), lax.axis_index("tp")
    heads = q_ref.shape[2] // HEAD
    early, late = early_parts(nz), late_parts(nz)[:-1]
    stages = fs.bit_length() - 1
    rest = pl.ds(cut, g_ref.shape[-1] - cut)
    barrier = pltpu.get_barrier_semaphore()
    bits = bit_orders(fs)[0]
    for bit in bits:
        pl.semaphore_signal(barrier, inc=1, device_id={"fsdp": flip(f, bit)}, device_id_type=MESH)
    for dz in range(1, nz):
        pl.semaphore_signal(barrier, inc=1, device_id={"tp": lax.rem(z + dz, nz)}, device_id_type=MESH)
    tables = [pltpu.make_async_copy(src, dst, lp.at[i]) for i, (src, dst) in enumerate(((pre_hbm, pre_ref), (cos_hbm, cos_ref), (sin_hbm, sin_ref)))]
    own = []
    for hi in range(2):
        for i, m in enumerate(reduce_masks(fs, hi)):
            for e, t in enumerate(early):
                own.append(pltpu.make_async_copy(g_ref.at[t, flip(f, m), hi, :, pl.ds(0, cut)], he.at[e, hi, i], le.at[e, hi, i]))
                own.append(pltpu.make_async_copy(g_ref.at[t, flip(f, m), hi, :, rest], ho.at[e, hi, i], lo.at[e, hi, i]))
            for j, t in enumerate(late):
                own.append(pltpu.make_async_copy(g_ref.at[t, flip(f, m), hi], hl.at[j, hi, i], ll.at[j, hi, i]))
    for cp in own + tables:
        cp.start()
    pl.semaphore_wait(barrier, len(bits) + nz - 1)

    units = dr_ref.shape[2]
    def spot(side, zz):
        return pl.ds((side * nz + zz) * units, units)
    for dz in range(1, nz):
        to = lax.rem(z + dz, nz)
        for side in range(nc):
            remote(dr_ref.at[to, side], dr.at[spot(side, z)], xs.at[dz, side], xr.at[z, side], tp=to).start()
    keep_own = [pltpu.make_async_copy(dr_ref.at[z, side], dr.at[spot(side, z)], lp.at[3 + side]) for side in range(nc)]
    for cp in keep_own:
        cp.start()

    def first_rest(e, hi):
        return first_copies(hi, fs, f, lambda g: g_ref.at[early[e], g, hi, :, rest], lambda i: ro.at[e, hi, i], os.at[e, hi], orr.at[e, hi])

    def first_late(j, hi):
        return first_copies(hi, fs, f, lambda g: g_ref.at[late[j], g, hi], lambda i: rl.at[j, hi, i], fss.at[j, hi], fsr.at[j, hi])

    def later(e, hi, stage):
        return later_copies(hi, stage, fs, f, lambda i: he.at[e, hi, i], lambda i: rn.at[e, hi, i], nss.at[e, hi], nsr.at[e, hi])
    for cp in own:
        cp.wait()
    for e in range(len(early)):
        for hi in range(2):
            he[e, hi] = add_low(he[e, hi], re_ref[e, hi])
            if stages > 1:
                for cp in later(e, hi, 1):
                    cp.start()

    def hop(e):
        return remote(te_ref.at[e], ch_ref, hs.at[e], hr.at[0], tp=jnp.minimum(z + 1, nz - 1) if e == 0 else jnp.maximum(z - 1, 0))

    def finish_early():
        for stage in range(1, stages):
            keep = fs >> (stage + 1)
            base = fs // 2 - (fs >> stage)
            for e in range(len(early)):
                for hi in range(2):
                    for cp in later(e, hi, stage):
                        cp.wait_recv()
                    he[e, hi, :keep] = add_low(he[e, hi, :keep], rn[e, hi, base:base + keep])
                    if stage + 1 < stages:
                        for cp in later(e, hi, stage + 1):
                            cp.start()
        for e in range(len(early)):
            te_ref[e] = he[e, :, 0]
        pl.when(z == 0)(hop(0).start)
        pl.when(z == nz - 1)(hop(1).start)
        for e in range(len(early)):
            for hi in range(2):
                for cp in first_rest(e, hi):
                    cp.start()
        for j in range(len(late)):
            for hi in range(2):
                for cp in first_late(j, hi):
                    cp.start()

    tri = lax.broadcasted_iota(jnp.int32, (HALF, HALF), 0) <= lax.broadcasted_iota(jnp.int32, (HALF, HALF), 1)
    dk[...] = jnp.zeros_like(dk)
    dv[...] = jnp.zeros_like(dv)
    per = BLOCK // UNIT
    for h in range(heads):
        cols, logs = slice(h * HEAD, (h + 1) * HEAD), slice(h * BLOCK, (h + 1) * BLOCK)
        if h == 1:
            for cp in keep_own:
                cp.wait()
            for dz in range(1, nz):
                src = lax.rem(z + dz, nz)
                for side in range(nc):
                    remote(dr_ref.at[0, side], dr.at[spot(side, src)], xs.at[dz, side], xr.at[src, side], tp=src).wait_recv()
        for qb in range(BLOCKS):
            if h == 0 and qb == BLOCKS - 1:
                finish_early()
            at = slot_of(block_ref, qb)
            q = q_ref[at, :, cols]
            if h == 0:
                g = do_ref[at]
            else:
                g = jnp.concatenate([dr[at * per + i, :, (h - 1) * HEAD:h * HEAD] for i in range(per)], axis=0)
            delta = jnp.sum((g.astype(F32) * o_ref[at, :, cols].astype(F32)).T, axis=0, keepdims=True)
            log = l_ref[qb, 0:1, logs]

            def pair(kb, keys, start):
                k = k_ref[slot_of(block_ref, kb), keys]
                v = v_ref[slot_of(block_ref, kb), keys, :HEAD]
                qs, gs = q[start:], g[start:]
                p = jnp.exp2(dot(k, qs, NT) - log[:, start:])
                if diagonal:
                    width = k.shape[0]
                    p0 = jnp.where(tri, p[:, :width], 0.0)
                    p = p0 if p.shape[1] == width else jnp.concatenate([p0, p[:, width:]], axis=1)
                ds = (p * (dot(v, gs, NT) - delta[:, start:])).astype(BF16)
                dv[kb, keys] += dot(p.astype(BF16), gs, NN)
                dk[kb, keys] += dot(ds, qs, NN)
                return dot(k.T, ds, NN)
            diagonal = True
            low = pair(qb, slice(0, HALF), 0)
            high = pair(qb, slice(HALF, BLOCK), HALF)
            total = jnp.concatenate([low[:, :HALF], low[:, HALF:] + high], axis=1)
            diagonal = False
            for kb in range(full_keys(qb)):
                total = total + pair(kb, slice(0, BLOCK), 0)
            dq[qb, logs] = total.T

    for cp in tables:
        cp.wait()
    qgg_ref[...] = jnp.zeros_like(qgg_ref)
    kgg_ref[...] = jnp.zeros_like(kgg_ref)

    @pl.loop(0, BLOCKS)
    def _(s):
        b = block_ref[s]
        cos, sins = rope_rows(cos_ref, block_ref, s * per, per), rope_rows(sin_ref, block_ref, s * per, per)
        qs = dq[b]
        for h in range(heads):
            back, part = rope_norm_back(qs[h * BLOCK:(h + 1) * BLOCK] * HEAD ** -0.5, pre_ref[s, :, h * HEAD:(h + 1) * HEAD].astype(F32), qg_ref[...], cos, sins)
            d_ref[s, :, h * HEAD:(h + 1) * HEAD] = back.astype(BF16)
            qgg_ref[...] += jnp.sum(part, axis=0, keepdims=True)
        back, part = rope_norm_back(dk[b] * (1.0 / LOG2E), pre_ref[s, :, heads * HEAD:].astype(F32), kg_ref[...], cos, sins)
        d_ref[s, :, heads * HEAD:(heads + 1) * HEAD] = back.astype(BF16)
        kgg_ref[...] += jnp.sum(part, axis=0, keepdims=True)
        d_ref[s, :, (heads + 1) * HEAD:] = dv[b].astype(BF16)

    for e in range(len(early)):
        for hi in range(2):
            for cp in first_rest(e, hi):
                cp.wait_recv()
            to_ref[e, hi] = add_low(ho[e, hi], ro[e, hi])
    for j in range(len(late)):
        for hi in range(2):
            for cp in first_late(j, hi):
                cp.wait_recv()
            tl_ref[j, hi] = add_low(hl[j, hi], rl[j, hi])
    pl.when((z == 1) | (z == nz - 2))(hop(0).wait_recv)
    pl.when(z == 0)(hop(0).wait_send)
    pl.when(z == nz - 1)(hop(1).wait_send)
    for dz in range(1, nz):
        for side in range(nc):
            remote(dr_ref.at[0, side], dr.at[spot(side, 0)], xs.at[dz, side], xr.at[0, side], tp=lax.rem(z + dz, nz)).wait_send()
    for hi in range(2):
        for j in range(len(late)):
            for cp in first_late(j, hi):
                cp.wait_send()
        for e in range(len(early)):
            for cp in first_rest(e, hi):
                cp.wait_send()
            for stage in range(1, stages):
                for cp in later(e, hi, stage):
                    cp.wait_send()


def attend_back_call(dims, block, q, k, v, o, l, do, pre, cos, sin, qg, kg, re, dr, g):
    fs, nc, nz = dims
    q_cols = q.shape[2]
    heads = q_cols // HEAD
    early, late = len(early_parts(nz)), len(late_parts(nz)) - 1
    shard, cols = g.shape[3:]
    cut = re.shape[4]
    half, more = fs // 2, max(fs // 2 - 1, 1)
    DMA = pltpu.SemaphoreType.DMA
    V = pltpu.VMEM
    return pl.pallas_call(
        lambda *refs: attend_back_kernel(dims, cut, *refs),
        out_shape=(
            jax.ShapeDtypeStruct((BLOCKS, BLOCK, q_cols + 2 * HEAD), BF16),
            jax.ShapeDtypeStruct((early, 2, shard, cut), BF16),
            jax.ShapeDtypeStruct((early, 2, half, shard, cols - cut), BF16),
            jax.ShapeDtypeStruct((late, 2, half, shard, cols), BF16),
            jax.ShapeDtypeStruct((2, shard, cut), BF16),
            jax.ShapeDtypeStruct((1, HEAD), F32),
            jax.ShapeDtypeStruct((1, HEAD), F32),
        ),
        in_specs=[SMEM_SPEC] + [VMEM_SPEC] * 6 + [ANY_SPEC] * 3 + [VMEM_SPEC] * 3 + [ANY_SPEC] * 2,
        out_specs=(VMEM_SPEC,) * 7,
        scratch_shapes=[
            V(pre.shape, BF16), V(cos.shape, F32), V(sin.shape, F32), DMA((3 + nc,)),
            V((BLOCKS * BLOCK // UNIT, UNIT, q_cols - HEAD), BF16),
            V((BLOCKS, heads * BLOCK, HEAD), F32), V((BLOCKS, BLOCK, HEAD), F32), V((BLOCKS, BLOCK, HEAD), F32),
            V((early, 2, half, shard, cut), BF16), V((early, 2, half, shard, cols - cut), BF16), V((late, 2, half, shard, cols), BF16),
            V((early, 2, half, shard, cols - cut), BF16), V((late, 2, half, shard, cols), BF16), V((early, 2, more, shard, cut), BF16),
            DMA((early, 2, half)), DMA((early, 2, half)), DMA((late, 2, half)),
            DMA((early, 2, half)), DMA((early, 2, half)), DMA((late, 2, half)), DMA((late, 2, half)),
            DMA((early, 2, more)), DMA((early, 2, more)), DMA((nz, nc)), DMA((nz, nc)), DMA((2,)), DMA((1,)),
        ],
        compiler_params=pltpu.CompilerParams(collective_id=3, has_side_effects=True, vmem_limit_bytes=VMEM_LIMIT),
        cost_estimate=pl.CostEstimate(flops=2 * 20 * BLOCK * BLOCK * heads * 5 * HEAD, bytes_accessed=40 * 2**20, transcendentals=0),
    )(block, q, k, v, o, l, do, pre, cos, sin, qg, kg, re, dr, g)
def column_parts(dims, hidden, q_cols):
    return (0, hidden, 2 * hidden, 3 * hidden, 3 * hidden + q_cols)


def feed_kernel(dims, x_ref, dy_ref, o_ref, w_ref, gain_ref, out_ref, dh_ref, fg_ref, do_ref, dr_ref, g_ref, re_ref,
                wb, ge, hs, b_ref, da_ref, dgu, u_ref, acc, snd, rcv, dos, bt, yt, at,
                ls, gs, ss, sr, xs, xr, fss, fsr, os, orr, ps, pr, lq):
    fs, nc, nz = dims
    f, c, z = lax.axis_index("fsdp"), lax.axis_index("ctx"), lax.axis_index("tp")
    o = 1 - c
    rows, width = x_ref.shape
    q_cols = o_ref.shape[3]
    hidden = (w_ref.shape[2] - q_cols) // 3
    gate, up_, down_, out_, end = column_parts(dims, hidden, q_cols)
    edge = (z == 0) | (z == nz - 1)
    low = z < nz // 2
    last = jnp.where(low, nz - 1, 0)
    keep = down_

    def load_out(zz):
        part = pl.ds(out_, end - out_)
        return pltpu.make_async_copy(w_ref.at[zz, :, part], wb.at[zz, :, part], ls.at[0, zz])

    def loads(act):
        for zz in range(nz):
            here = last == zz
            for late in range(2):
                part = pl.ds(keep if late else 0, out_ - (keep if late else 0))

                @pl.when(here if late else jnp.logical_not(here))
                def _():
                    act(pltpu.make_async_copy(w_ref.at[zz, :, part], wb.at[zz, :, part], ls.at[1, zz]))
    for zz in range(nz):
        load_out(zz).start()
    loads(lambda cp: cp.start())
    barrier = pltpu.get_barrier_semaphore()
    pl.semaphore_signal(barrier, inc=1, device_id={"ctx": o}, device_id_type=MESH)
    for dz in range(1, nz):
        pl.semaphore_signal(barrier, inc=1, device_id={"tp": lax.rem(z + dz, nz)}, device_id_type=MESH)
    bits = bit_orders(fs)[0]
    stages = len(bits)
    for bit in bits:
        pl.semaphore_signal(barrier, inc=1, device_id={"fsdp": flip(f, bit)}, device_id_type=MESH)
    pl.semaphore_wait(barrier, nz + len(bits))
    early = early_parts(nz)
    shard = width // (fs * nc)

    def shard_rows(g, hi, n=1):
        return pl.ds(pl.multiple_of((g * nc + hi) * shard, shard), n * shard)

    def chunk(k):
        return pl.ds(k * (keep // 2), keep // 2)

    def outward(way, k):
        part = 0 if way == 0 else nz - 1
        to = jnp.minimum(z + 1, nz - 1) if way == 0 else jnp.maximum(z - 1, 0)
        ref = shard_rows(f, 0, nc)
        return remote(w_ref.at[part, ref, chunk(k)], wb.at[part, ref, chunk(k)], os.at[way, k], orr.at[k], tp=to)

    def out_copies(act):
        for k in range(2):
            pl.when(z == nz - 2)(lambda: act(outward(0, k)))
            pl.when(z == 1)(lambda: act(outward(1, k)))
    out_copies(lambda cp: cp.start())

    def own_part(k):
        ref = shard_rows(f, 0, nc)
        return pltpu.make_async_copy(w_ref.at[last, ref, chunk(k)], wb.at[last, ref, chunk(k)], lq.at[k])

    @pl.when(jnp.logical_not(edge))
    def _():
        for k in range(2):
            own_part(k).start()

    def late_plane(hi, stage, k):
        return plane_copies(hi, stage, fs, f, lambda g: wb.at[last, shard_rows(g, hi), chunk(k)], ps.at[hi, k], pr.at[hi, k])

    def late_arrive(k):
        @pl.when(edge)
        def _():
            ref = shard_rows(f, 0, nc)
            remote(w_ref.at[0, ref, chunk(k)], wb.at[last, ref, chunk(k)], os.at[0, k], orr.at[k], ctx=o).wait_recv()

        @pl.when(jnp.logical_not(edge))
        def _():
            own_part(k).wait()
        for hi in range(2):
            for cp in late_plane(hi, 0, k):
                cp.start()

    def late_spread(stage, k):
        for hi in range(2):
            for cp in late_plane(hi, stage, k):
                cp.wait_recv()
            if stage + 1 < stages:
                for cp in late_plane(hi, stage + 1, k):
                    cp.start()

    def first(e, hi):
        def view(g):
            return ge.at[e, shard_rows(g, hi)]
        return first_copies(hi, fs, f, view, lambda i: re_ref.at[e, hi, i], fss.at[e, hi], fsr.at[e, hi])

    def cross(i, src, dst):
        return remote(src, dst, ss.at[i], sr.at[i], ctx=o)
    for zz in range(nz):
        load_out(zz).wait()

    def project(side):
        total = dot(o_ref[0, side], wb[0, :, out_:end], NT)
        for zz in range(1, nz):
            total += dot(o_ref[zz, side], wb[zz, :, out_:end], NT)
        return total
    snd[0] = project(o).astype(BF16)
    cross(0, snd.at[0], rcv.at[0]).start()
    own = project(c)
    loads(lambda cp: cp.wait())

    @pl.loop(0, nz)
    def _(zz):
        dgu[zz, :, :hidden] = dot(dy_ref[...].reshape(nc * rows, width), wb[zz, :, down_:out_], NN).astype(BF16)
    late_arrive(0)
    cross(0, snd.at[0], rcv.at[0]).wait_recv()
    h = x_ref[...].astype(F32) + own + rcv[0].astype(F32)
    hs[...] = h
    b_ref[c] = (h * lax.rsqrt(jnp.mean(h * h, axis=-1, keepdims=True) + EPS) * gain_ref[...]).astype(BF16)
    cross(1, b_ref.at[c], b_ref.at[c]).start()
    yt[...] = dy_ref[...].reshape(nc * rows, width).T
    late_spread(0, 0)
    late_arrive(1)
    cross(1, b_ref.at[c], b_ref.at[o]).wait_recv()

    @pl.loop(0, nz)
    def _(i):
        zz = jnp.where(low, i, nz - 1 - i)

        @pl.when(i == 1)
        def _():
            late_spread(0, 1)

        @pl.when(i == nz - 1)
        def _():
            for stage in range(1, stages):
                for k in range(2):
                    late_spread(stage, k)
        both = b_ref[...].reshape(nc * rows, width)
        gu = dot(both, wb[zz, :, gate:down_], NN)
        du = dgu[zz, :, :hidden].astype(F32)
        gt, uv = gu[:, :hidden], gu[:, hidden:]
        sig = 1.0 / (1.0 + jnp.exp(-gt))
        silu = gt * sig
        hid = (silu * uv).astype(BF16)
        u_ref[zz] = hid
        dgu[zz, :, :hidden] = (du * uv * sig * (1.0 + gt * (1.0 - sig))).astype(BF16)
        dgu[zz, :, hidden:] = (du * silu).astype(BF16)

    def side_rows(side):
        return pl.ds(pl.multiple_of(side * rows, 128), rows)

    def feed_sum(side, left, start, stop):
        total = dot(left[0, side_rows(side)], wb[0, :, start:stop], NT)
        for zz in range(1, nz):
            total += dot(left[zz, side_rows(side)], wb[zz, :, start:stop], NT)
        return total
    snd[1] = feed_sum(o, dgu, gate, down_).astype(BF16)
    cross(2, snd.at[1], rcv.at[1]).start()
    acc[...] = feed_sum(c, dgu, gate, down_)
    bt[...] = b_ref[...].reshape(nc * rows, width).T

    def feed_grads(zz, into):
        into[:, gate:down_] = dot(bt[...], dgu[zz], NN).astype(BF16)
        into[:, down_:out_] = dot(yt[...], u_ref[zz], NN).astype(BF16)

    def early_grads(e):
        feed_grads(early[e], ge.at[e])
        for hi in range(2):
            for cp in first(e, hi):
                cp.start()
    early_grads(0)
    cross(2, snd.at[1], rcv.at[1]).wait_recv()
    db = acc[...] + rcv[1].astype(F32)
    h = hs[...]
    inv = lax.rsqrt(jnp.mean(h * h, axis=-1, keepdims=True) + EPS)
    n = h * inv
    sc = db * gain_ref[...]
    dh = dy_ref[c].astype(F32) + inv * (sc - n * jnp.mean(sc * n, axis=-1, keepdims=True))
    fg_ref[...] = jnp.sum(db * n, axis=0, keepdims=True)
    dh_ref[...] = dh
    da_ref[c] = dh.astype(BF16)
    cross(4, da_ref.at[c], da_ref.at[c]).start()
    for e in range(1, len(early)):
        early_grads(e)
    snd[2] = feed_sum(o, u_ref, down_, out_).astype(BF16)
    cross(3, snd.at[2], rcv.at[2]).start()
    acc[...] = feed_sum(c, u_ref, down_, out_)
    cross(4, da_ref.at[c], da_ref.at[o]).wait_recv()

    def stores(zz):
        if zz not in early:
            return [pltpu.make_async_copy(wb.at[zz], g_ref.at[zz], gs.at[0, zz])]
        lead, tail = pl.ds(0, out_), pl.ds(out_, end - out_)
        return [pltpu.make_async_copy(ge.at[early.index(zz)], g_ref.at[zz, :, lead], gs.at[0, zz]),
                pltpu.make_async_copy(wb.at[zz, :, tail], g_ref.at[zz, :, tail], gs.at[1, zz])]

    @pl.loop(1, nz + 1)
    def _(dz):
        to = lax.rem(z + dz, nz)
        both = dot(da_ref[...].reshape(nc * rows, width), wb[to, :, out_:end], NN).astype(BF16).reshape(nc, rows, q_cols)
        dos[to] = both[:, :, :HEAD]
        dr_ref[to] = both[:, :, HEAD:]

        @pl.when(dz < nz)
        def _():
            for side in range(nc):
                remote(dos.at[to, side], do_ref.at[side, z], xs.at[dz, side], xr.at[z, side], tp=to).start()
    for side in range(nc):
        do_ref[side, z] = dos[z, side]
    cross(3, snd.at[2], rcv.at[2]).wait_recv()
    out_ref[...] = (hs[...] + acc[...] + rcv[2].astype(F32)).astype(BF16)
    at[...] = da_ref[...].reshape(nc * rows, width).T
    for zz in early + late_parts(nz):
        wb[zz, :, out_:end] = dot(at[...], o_ref[zz].reshape(nc * rows, q_cols), NN).astype(BF16)
        if zz not in early:
            feed_grads(zz, wb.at[zz])
        for cp in stores(zz):
            cp.start()
    for zz in range(nz):
        for cp in stores(zz):
            cp.wait()

    for hi in range(2):
        for stage in range(stages):
            for k in range(2):
                for cp in late_plane(hi, stage, k):
                    cp.wait_send()
    for dz in range(1, nz):
        src = lax.rem(z + dz, nz)
        for side in range(nc):
            cp = remote(dos.at[0, side], do_ref.at[side, src], xs.at[dz, side], xr.at[src, side], tp=src)
            cp.wait_recv()
            cp.wait_send()
    out_copies(lambda cp: cp.wait_send())
    for e in range(len(early)):
        for hi in range(2):
            for cp in first(e, hi):
                cp.wait_recv()
                cp.wait_send()
    for i, part in enumerate((snd.at[0], b_ref.at[c], snd.at[1], snd.at[2], da_ref.at[c])):
        cross(i, part, part).wait_send()


def feed_call(dims, x, dyp, o, w, gain):
    fs, nc, nz = dims
    rows, width = x.shape
    q_cols = o.shape[3]
    cols = w.shape[2]
    hidden = (cols - q_cols) // 3
    early = len(early_parts(nz))
    DMA = pltpu.SemaphoreType.DMA
    V = pltpu.VMEM
    return pl.pallas_call(
        lambda *refs: feed_kernel(dims, *refs),
        out_shape=(
            jax.ShapeDtypeStruct((rows, width), BF16),
            jax.ShapeDtypeStruct((rows, width), F32),
            jax.ShapeDtypeStruct((1, width), F32),
            jax.ShapeDtypeStruct((nc, nz, rows, HEAD), BF16),
            jax.ShapeDtypeStruct((nz, nc, rows, q_cols - HEAD), BF16),
            jax.ShapeDtypeStruct(w.shape, BF16),
            jax.ShapeDtypeStruct((early, 2, fs // 2, width // (fs * nc), 3 * hidden), BF16),
        ),
        in_specs=[VMEM_SPEC] * 3 + [ANY_SPEC, VMEM_SPEC],
        out_specs=(VMEM_SPEC,) * 5 + (ANY_SPEC, ANY_SPEC),
        scratch_shapes=[
            V(w.shape, BF16), V((early, width, 3 * hidden), BF16), V((rows, width), F32), V((nc, rows, width), BF16), V((nc, rows, width), BF16),
            V((nz, nc * rows, 2 * hidden), BF16), V((nz, nc * rows, hidden), BF16),
            V((rows, width), F32),
            V((3, rows, width), BF16), V((3, rows, width), BF16), V((nz, nc, rows, HEAD), BF16),
            V((width, nc * rows), BF16), V((width, nc * rows), BF16), V((width, nc * rows), BF16),
            DMA((2, nz)), DMA((2, nz)), DMA((5,)), DMA((5,)), DMA((nz, nc)), DMA((nz, nc)),
            DMA((early, 2, fs // 2)), DMA((early, 2, fs // 2)),
            DMA((2, 2)), DMA((2,)), DMA((2, 2, fs - 1)), DMA((2, 2, fs - 1)), DMA((2,)),
        ],
        compiler_params=pltpu.CompilerParams(collective_id=2, has_side_effects=True, vmem_limit_bytes=VMEM_LIMIT),
        cost_estimate=pl.CostEstimate(flops=2 * 13 * 2**30, bytes_accessed=40 * 2**20, transcendentals=0),
    )(x, dyp, o, w, gain)
def line_events(nz):
    out = []
    for z in range(nz):
        events = [(z + nz - 1 - t, 0, t) for t in range(z + 1, nz)] + [(nz - 1 - z + t, 1, t) for t in range(z)]
        out.append([(way, t) for _, way, t in sorted(events)])
    return out


def at_place(z, rows):
    return pick(z, rows)


def finish_kernel(dims, cut, d_ref, wall_ref, a_hbm, x_hbm, dh_hbm, gain_ref, te_hbm, to_hbm, tl_hbm, ch_hbm, fg_ref, qgg_ref, kgg_ref, g_ref,
                  ig_ref, dwq_ref, dwz_ref, gains_ref,
                  a_ref, x_ref, dh_ref, te_ref, to_ref, tl_ref, ch_ref, pa, sib, ru, snd, rq, wq, rw, tw, hx, rx, rno, rn, fin, share, sc_, gx, gy,
                  la, lx, xs, xr, os, orr, bs, br, us, ur, qs, qr, vs, vr, ns, nr, cs, cr, hs, hr):
    fs, nc, nz = dims
    f, c, z = lax.axis_index("fsdp"), lax.axis_index("ctx"), lax.axis_index("tp")
    o = 1 - c
    me = f * nc + c
    rows, width = ig_ref.shape
    shard = dwq_ref.shape[1]
    early, late, final = early_parts(nz), late_parts(nz)[:-1], late_parts(nz)[-1]
    stages = fs.bit_length() - 1
    rest = pl.ds(cut, tw.shape[-1] - cut)
    others = [(df, dc) for df in range(fs) for dc in range(nc) if (df, dc) != (0, 0)]
    barrier = pltpu.get_barrier_semaphore()
    for df, dc in others:
        pl.semaphore_signal(barrier, inc=1, device_id={"fsdp": lax.rem(f + df, fs), "ctx": lax.rem(c + dc, nc)}, device_id_type=MESH)
    for dz in range(1, nz):
        pl.semaphore_signal(barrier, inc=1, device_id={"tp": lax.rem(z + dz, nz)}, device_id_type=MESH)
    pairs = ((to_hbm, to_ref), (tl_hbm, tl_ref), (te_hbm, te_ref), (ch_hbm, ch_ref), (x_hbm, x_ref), (dh_hbm, dh_ref), (a_hbm, a_ref))
    fills = [pltpu.make_async_copy(src, dst, la.at[i]) for i, (src, dst) in enumerate(pairs)]
    for cp in fills:
        cp.start()
    own = []
    for hi in range(2):
        for i, m in enumerate(reduce_masks(fs, hi)):
            own.append(pltpu.make_async_copy(g_ref.at[final, flip(f, m), hi], hx.at[hi, i], lx.at[hi, i]))
    for cp in own:
        cp.start()
    pl.semaphore_wait(barrier, len(others) + nz - 1)

    def last(hi):
        return first_copies(hi, fs, f, lambda g: g_ref.at[final, g, hi], lambda i: rx.at[hi, i], xs.at[hi], xr.at[hi])

    def later_rest(e, hi, stage):
        return later_copies(hi, stage, fs, f, lambda i: to_ref.at[e, hi, i], lambda i: rno.at[e, hi, i], os.at[e, hi], orr.at[e, hi])

    def later(j, hi, stage):
        held = (lambda i: tl_ref.at[j, hi, i]) if j < len(late) else (lambda i: hx.at[hi, i])
        return later_copies(hi, stage, fs, f, held, lambda i: rn.at[j, hi, i], ns.at[j, hi], nr.at[j, hi])

    def begin(copies):
        for cp in copies:
            cp.start()
    def reduce_last():
        for cp in own:
            cp.wait()
        for hi in range(2):
            for cp in last(hi):
                cp.wait_recv()
            hx[hi] = add_low(hx[hi], rx[hi])
            if stages > 1:
                begin(later(len(late), hi, 1))

    def reduce_more(copies, held, got, done):
        for stage in range(1, stages):
            keep = fs >> (stage + 1)
            base = fs // 2 - (fs >> stage)
            for cp in copies(stage):
                cp.wait_recv()
            if stage + 1 == stages:
                done(add_low(held[0], got[base]))
            else:
                held[:keep] = add_low(held[:keep], got[base:base + keep])
                begin(copies(stage + 1))
        if stages == 1:
            done(held[0])

    def put(t, hi, where):
        def done(value):
            tw[t, hi, :, where] = value
        return done

    def reduce_rest():
        for hi in range(2):
            for e in range(len(early)):
                reduce_more(lambda stage: later_rest(e, hi, stage), to_ref.at[e, hi], rno.at[e, hi], put(early[e], hi, rest))
            for j, t in enumerate(late + (final,)):
                held = tl_ref.at[j, hi] if j < len(late) else hx.at[hi]
                reduce_more(lambda stage: later(j, hi, stage), held, rn.at[j, hi], put(t, hi, slice(None)))

    def cross(t):
        return remote(snd.at[t], sib.at[t], bs.at[t], br.at[t], ctx=o)
    events = line_events(nz)

    def event(i):
        way = at_place(z, [events[zz][i][0] for zz in range(nz)])
        t = at_place(z, [events[zz][i][1] for zz in range(nz)])
        arrives = jnp.where(way == 0, z > 0, z < nz - 1)
        to = jnp.where(way == 0, jnp.minimum(z + 1, nz - 1), jnp.maximum(z - 1, 0))
        slot = jnp.where((way == 1) & (t == to), nz, t)
        return t, arrives, to, slot

    def rows_copy(i):
        t, _, to, slot = event(i)
        return remote(snd.at[t], ru.at[slot], us.at[i], ur.at[slot], tp=to)

    def rows_event(i):
        t, arrives, _, _ = event(i)
        cross(t).wait()

        @pl.when(arrives)
        def _():
            remote(snd.at[t], ru.at[t], us.at[i], ur.at[t], ctx=o).wait_recv()
            snd[t] = (pa[t] + sib[t].astype(F32) + ru[t].astype(F32)).astype(BF16)

        @pl.when(jnp.logical_not(arrives))
        def _():
            snd[t] = (pa[t] + sib[t].astype(F32)).astype(BF16)
        rows_copy(i).start()

    def weights(r):
        return pl.ds(pl.multiple_of(r * shard, shard), shard)

    def project(t):
        snd[t] = dot(d_ref[o * nz + t], wall_ref[...], NT).astype(BF16)
        cross(t).start()
        pa[t] = dot(d_ref[c * nz + t], wall_ref[...], NT)

    @pl.loop(0, nz)
    def _(i):
        t = z
        for k in range(nz - 1):
            t = jnp.where(i == k, event(k)[0], t)
        project(t)

        @pl.when(i == 0)
        def _():
            for cp in fills[:2]:
                cp.wait()
            for hi in range(2):
                begin(last(hi))
                if stages > 1:
                    for e in range(len(early)):
                        begin(later_rest(e, hi, 1))
                    for j in range(len(late)):
                        begin(later(j, hi, 1))

        @pl.when(i == min(2, nz - 1))
        def _():
            rows_event(0)
    for cp in fills[2:]:
        cp.wait()
    wq[...] = jnp.zeros_like(wq)

    @pl.loop(0, nc * nz)
    def _(s):
        wq[...] += dot(a_ref[s], d_ref[s], TN)
    rq[me] = wq[weights(me)].astype(BF16)
    for i, (df, dc) in enumerate(others):
        tf, tc = lax.rem(f + df, fs), lax.rem(c + dc, nc)
        sc_[i] = wq[weights(tf * nc + tc)].astype(BF16)
        remote(sc_.at[i], rq.at[me], qs.at[i], qr.at[me], fsdp=tf, ctx=tc).start()
    for e in range(len(early)):
        tw[early[e], :, :, :cut] = te_ref[e]

    @pl.when(z == 1)
    def _():
        rw[nz - 1, :, :, :cut] = ch_ref[...]

    @pl.when(z == nz - 2)
    def _():
        rw[0, :, :, :cut] = ch_ref[...]
    reduce_last()
    for i in range(1, nz - 1):
        rows_event(i)

    reduce_rest()
    firsts = ((z == 0), (z == nz - 1))

    def grads_copy(i, part=None):
        t, _, to, slot = event(i)
        src, dst = (tw.at[t], rw.at[slot]) if part is None else (tw.at[t, :, :, part], rw.at[slot, :, :, part])
        return remote(src, dst, vs.at[i], vr.at[slot], tp=to)

    def grads_came(i, t, part=None):
        src, dst = (tw.at[t], rw.at[t]) if part is None else (tw.at[t, :, :, part], rw.at[t, :, :, part])
        remote(src, dst, vs.at[i], vr.at[t], ctx=o).wait_recv()

    def leads(i):
        t = event(i)[0]
        return ((z == 0) & (t == nz - 1)) | ((z == nz - 1) & (t == 0))

    def follows(i):
        t = event(i)[0]
        return ((z == 1) & (t == nz - 1)) | ((z == nz - 2) & (t == 0))

    def grads_event(i):
        t, arrives, _, _ = event(i)

        @pl.when(arrives)
        def _():
            pl.when(follows(i))(lambda: grads_came(i, t, rest))
            pl.when(jnp.logical_not(follows(i)))(lambda: grads_came(i, t))
            tw[t] = add_low(tw[t], rw[t])
        pl.when(leads(i))(lambda: grads_copy(i, rest).start())
        pl.when(jnp.logical_not(leads(i)))(lambda: grads_copy(i).start())
    grads_event(0)

    def rows_arrival(way):
        slot = nz if way else z
        return remote(snd.at[0], ru.at[slot], us.at[0], ur.at[slot], ctx=o)

    cross(z).wait()
    pa[z] += sib[z].astype(F32)

    @pl.when(z > 0)
    def _():
        rows_arrival(0).wait_recv()
        pa[z] += ru[z].astype(F32)

    @pl.when(z < nz - 1)
    def _():
        rows_arrival(1).wait_recv()
        pa[z] += ru[nz].astype(F32)
    da = pa[z]
    x = x_ref[...].astype(F32)
    inv = lax.rsqrt(jnp.mean(x * x, axis=-1, keepdims=True) + EPS)
    n = x * inv
    sc = da * gain_ref[...]
    ig_ref[...] = dh_ref[...] + inv * (sc - n * jnp.mean(sc * n, axis=-1, keepdims=True))
    gx[z, 0:1] = jnp.sum(da * n, axis=0, keepdims=True)
    gx[z, 1:2] = fg_ref[...]
    gx[z, 2:3] = jnp.concatenate([qgg_ref[...], kgg_ref[...]] + [jnp.zeros((1, width - 2 * HEAD), F32)], axis=1)
    gx[z, 3:] = jnp.zeros_like(gx[z, 3:])
    for dz in range(1, nz):
        to = lax.rem(z + dz, nz)
        remote(gx.at[z], gx.at[z], hs.at[dz - 1], hr.at[z], tp=to).start()
    for i in range(1, nz - 1):
        grads_event(i)

    for i, (df, dc) in enumerate(others):
        src = lax.rem(f + df, fs) * nc + lax.rem(c + dc, nc)
        remote(sc_.at[0], rq.at[src], qs.at[i], qr.at[src], ctx=o).wait_recv()
    for cc in range(nc):
        total = rq[cc].astype(F32)
        for ff in range(1, fs):
            total += rq[ff * nc + cc].astype(F32)
        dwq_ref[cc] = total

    def grads_arrival(way):
        slot = nz if way else z
        return remote(tw.at[0], rw.at[slot], vs.at[0], vr.at[slot], ctx=o)

    for dz in range(1, nz):
        src = lax.rem(z + dz, nz)
        remote(gx.at[src], gx.at[src], hs.at[dz - 1], hr.at[src], tp=src).wait_recv()
    total = gx[0]
    for zz in range(1, nz):
        total += gx[zz]
    gy[me] = total
    for i, (df, dc) in enumerate(others):
        remote(gy.at[me], gy.at[me], hs.at[nz - 1 + i], hr.at[nz + me], fsdp=lax.rem(f + df, fs), ctx=lax.rem(c + dc, nc)).start()

    fin[...] = tw[z].astype(F32)

    @pl.when(z > 0)
    def _():
        grads_arrival(0).wait_recv()
        fin[...] += rw[z].astype(F32)

    @pl.when(z < nz - 1)
    def _():
        grads_arrival(1).wait_recv()
        fin[...] += rw[nz].astype(F32)
    share[0] = fin[o].astype(BF16)
    swap = remote(share.at[0], share.at[1], cs.at[0], cr.at[0], ctx=o)
    swap.start()
    dwz_ref[c] = fin[c]

    for i, (df, dc) in enumerate(others):
        src = lax.rem(f + df, fs) * nc + lax.rem(c + dc, nc)
        remote(gy.at[src], gy.at[src], hs.at[nz - 1 + i], hr.at[nz + src], ctx=o).wait_recv()
    total = gy[0]
    for r in range(1, fs * nc):
        total += gy[r]
    gains_ref[...] = total
    swap.wait_recv()
    dwz_ref[o] = share[1].astype(F32)

    swap.wait_send()
    for i in range(nz - 1):
        rows_copy(i).wait_send()
        pl.when(leads(i))(lambda: grads_copy(i, rest).wait_send())
        pl.when(jnp.logical_not(leads(i)))(lambda: grads_copy(i).wait_send())
    for i in range(nz - 1):
        remote(gx.at[0], gx.at[0], hs.at[i], hr.at[0], ctx=o).wait_send()
    for i in range(len(others)):
        remote(sc_.at[0], rq.at[0], qs.at[i], qr.at[0], ctx=o).wait_send()
        remote(gy.at[0], gy.at[0], hs.at[nz - 1 + i], hr.at[nz], ctx=o).wait_send()
    for hi in range(2):
        for cp in last(hi):
            cp.wait_send()
        for stage in range(1, stages):
            for e in range(len(early)):
                for cp in later_rest(e, hi, stage):
                    cp.wait_send()
            for j in range(len(late) + 1):
                for cp in later(j, hi, stage):
                    cp.wait_send()


def finish_call(dims, d, wall, a, x, dh, gain, te, to, tl, ch, fg, qgg, kgg, g):
    fs, nc, nz = dims
    rows, width = x.shape
    shard, cols = g.shape[3:]
    cut = te.shape[3]
    early = te.shape[0]
    half, more = fs // 2, max(fs // 2 - 1, 1)
    proj = wall.shape[1]
    late = len(late_parts(nz))
    n = fs * nc
    DMA = pltpu.SemaphoreType.DMA
    V = pltpu.VMEM
    return pl.pallas_call(
        lambda *refs: finish_kernel(dims, cut, *refs),
        out_shape=(
            jax.ShapeDtypeStruct((rows, width), F32),
            jax.ShapeDtypeStruct((nc, width // n, proj), F32),
            jax.ShapeDtypeStruct((nc, shard, cols), F32),
            jax.ShapeDtypeStruct((8, width), F32),
        ),
        in_specs=[VMEM_SPEC] * 2 + [ANY_SPEC] * 3 + [VMEM_SPEC] + [ANY_SPEC] * 4 + [VMEM_SPEC] * 3 + [ANY_SPEC],
        out_specs=(VMEM_SPEC,) * 4,
        scratch_shapes=[
            V(a.shape, BF16), V(x.shape, BF16), V(dh.shape, F32), V(te.shape, BF16), V(to.shape, BF16), V(tl.shape, BF16), V(ch.shape, BF16),
            V((nz, rows, width), F32), V((nz, rows, width), BF16), V((nz + 1, rows, width), BF16),
            V((nz, rows, width), BF16),
            V((n, width // n, proj), BF16), V((width, proj), F32),
            V((nz + 1, 2, shard, cols), BF16), V((nz, 2, shard, cols), BF16),
            V((2, half, shard, cols), BF16), V((2, half, shard, cols), BF16),
            V((early, 2, more, shard, cols - cut), BF16), V((late, 2, more, shard, cols), BF16),
            V((2, shard, cols), F32), V((2, shard, cols), BF16),
            V((n - 1, width // n, proj), BF16), V((nz, 8, width), F32), V((n, 8, width), F32),
            DMA((7,)), DMA((2, half)), DMA((2, half)), DMA((2, half)), DMA((early, 2, more)), DMA((early, 2, more)),
            DMA((nz,)), DMA((nz,)), DMA((nz - 1,)), DMA((nz + 1,)),
            DMA((n - 1,)), DMA((n,)), DMA((nz - 1,)), DMA((nz + 1,)),
            DMA((late, 2, max(fs // 2 - 1, 1))), DMA((late, 2, max(fs // 2 - 1, 1))),
            DMA((1,)), DMA((1,)), DMA((nz - 1 + n - 1,)), DMA((nz + n,)),
        ],
        compiler_params=pltpu.CompilerParams(collective_id=4, has_side_effects=True, vmem_limit_bytes=VMEM_LIMIT),
        cost_estimate=pl.CostEstimate(flops=2 * 4 * 2**30, bytes_accessed=40 * 2**20, transcendentals=0),
    )(d, wall, a, x, dh, gain, te, to, tl, ch, fg, qgg, kgg, g)
def unpack_kernel(parts, result_ref, ig_ref, gains_ref, dwq_ref, dwz_ref, *outs):
    outs[0][...] = result_ref[...]
    outs[1][...] = ig_ref[...]
    outs[2][...] = gains_ref[0:1]
    outs[3][...] = gains_ref[1:2]
    outs[4][...] = gains_ref[2:3, :HEAD]
    outs[5][...] = gains_ref[2:3, HEAD:2 * HEAD]
    for (which, at, step, turned), out in zip(parts, outs[6:]):
        ref = (dwq_ref, dwz_ref)[which]
        value = jnp.concatenate([ref[cc, :, at:at + step] for cc in range(ref.shape[0])], axis=1)
        out[...] = value.T if turned else value


def unpack_call(result, ig, gains, dwq, dwz, hidden, q_cols):
    nc, shard, _ = dwq.shape
    parts = ((0, 0, q_cols, False), (0, q_cols, HEAD, False), (0, q_cols + HEAD, HEAD, False),
             (1, 3 * hidden, q_cols, True), (1, 0, hidden, False), (1, hidden, hidden, False), (1, 2 * hidden, hidden, True))
    width = gains.shape[1]
    shapes = [(shard, nc * step)[::-1] if turned else (shard, nc * step) for _, _, step, turned in parts]
    return pl.pallas_call(
        lambda *refs: unpack_kernel(parts, *refs),
        out_shape=[jax.ShapeDtypeStruct(result.shape, BF16), jax.ShapeDtypeStruct(ig.shape, F32)]
        + [jax.ShapeDtypeStruct((1, n), F32) for n in (width, width, HEAD, HEAD)]
        + [jax.ShapeDtypeStruct(shape, F32) for shape in shapes],
        in_specs=[VMEM_SPEC] * 5,
        out_specs=[VMEM_SPEC] * 13,
        compiler_params=pltpu.CompilerParams(vmem_limit_bytes=VMEM_LIMIT),
    )(result, ig, gains, dwq, dwz)


def on_device(dims, tokens, out_grad, block_slot, attn_gain, ffn_gain, query_gain, key_norm_gain,
              w_query, key_weight, value_weight, w_out, w_gate, w_up, w_down):
    fs, nc, nz = dims
    rows, width = tokens.shape
    shard = w_query.shape[0]
    block_ids = block_slot[0]
    cos, sins = rope_tables()
    hidden, q_cols = w_gate.shape[1] // nc, w_query.shape[1] // nc
    ag, fg = attn_gain[None], ffn_gain[None]
    qg, kg = query_gain[None], key_norm_gain[None]
    weights = (w_query, key_weight, value_weight, w_gate, w_up, w_down, w_out)
    a, q, k, v, pre, wall, w, dyp = gather_call(dims, block_ids, tokens, out_grad, ag, weights, cos, sins, qg, kg)
    blocks = lambda t: t.reshape(BLOCKS, BLOCK, -1)
    q, k, v, pre = blocks(q), blocks(k), blocks(v), blocks(pre)
    w, mixed, o, logs = attend_call(dims, 2 * hidden, block_ids, q, k, v, w, rows)
    cols = w.shape[4]
    result, dh, ffn_part, do, dr, g, re = feed_call(dims, tokens, dyp, mixed, w.reshape(nz, width, cols), fg)
    g = g.reshape(nz, fs, nc, shard, cols)
    dr = dr.reshape(nz, nc, rows // UNIT, UNIT, q_cols - HEAD)
    d, te, to, tl, ch, q_part, k_part = attend_back_call(
        dims, block_ids, q, k, v, blocks(o), logs, blocks(do), pre, cos, sins, qg, kg, re, dr, g)
    input_grad, dwq, dwz, gains = finish_call(
        dims, d.reshape(nc * nz, rows, -1), wall.reshape(width, -1), a, tokens, dh, ag, te, to, tl, ch, ffn_part, q_part, k_part, g)
    outs = unpack_call(result, input_grad, gains, dwq, dwz, hidden, q_cols)
    return tuple(t[0] if 2 <= i < 6 else t for i, t in enumerate(outs))


def solution(mesh):
    dims = (mesh.shape["fsdp"], mesh.shape["ctx"], mesh.shape["tp"])
    everything, weights = ("fsdp", "ctx", "tp"), ("fsdp", "ctx")
    split, turned = P(weights, "tp"), P("tp", weights)
    return jax.shard_map(
        lambda *args: on_device(dims, *args),
        mesh=mesh,
        in_specs=(P(everything, None), P(everything, None), P("fsdp", None), P(), P(), P(), P(), split, split, split, turned, split, split, turned),
        out_specs=(P(everything, None), P(everything, None), P(), P(), P(), P(), split, split, split, turned, split, split, turned),
        check_vma=False,
    )
```

```python
import numpy as np
import jax
import jax.numpy as jnp
from jax import lax
from jax.experimental import pallas as pl
from jax.experimental.pallas import tpu as pltpu
from jax.sharding import PartitionSpec as P

HEAD = 128
BLOCK = 512
PBLOCKS = 4
BLOCKS = 6
EPS = 1e-6
ROPE_BASE = 1e6
MESH = pl.DeviceIdType.MESH
F32, BF16 = jnp.float32, jnp.bfloat16
LOG2E = 1.4426950408889634
QSCALE = HEAD ** -0.5 * LOG2E
VMEM_SPEC = pl.BlockSpec(memory_space=pltpu.VMEM)
ANY_SPEC = pl.BlockSpec(memory_space=pl.ANY)
SMEM_SPEC = pl.BlockSpec(memory_space=pltpu.SMEM)
VMEM_LIMIT = 60 * 2**20


def dot(a, b, dims):
    return lax.dot_general(a, b, (dims, ((), ())), preferred_element_type=F32)


NN = ((1,), (0,))
NT = ((1,), (1,))
TN = ((0,), (0,))


def flip(f, mask):
    bit = 1
    while bit <= mask:
        if mask & bit:
            f = f + bit - 2 * bit * lax.rem(lax.div(f, bit), 2)
        bit *= 2
    return f


def remote(src, dst, send, recv, **where):
    return pltpu.make_async_remote_copy(
        src_ref=src, dst_ref=dst, send_sem=send, recv_sem=recv,
        device_id=where, device_id_type=MESH)


def pick(index, values):
    out = jnp.int32(values[-1])
    for k in range(len(values) - 1):
        out = jnp.where(index == k, jnp.int32(values[k]), out)
    return out


def near_order(n):
    return [sorted(range(n), key=lambda s: (abs(s - z), s)) for z in range(n)]


def bit_orders(fs):
    bits = [1 << b for b in range(fs.bit_length() - 1)]
    return bits, bits[::-1]


def combos(bits):
    out = [0]
    for b in bits:
        out = out + [m + b for m in out]
    return out


def plane_copies(half, stage, fs, f, view, ssem, rsem):
    order = bit_orders(fs)[half]
    partner = flip(f, order[stage])
    base = (1 << stage) - 1
    out = []
    for m, mask in enumerate(combos(order[:stage])):
        g = flip(f, mask)
        out.append(remote(view(g), view(g), ssem.at[base + m], rsem.at[base + m], fsdp=partner))
    return out


UNIT = 128


def head_means(*values):
    ones = jnp.full((HEAD, HEAD), 1.0 / HEAD, BF16)
    return [dot(v.astype(BF16), ones, NN) for v in values]


def rope_tables():
    freqs = np.float32(ROPE_BASE) ** (-(np.arange(0, HEAD, 2, dtype=np.float32) / np.float32(HEAD)))
    places = np.arange((PBLOCKS + 1) * BLOCK, dtype=np.float32)
    angles = (places[:, None] * freqs[None, :].astype(np.float32)).astype(np.float64)
    cos, sin = np.cos(angles), np.sin(angles)
    shape = (-1, UNIT, HEAD)
    return (np.concatenate([cos, cos], axis=1).astype(np.float32).reshape(shape),
            np.concatenate([-sin, sin], axis=1).astype(np.float32).reshape(shape))


def rope_rows(table_ref, block_ref, first, count):
    per = BLOCK // UNIT
    out = []
    for i in range(count):
        unit = first + i
        out.append(table_ref[jnp.minimum(block_ref[lax.div(unit, per)], PBLOCKS) * per + lax.rem(unit, per)])
    return jnp.concatenate(out, axis=0)


def head_norm_rope(pre, gain, cos, sins):
    n = pre * lax.rsqrt(jnp.mean(pre * pre, axis=-1, keepdims=True) + EPS) * gain
    return n * cos + pltpu.roll(n, HEAD // 2, 1) * sins


def gather_kernel(dims, block_ref, x_ref, dy_ref, gain_ref, wq_in, wk_in, wv_in, wg_in, wu_in, wd_in, wo_in,
                  cos_ref, sin_ref, qg_ref, kg_ref,
                  a_out, q_out, k_out, v_out, pre_out, wall_ref, w_ref, dyp_ref,
                  a_ref, q_ref, k_ref, v_ref, pre_ref, out_sems, wqkv_ref, wz_ref, zs, zr, cs, cr, ws, wr, ms, mr, ps, pr, ls):
    fs, nc, nz = dims
    f, c, z = lax.axis_index("fsdp"), lax.axis_index("ctx"), lax.axis_index("tp")
    o = 1 - c
    me = f * nc + c
    others = [(df, dc) for df in range(fs) for dc in range(nc) if (df, dc) != (0, 0)]

    barrier = pltpu.get_barrier_semaphore()
    for df, dc in others:
        pl.semaphore_signal(barrier, inc=1, device_id={"fsdp": lax.rem(f + df, fs), "ctx": lax.rem(c + dc, nc)}, device_id_type=MESH)

    @pl.when(z > 0)
    def _():
        pl.semaphore_signal(barrier, inc=1, device_id={"tp": z - 1}, device_id_type=MESH)

    @pl.when(z < nz - 1)
    def _():
        pl.semaphore_signal(barrier, inc=1, device_id={"tp": z + 1}, device_id_type=MESH)
    x = x_ref[...].astype(F32)
    a_ref[c * nz + z] = (x * lax.rsqrt(jnp.mean(x * x, axis=-1, keepdims=True) + EPS) * gain_ref[...]).astype(BF16)
    pl.semaphore_wait(barrier, len(others) + jnp.where(z > 0, 1, 0) + jnp.where(z < nz - 1, 1, 0))

    row = a_ref.at[c * nz + z]
    up = remote(row, row, zs.at[z], zr.at[z], tp=jnp.minimum(z + 1, nz - 1))
    down = remote(row, row, zs.at[nz], zr.at[z], tp=jnp.maximum(z - 1, 0))
    pl.when(z < nz - 1)(up.start)
    pl.when(z > 0)(down.start)
    across = remote(row, row, cs.at[z], cr.at[z], ctx=o)
    across.start()
    dyc = remote(dy_ref, dyp_ref.at[c], ms.at[1], mr.at[1], ctx=o)
    dyc.start()
    dyp_ref[c] = dy_ref[...]

    def pack(packed, parts):
        at = 0
        for ref, turned in parts:
            value = ref[...].T if turned else ref[...]
            step = value.shape[1] // nc
            for cc in range(nc):
                packed[cc, :, at:at + step] = value[:, cc * step:(cc + 1) * step]
            at += step
    pack(wqkv_ref, ((wq_in, False), (wk_in, False), (wv_in, False)))
    wall_ref[me] = wqkv_ref[c]
    pack(wz_ref, ((wg_in, False), (wu_in, False), (wd_in, True), (wo_in, True)))
    own_w = pltpu.make_async_copy(wz_ref.at[c], w_ref.at[z, f, c], ls.at[0])
    own_w.start()
    for i, (df, dc) in enumerate(others):
        tf, tc = lax.rem(f + df, fs), lax.rem(c + dc, nc)
        remote(wqkv_ref.at[tc], wall_ref.at[me], ws.at[i], wr.at[me], fsdp=tf, ctx=tc).start()
    half = remote(wz_ref.at[o], w_ref.at[z, f, c], ms.at[0], mr.at[0], ctx=o)
    half.start()

    def plane(half_index, stage):
        return plane_copies(half_index, stage, fs, f, lambda g: w_ref.at[z, g, half_index], ps.at[half_index], pr.at[half_index])
    stages = fs.bit_length() - 1

    own_w.wait()
    remote(wz_ref.at[0], w_ref.at[z, f, o], ms.at[0], mr.at[0], ctx=o).wait_recv()
    for hi in range(2):
        for cp in plane(hi, 0):
            cp.start()
    q_cols = q_ref.shape[-1]

    def project(s):
        y = dot(a_ref[s], wall_ref[...].reshape(-1, wall_ref.shape[2]), NN)
        pre_ref[s] = y[:, :q_cols + HEAD].astype(BF16)
        units = a_ref.shape[1] // UNIT
        cos, sins = rope_rows(cos_ref, block_ref, s * units, units), rope_rows(sin_ref, block_ref, s * units, units)
        for h in range(q_cols // HEAD):
            q_ref[s, :, h * HEAD:(h + 1) * HEAD] = (head_norm_rope(y[:, h * HEAD:(h + 1) * HEAD], qg_ref[...], cos, sins) * QSCALE).astype(BF16)
        k_ref[s] = head_norm_rope(y[:, q_cols:q_cols + HEAD], kg_ref[...], cos, sins).astype(BF16)
        v_ref[s, :, :HEAD] = y[:, q_cols + HEAD:].astype(BF16)
        v_ref[s, :, HEAD:] = jnp.ones_like(v_ref[s, :, HEAD:])

    def take(hop):
        @pl.loop(0, 2 if hop == 0 else 4)
        def _(i):
            across_, way = (i, 0) if hop == 0 else (lax.rem(i, 2), lax.div(i, 2))
            src = z + (2 * way - 1) * hop

            @pl.when((src >= 0) & (src < nz))
            def _():
                s = jnp.where(across_ == 0, c, o) * nz + src

                @pl.when(across_ == 1)
                def _():
                    remote(a_ref.at[s], a_ref.at[s], cs.at[src], cr.at[src], ctx=o).wait_recv()
                project(s)
                for cp in results(s):
                    cp.start()

    def results(s):
        pairs = ((a_ref, a_out), (q_ref, q_out), (k_ref, k_out), (v_ref, v_out), (pre_ref, pre_out))
        return [pltpu.make_async_copy(src.at[s], dst.at[s], out_sems.at[i, s]) for i, (src, dst) in enumerate(pairs)]

    for hop in range(1, nz):
        for way in range(2):
            src = z + (2 * way - 1) * hop

            @pl.when((src >= 0) & (src < nz))
            def _():
                part = a_ref.at[c * nz + src]
                remote(part, part, zs.at[src], zr.at[src], ctx=o).wait_recv()
                if way == 0:
                    pl.when(z < nz - 1)(remote(part, part, zs.at[src], zr.at[src], tp=jnp.minimum(z + 1, nz - 1)).start)
                else:
                    pl.when(z > 0)(remote(part, part, zs.at[src], zr.at[src], tp=jnp.maximum(z - 1, 0)).start)
                remote(part, part, cs.at[src], cr.at[src], ctx=o).start()
        if hop == 1:
            for i, (df, dc) in enumerate(others):
                src = lax.rem(f + df, fs) * nc + lax.rem(c + dc, nc)
                remote(wqkv_ref.at[0], wall_ref.at[src], ws.at[i], wr.at[src], ctx=o).wait_recv()
        take(hop - 1)
        stage = hop - 1
        if stage < stages:
            for hi in range(2):
                for cp in plane(hi, stage):
                    cp.wait_recv()
                if stage + 1 < stages:
                    for cp in plane(hi, stage + 1):
                        cp.start()
    take(nz - 1)
    for stage in range(nz - 1, stages):
        for hi in range(2):
            for cp in plane(hi, stage):
                cp.wait_recv()
            if stage + 1 < stages:
                for cp in plane(hi, stage + 1):
                    cp.start()
    for s in range(nc * nz):
        for cp in results(s):
            cp.wait()
    for stage in range(stages):
        for hi in range(2):
            for cp in plane(hi, stage):
                cp.wait_send()
    for src in range(nz):
        @pl.when(((src <= z) & (z < nz - 1)) | ((src > z) & (z > 0)))
        def _():
            remote(row, row, zs.at[src], zr.at[src], ctx=o).wait_send()
        remote(row, row, cs.at[src], cr.at[src], ctx=o).wait_send()

    @pl.when(z > 0)
    def _():
        remote(row, row, zs.at[nz], zr.at[0], ctx=o).wait_send()
    for i in range(len(others)):
        remote(wqkv_ref.at[0], wall_ref.at[0], ws.at[i], wr.at[0], ctx=o).wait_send()
    half.wait_send()
    dyc.wait_send()
    remote(dy_ref, dyp_ref.at[o], ms.at[1], mr.at[1], ctx=o).wait_recv()


def gather_call(dims, block, x, dy, gain, weights, cos, sin, qg, kg):
    fs, nc, nz = dims
    rows, width = x.shape
    ns = nc * nz
    shard = weights[0].shape[0]
    q_cols = weights[0].shape[1] // nc
    cols = q_cols + 2 * HEAD
    wcols = 3 * (weights[3].shape[1] // nc) + q_cols
    DMA = pltpu.SemaphoreType.DMA
    return pl.pallas_call(
        lambda *refs: gather_kernel(dims, *refs),
        out_shape=(
            jax.ShapeDtypeStruct((ns, rows, width), BF16),
            jax.ShapeDtypeStruct((ns, rows, q_cols), BF16),
            jax.ShapeDtypeStruct((ns, rows, HEAD), BF16),
            jax.ShapeDtypeStruct((ns, rows, 2 * HEAD), BF16),
            jax.ShapeDtypeStruct((ns, rows, q_cols + HEAD), BF16),
            jax.ShapeDtypeStruct((fs * nc, shard, cols), BF16),
            jax.ShapeDtypeStruct((nz, fs, nc, shard, wcols), BF16),
            jax.ShapeDtypeStruct((nc, rows, width), BF16),
        ),
        in_specs=[SMEM_SPEC] + [VMEM_SPEC] * 14,
        out_specs=(ANY_SPEC,) * 5 + (VMEM_SPEC, ANY_SPEC, VMEM_SPEC),
        scratch_shapes=[
            pltpu.VMEM((ns, rows, width), BF16), pltpu.VMEM((ns, rows, q_cols), BF16), pltpu.VMEM((ns, rows, HEAD), BF16),
            pltpu.VMEM((ns, rows, 2 * HEAD), BF16), pltpu.VMEM((ns, rows, q_cols + HEAD), BF16), DMA((5, ns)),
            pltpu.VMEM((nc, shard, cols), BF16), pltpu.VMEM((nc, shard, wcols), BF16),
            DMA((nz + 1,)), DMA((nz,)), DMA((nz,)), DMA((nz,)),
            DMA((fs * nc - 1,)), DMA((fs * nc,)), DMA((2,)), DMA((2,)),
            DMA((2, fs - 1)), DMA((2, fs - 1)), DMA((2,)),
        ],
        compiler_params=pltpu.CompilerParams(collective_id=0, has_side_effects=True, vmem_limit_bytes=VMEM_LIMIT),
        cost_estimate=pl.CostEstimate(flops=2 * ns * rows * width * cols, bytes_accessed=30 * 2**20, transcendentals=0),
    )(block, x, dy, gain, *weights, cos, sin, qg, kg)
HALF = BLOCK // 2


def full_keys(qb):
    return min(qb, PBLOCKS)


def stack_heads(rows):
    return jnp.concatenate([rows[:, h * HEAD:(h + 1) * HEAD] for h in range(rows.shape[1] // HEAD)], axis=0)


def slot_of(block_ref, b):
    out = jnp.int32(0)
    for s in range(1, BLOCKS):
        out = jnp.where(block_ref[s] == b, jnp.int32(s), out)
    return out


def attend_kernel(dims, keep, block_ref, q_ref, k_ref, v_ref, wi_ref, w_ref, or_ref, o_ref, l_ref,
                  ob, zs, zr, ps, pr, xs, xr):
    fs, nc, nz = dims
    f, c, z = lax.axis_index("fsdp"), lax.axis_index("ctx"), lax.axis_index("tp")
    rows = or_ref.shape[2]
    barrier = pltpu.get_barrier_semaphore()
    bits = bit_orders(fs)[0]
    for bit in bits:
        pl.semaphore_signal(barrier, inc=1, device_id={"fsdp": flip(f, bit)}, device_id_type=MESH)
    for dz in range(1, nz):
        pl.semaphore_signal(barrier, inc=1, device_id={"tp": lax.rem(z + dz, nz)}, device_id_type=MESH)
    pl.semaphore_wait(barrier, len(bits) + nz - 1)

    def piece(ref, hop):
        return ref.at[:, :, pl.ds(keep, ref.shape[-1] - keep)] if hop == nz - 1 else ref

    def up(src, sem, hop):
        part = piece(w_ref.at[src, f], hop)
        return remote(part, part, zs.at[sem], zr.at[src], tp=jnp.minimum(z + 1, nz - 1))

    def down(src, sem, hop):
        part = piece(w_ref.at[src, f], hop)
        return remote(part, part, zs.at[sem], zr.at[src], tp=jnp.maximum(z - 1, 0))
    pl.when(z < nz - 1)(up(z, z, 1).start)
    pl.when(z > 0)(down(z, nz, 1).start)
    stages = fs.bit_length() - 1

    def plane(src, hi, stage, cut):
        def view(g):
            ref = w_ref.at[src, g, hi]
            return ref.at[:, pl.ds(keep, ref.shape[-1] - keep)] if cut else ref
        return plane_copies(hi, stage, fs, f, view, ps.at[src, hi], pr.at[src, hi])

    edge = (z == 0) | (z == nz - 1)

    def planes(hop, act):
        if hop == nz - 2:
            pl.when(edge)(lambda: act(False))
            pl.when(jnp.logical_not(edge))(lambda: act(True))
        else:
            act(hop == nz - 1)

    def each(hop, act):
        for way in range(2):
            src = z + (2 * way - 1) * hop

            @pl.when((src >= 0) & (src < nz))
            def _():
                act(way, src)

    def arrive(hop):
        def act(way, src):
            up(src, src, hop).wait_recv()
            if way == 0:
                pl.when(z < nz - 1)(up(src, src, hop + 1).start)
            else:
                pl.when(z > 0)(down(src, src, hop + 1).start)

            def go(cut):
                for hi in range(2):
                    for cp in plane(src, hi, 0, cut):
                        cp.start()
            planes(hop, go)
        each(hop, act)

    def spread(hop, stage):
        def act(way, src):
            def go(cut):
                for hi in range(2):
                    for cp in plane(src, hi, stage, cut):
                        cp.wait_recv()
                    if stage + 1 < stages:
                        for cp in plane(src, hi, stage + 1, cut):
                            cp.start()
            planes(hop, go)
        each(hop, act)

    tri = lax.broadcasted_iota(jnp.int32, (HALF, HALF), 0) >= lax.broadcasted_iota(jnp.int32, (HALF, HALF), 1)
    heads = q_ref.shape[2] // HEAD
    for qb in range(BLOCKS):
        if qb == BLOCKS - 1:
            arrive(1)
        q2 = stack_heads(q_ref[slot_of(block_ref, qb)])

        def step(kb, acc):
            k = k_ref[slot_of(block_ref, kb)]
            v = v_ref[slot_of(block_ref, kb)]
            return acc + dot(jnp.exp2(dot(q2, k, NT)).astype(BF16), v, NN)
        acc = jnp.zeros((heads * BLOCK, 2 * HEAD), F32)
        if full_keys(qb):
            acc = lax.fori_loop(0, full_keys(qb), step, acc)
        k = k_ref[slot_of(block_ref, qb)]
        v = v_ref[slot_of(block_ref, qb)]
        for h in range(heads):
            part = slice(h * BLOCK, (h + 1) * BLOCK)
            first = slice(h * BLOCK, h * BLOCK + HALF)
            second = slice(h * BLOCK + HALF, (h + 1) * BLOCK)
            p0 = jnp.where(tri, jnp.exp2(dot(q2[first], k[:HALF], NT)), 0.0).astype(BF16)
            p1 = jnp.exp2(dot(q2[second], k, NT))
            p1 = jnp.concatenate([p1[:, :HALF], jnp.where(tri, p1[:, HALF:], 0.0)], axis=1).astype(BF16)
            a = acc[part] + jnp.concatenate([dot(p0, v[:HALF], NN), dot(p1, v, NN)], axis=0)
            ob[qb, :, h * HEAD:(h + 1) * HEAD] = (a[:, :HEAD] / a[:, HEAD:]).astype(BF16)
            l_ref[qb, :, part] = jnp.log2(a[:, HEAD:]).T[0:8]
    for s in range(BLOCKS):
        o_ref[s * BLOCK:(s + 1) * BLOCK] = ob[block_ref[s]]

    def part_rows(side, zz):
        return pl.ds(pl.multiple_of((side * nz + zz) * rows, 128), rows)
    for hop in range(2, nz - 1):
        arrive(hop)
    for dz in range(1, nz):
        to = lax.rem(z + dz, nz)
        for side in range(nc):
            remote(o_ref.at[part_rows(side, to)], or_ref.at[z, side], xs.at[dz, side], xr.at[z, side], tp=to).start()
    for side in range(nc):
        or_ref[z, side] = o_ref[part_rows(side, z)]
    for hop in range(1, nz):
        for stage in range(stages):
            spread(hop, stage)
            if hop == nz - 2 and stage == 0:
                arrive(nz - 1)
    for dz in range(1, nz):
        src = lax.rem(z + dz, nz)
        for side in range(nc):
            cp = remote(o_ref.at[part_rows(side, 0)], or_ref.at[src, side], xs.at[dz, side], xr.at[src, side], tp=src)
            cp.wait_recv()
            cp.wait_send()
    for hop in range(1, nz):
        def left(way, src):
            if way == 0:
                pl.when(z < nz - 1)(up(src, src, hop + 1).wait_send)
            else:
                pl.when(z > 0)(down(src, src, hop + 1).wait_send)

            def go(cut):
                for hi in range(2):
                    for stage in range(stages):
                        for cp in plane(src, hi, stage, cut):
                            cp.wait_send()
            planes(hop, go)
        each(hop, left)
    pl.when(z < nz - 1)(up(z, z, 1).wait_send)
    pl.when(z > 0)(down(z, nz, 1).wait_send)


def attend_call(dims, keep, block, q, k, v, w, rows):
    fs, nc, nz = dims
    q_cols = q.shape[2]
    span = BLOCKS * BLOCK
    heads = q_cols // HEAD
    DMA = pltpu.SemaphoreType.DMA
    return pl.pallas_call(
        lambda *refs: attend_kernel(dims, keep, *refs),
        out_shape=(
            jax.ShapeDtypeStruct(w.shape, BF16),
            jax.ShapeDtypeStruct((nz, nc, rows, q_cols), BF16),
            jax.ShapeDtypeStruct((span, q_cols), BF16),
            jax.ShapeDtypeStruct((BLOCKS, 8, heads * BLOCK), F32),
        ),
        in_specs=[SMEM_SPEC] + [VMEM_SPEC] * 3 + [ANY_SPEC],
        out_specs=(ANY_SPEC, VMEM_SPEC, VMEM_SPEC, VMEM_SPEC),
        scratch_shapes=[
            pltpu.VMEM((BLOCKS, BLOCK, q_cols), BF16),
            DMA((nz + 1,)), DMA((nz,)), DMA((nz, 2, fs - 1)), DMA((nz, 2, fs - 1)), DMA((nz, nc)), DMA((nz, nc)),
        ],
        input_output_aliases={4: 0},
        compiler_params=pltpu.CompilerParams(collective_id=1, has_side_effects=True, vmem_limit_bytes=VMEM_LIMIT),
        cost_estimate=pl.CostEstimate(flops=2 * 20 * BLOCK * BLOCK * heads * 3 * HEAD, bytes_accessed=30 * 2**20, transcendentals=0),
    )(block, q, k, v, w)
def reduce_order(fs, hi):
    return bit_orders(fs)[hi][::-1]


def reduce_masks(fs, hi):
    return combos(reduce_order(fs, hi)[1:][::-1])


def first_copies(hi, fs, f, view, land, ssem, rsem):
    bit = reduce_order(fs, hi)[0]
    return [remote(view(flip(flip(f, m), bit)), land(i), ssem.at[i], rsem.at[i], fsdp=flip(f, bit))
            for i, m in enumerate(reduce_masks(fs, hi))]


def later_copies(hi, stage, fs, f, held, land, ssem, rsem):
    bit = reduce_order(fs, hi)[stage]
    keep = fs >> (stage + 1)
    base = fs // 2 - (fs >> stage)
    return [remote(held(keep + i), land(base + i), ssem.at[base + i], rsem.at[base + i], fsdp=flip(f, bit)) for i in range(keep)]


def add_low(a, b):
    return (a.astype(F32) + b.astype(F32)).astype(BF16)


def early_parts(nz):
    return (nz - 1, 0) if nz > 1 else (0,)


def late_parts(nz):
    return tuple(t for t in range(nz - 2, 0, -1))


def rope_norm_back(g, pre, gain, cos, sins):
    c = g * cos + pltpu.roll(g * sins, HEAD // 2, 1)
    sc = c * gain
    square, mixed = head_means(pre * pre, sc * pre)
    inv = lax.rsqrt(square + EPS)
    n = pre * inv
    return inv * (sc - n * (inv * mixed)), c * n


def attend_back_kernel(dims, cut, block_ref, q_ref, k_ref, v_ref, o_ref, l_ref, do_ref, pre_hbm, cos_hbm, sin_hbm,
                       qg_ref, kg_ref, re_ref, dr_ref, g_ref, d_ref, te_ref, to_ref, tl_ref, ch_ref, qgg_ref, kgg_ref,
                       pre_ref, cos_ref, sin_ref, lp, dr, dq, dk, dv, he, ho, hl, ro, rl, rn, le, lo, ll, os, orr, fss, fsr, nss, nsr, xs, xr, hs, hr):
    fs, nc, nz = dims
    f, z = lax.axis_index("fsdp"), lax.axis_index("tp")
    heads = q_ref.shape[2] // HEAD
    early, late = early_parts(nz), late_parts(nz)[:-1]
    stages = fs.bit_length() - 1
    rest = pl.ds(cut, g_ref.shape[-1] - cut)
    barrier = pltpu.get_barrier_semaphore()
    bits = bit_orders(fs)[0]
    for bit in bits:
        pl.semaphore_signal(barrier, inc=1, device_id={"fsdp": flip(f, bit)}, device_id_type=MESH)
    for dz in range(1, nz):
        pl.semaphore_signal(barrier, inc=1, device_id={"tp": lax.rem(z + dz, nz)}, device_id_type=MESH)
    tables = [pltpu.make_async_copy(src, dst, lp.at[i]) for i, (src, dst) in enumerate(((pre_hbm, pre_ref), (cos_hbm, cos_ref), (sin_hbm, sin_ref)))]
    own = []
    for hi in range(2):
        for i, m in enumerate(reduce_masks(fs, hi)):
            for e, t in enumerate(early):
                own.append(pltpu.make_async_copy(g_ref.at[t, flip(f, m), hi, :, pl.ds(0, cut)], he.at[e, hi, i], le.at[e, hi, i]))
                own.append(pltpu.make_async_copy(g_ref.at[t, flip(f, m), hi, :, rest], ho.at[e, hi, i], lo.at[e, hi, i]))
            for j, t in enumerate(late):
                own.append(pltpu.make_async_copy(g_ref.at[t, flip(f, m), hi], hl.at[j, hi, i], ll.at[j, hi, i]))
    for cp in own + tables:
        cp.start()
    pl.semaphore_wait(barrier, len(bits) + nz - 1)

    units = dr_ref.shape[2]
    def spot(side, zz):
        return pl.ds((side * nz + zz) * units, units)
    for dz in range(1, nz):
        to = lax.rem(z + dz, nz)
        for side in range(nc):
            remote(dr_ref.at[to, side], dr.at[spot(side, z)], xs.at[dz, side], xr.at[z, side], tp=to).start()
    keep_own = [pltpu.make_async_copy(dr_ref.at[z, side], dr.at[spot(side, z)], lp.at[3 + side]) for side in range(nc)]
    for cp in keep_own:
        cp.start()

    def first_rest(e, hi):
        return first_copies(hi, fs, f, lambda g: g_ref.at[early[e], g, hi, :, rest], lambda i: ro.at[e, hi, i], os.at[e, hi], orr.at[e, hi])

    def first_late(j, hi):
        return first_copies(hi, fs, f, lambda g: g_ref.at[late[j], g, hi], lambda i: rl.at[j, hi, i], fss.at[j, hi], fsr.at[j, hi])

    def later(e, hi, stage):
        return later_copies(hi, stage, fs, f, lambda i: he.at[e, hi, i], lambda i: rn.at[e, hi, i], nss.at[e, hi], nsr.at[e, hi])
    for cp in own:
        cp.wait()
    for e in range(len(early)):
        for hi in range(2):
            he[e, hi] = add_low(he[e, hi], re_ref[e, hi])
            if stages > 1:
                for cp in later(e, hi, 1):
                    cp.start()

    def hop(e):
        return remote(te_ref.at[e], ch_ref, hs.at[e], hr.at[0], tp=jnp.minimum(z + 1, nz - 1) if e == 0 else jnp.maximum(z - 1, 0))

    def finish_early():
        for stage in range(1, stages):
            keep = fs >> (stage + 1)
            base = fs // 2 - (fs >> stage)
            for e in range(len(early)):
                for hi in range(2):
                    for cp in later(e, hi, stage):
                        cp.wait_recv()
                    he[e, hi, :keep] = add_low(he[e, hi, :keep], rn[e, hi, base:base + keep])
                    if stage + 1 < stages:
                        for cp in later(e, hi, stage + 1):
                            cp.start()
        for e in range(len(early)):
            te_ref[e] = he[e, :, 0]
        pl.when(z == 0)(hop(0).start)
        pl.when(z == nz - 1)(hop(1).start)
        for e in range(len(early)):
            for hi in range(2):
                for cp in first_rest(e, hi):
                    cp.start()
        for j in range(len(late)):
            for hi in range(2):
                for cp in first_late(j, hi):
                    cp.start()

    tri = lax.broadcasted_iota(jnp.int32, (HALF, HALF), 0) <= lax.broadcasted_iota(jnp.int32, (HALF, HALF), 1)
    dk[...] = jnp.zeros_like(dk)
    dv[...] = jnp.zeros_like(dv)
    per = BLOCK // UNIT
    for h in range(heads):
        cols, logs = slice(h * HEAD, (h + 1) * HEAD), slice(h * BLOCK, (h + 1) * BLOCK)
        if h == 1:
            for cp in keep_own:
                cp.wait()
            for dz in range(1, nz):
                src = lax.rem(z + dz, nz)
                for side in range(nc):
                    remote(dr_ref.at[0, side], dr.at[spot(side, src)], xs.at[dz, side], xr.at[src, side], tp=src).wait_recv()
        for qb in range(BLOCKS):
            if h == 0 and qb == BLOCKS - 1:
                finish_early()
            at = slot_of(block_ref, qb)
            q = q_ref[at, :, cols]
            if h == 0:
                g = do_ref[at]
            else:
                g = jnp.concatenate([dr[at * per + i, :, (h - 1) * HEAD:h * HEAD] for i in range(per)], axis=0)
            delta = jnp.sum((g.astype(F32) * o_ref[at, :, cols].astype(F32)).T, axis=0, keepdims=True)
            log = l_ref[qb, 0:1, logs]

            def pair(kb, keys, start):
                k = k_ref[slot_of(block_ref, kb), keys]
                v = v_ref[slot_of(block_ref, kb), keys, :HEAD]
                qs, gs = q[start:], g[start:]
                p = jnp.exp2(dot(k, qs, NT) - log[:, start:])
                if diagonal:
                    width = k.shape[0]
                    p0 = jnp.where(tri, p[:, :width], 0.0)
                    p = p0 if p.shape[1] == width else jnp.concatenate([p0, p[:, width:]], axis=1)
                ds = (p * (dot(v, gs, NT) - delta[:, start:])).astype(BF16)
                dv[kb, keys] += dot(p.astype(BF16), gs, NN)
                dk[kb, keys] += dot(ds, qs, NN)
                return dot(k.T, ds, NN)
            diagonal = True
            low = pair(qb, slice(0, HALF), 0)
            high = pair(qb, slice(HALF, BLOCK), HALF)
            total = jnp.concatenate([low[:, :HALF], low[:, HALF:] + high], axis=1)
            diagonal = False
            for kb in range(full_keys(qb)):
                total = total + pair(kb, slice(0, BLOCK), 0)
            dq[qb, logs] = total.T

    for cp in tables:
        cp.wait()
    qgg_ref[...] = jnp.zeros_like(qgg_ref)
    kgg_ref[...] = jnp.zeros_like(kgg_ref)

    @pl.loop(0, BLOCKS)
    def _(s):
        b = block_ref[s]
        cos, sins = rope_rows(cos_ref, block_ref, s * per, per), rope_rows(sin_ref, block_ref, s * per, per)
        qs = dq[b]
        for h in range(heads):
            back, part = rope_norm_back(qs[h * BLOCK:(h + 1) * BLOCK] * HEAD ** -0.5, pre_ref[s, :, h * HEAD:(h + 1) * HEAD].astype(F32), qg_ref[...], cos, sins)
            d_ref[s, :, h * HEAD:(h + 1) * HEAD] = back.astype(BF16)
            qgg_ref[...] += jnp.sum(part, axis=0, keepdims=True)
        back, part = rope_norm_back(dk[b] * (1.0 / LOG2E), pre_ref[s, :, heads * HEAD:].astype(F32), kg_ref[...], cos, sins)
        d_ref[s, :, heads * HEAD:(heads + 1) * HEAD] = back.astype(BF16)
        kgg_ref[...] += jnp.sum(part, axis=0, keepdims=True)
        d_ref[s, :, (heads + 1) * HEAD:] = dv[b].astype(BF16)

    for e in range(len(early)):
        for hi in range(2):
            for cp in first_rest(e, hi):
                cp.wait_recv()
            to_ref[e, hi] = add_low(ho[e, hi], ro[e, hi])
    for j in range(len(late)):
        for hi in range(2):
            for cp in first_late(j, hi):
                cp.wait_recv()
            tl_ref[j, hi] = add_low(hl[j, hi], rl[j, hi])
    pl.when((z == 1) | (z == nz - 2))(hop(0).wait_recv)
    pl.when(z == 0)(hop(0).wait_send)
    pl.when(z == nz - 1)(hop(1).wait_send)
    for dz in range(1, nz):
        for side in range(nc):
            remote(dr_ref.at[0, side], dr.at[spot(side, 0)], xs.at[dz, side], xr.at[0, side], tp=lax.rem(z + dz, nz)).wait_send()
    for hi in range(2):
        for j in range(len(late)):
            for cp in first_late(j, hi):
                cp.wait_send()
        for e in range(len(early)):
            for cp in first_rest(e, hi):
                cp.wait_send()
            for stage in range(1, stages):
                for cp in later(e, hi, stage):
                    cp.wait_send()


def attend_back_call(dims, block, q, k, v, o, l, do, pre, cos, sin, qg, kg, re, dr, g):
    fs, nc, nz = dims
    q_cols = q.shape[2]
    heads = q_cols // HEAD
    early, late = len(early_parts(nz)), len(late_parts(nz)) - 1
    shard, cols = g.shape[3:]
    cut = re.shape[4]
    half, more = fs // 2, max(fs // 2 - 1, 1)
    DMA = pltpu.SemaphoreType.DMA
    V = pltpu.VMEM
    return pl.pallas_call(
        lambda *refs: attend_back_kernel(dims, cut, *refs),
        out_shape=(
            jax.ShapeDtypeStruct((BLOCKS, BLOCK, q_cols + 2 * HEAD), BF16),
            jax.ShapeDtypeStruct((early, 2, shard, cut), BF16),
            jax.ShapeDtypeStruct((early, 2, half, shard, cols - cut), BF16),
            jax.ShapeDtypeStruct((late, 2, half, shard, cols), BF16),
            jax.ShapeDtypeStruct((2, shard, cut), BF16),
            jax.ShapeDtypeStruct((1, HEAD), F32),
            jax.ShapeDtypeStruct((1, HEAD), F32),
        ),
        in_specs=[SMEM_SPEC] + [VMEM_SPEC] * 6 + [ANY_SPEC] * 3 + [VMEM_SPEC] * 3 + [ANY_SPEC] * 2,
        out_specs=(VMEM_SPEC,) * 7,
        scratch_shapes=[
            V(pre.shape, BF16), V(cos.shape, F32), V(sin.shape, F32), DMA((3 + nc,)),
            V((BLOCKS * BLOCK // UNIT, UNIT, q_cols - HEAD), BF16),
            V((BLOCKS, heads * BLOCK, HEAD), F32), V((BLOCKS, BLOCK, HEAD), F32), V((BLOCKS, BLOCK, HEAD), F32),
            V((early, 2, half, shard, cut), BF16), V((early, 2, half, shard, cols - cut), BF16), V((late, 2, half, shard, cols), BF16),
            V((early, 2, half, shard, cols - cut), BF16), V((late, 2, half, shard, cols), BF16), V((early, 2, more, shard, cut), BF16),
            DMA((early, 2, half)), DMA((early, 2, half)), DMA((late, 2, half)),
            DMA((early, 2, half)), DMA((early, 2, half)), DMA((late, 2, half)), DMA((late, 2, half)),
            DMA((early, 2, more)), DMA((early, 2, more)), DMA((nz, nc)), DMA((nz, nc)), DMA((2,)), DMA((1,)),
        ],
        compiler_params=pltpu.CompilerParams(collective_id=3, has_side_effects=True, vmem_limit_bytes=VMEM_LIMIT),
        cost_estimate=pl.CostEstimate(flops=2 * 20 * BLOCK * BLOCK * heads * 5 * HEAD, bytes_accessed=40 * 2**20, transcendentals=0),
    )(block, q, k, v, o, l, do, pre, cos, sin, qg, kg, re, dr, g)
def column_parts(dims, hidden, q_cols):
    return (0, hidden, 2 * hidden, 3 * hidden, 3 * hidden + q_cols)


def feed_kernel(dims, x_ref, dy_ref, o_ref, w_ref, gain_ref, out_ref, dh_ref, fg_ref, do_ref, dr_ref, g_ref, re_ref,
                wb, ge, hs, b_ref, da_ref, dgu, u_ref, acc, snd, rcv, dos, bt, yt, at,
                ls, gs, ss, sr, xs, xr, fss, fsr, os, orr, ps, pr, lq):
    fs, nc, nz = dims
    f, c, z = lax.axis_index("fsdp"), lax.axis_index("ctx"), lax.axis_index("tp")
    o = 1 - c
    rows, width = x_ref.shape
    q_cols = o_ref.shape[3]
    hidden = (w_ref.shape[2] - q_cols) // 3
    gate, up_, down_, out_, end = column_parts(dims, hidden, q_cols)
    edge = (z == 0) | (z == nz - 1)
    low = z < nz // 2
    last = jnp.where(low, nz - 1, 0)
    keep = down_

    def load_out(zz):
        part = pl.ds(out_, end - out_)
        return pltpu.make_async_copy(w_ref.at[zz, :, part], wb.at[zz, :, part], ls.at[0, zz])

    def loads(act):
        for zz in range(nz):
            here = last == zz
            for late in range(2):
                part = pl.ds(keep if late else 0, out_ - (keep if late else 0))

                @pl.when(here if late else jnp.logical_not(here))
                def _():
                    act(pltpu.make_async_copy(w_ref.at[zz, :, part], wb.at[zz, :, part], ls.at[1, zz]))
    for zz in range(nz):
        load_out(zz).start()
    loads(lambda cp: cp.start())
    barrier = pltpu.get_barrier_semaphore()
    pl.semaphore_signal(barrier, inc=1, device_id={"ctx": o}, device_id_type=MESH)
    for dz in range(1, nz):
        pl.semaphore_signal(barrier, inc=1, device_id={"tp": lax.rem(z + dz, nz)}, device_id_type=MESH)
    bits = bit_orders(fs)[0]
    stages = len(bits)
    for bit in bits:
        pl.semaphore_signal(barrier, inc=1, device_id={"fsdp": flip(f, bit)}, device_id_type=MESH)
    pl.semaphore_wait(barrier, nz + len(bits))
    early = early_parts(nz)
    shard = width // (fs * nc)

    def shard_rows(g, hi, n=1):
        return pl.ds(pl.multiple_of((g * nc + hi) * shard, shard), n * shard)

    def chunk(k):
        return pl.ds(k * (keep // 2), keep // 2)

    def outward(way, k):
        part = 0 if way == 0 else nz - 1
        to = jnp.minimum(z + 1, nz - 1) if way == 0 else jnp.maximum(z - 1, 0)
        ref = shard_rows(f, 0, nc)
        return remote(w_ref.at[part, ref, chunk(k)], wb.at[part, ref, chunk(k)], os.at[way, k], orr.at[k], tp=to)

    def out_copies(act):
        for k in range(2):
            pl.when(z == nz - 2)(lambda: act(outward(0, k)))
            pl.when(z == 1)(lambda: act(outward(1, k)))
    out_copies(lambda cp: cp.start())

    def own_part(k):
        ref = shard_rows(f, 0, nc)
        return pltpu.make_async_copy(w_ref.at[last, ref, chunk(k)], wb.at[last, ref, chunk(k)], lq.at[k])

    @pl.when(jnp.logical_not(edge))
    def _():
        for k in range(2):
            own_part(k).start()

    def late_plane(hi, stage, k):
        return plane_copies(hi, stage, fs, f, lambda g: wb.at[last, shard_rows(g, hi), chunk(k)], ps.at[hi, k], pr.at[hi, k])

    def late_arrive(k):
        @pl.when(edge)
        def _():
            ref = shard_rows(f, 0, nc)
            remote(w_ref.at[0, ref, chunk(k)], wb.at[last, ref, chunk(k)], os.at[0, k], orr.at[k], ctx=o).wait_recv()

        @pl.when(jnp.logical_not(edge))
        def _():
            own_part(k).wait()
        for hi in range(2):
            for cp in late_plane(hi, 0, k):
                cp.start()

    def late_spread(stage, k):
        for hi in range(2):
            for cp in late_plane(hi, stage, k):
                cp.wait_recv()
            if stage + 1 < stages:
                for cp in late_plane(hi, stage + 1, k):
                    cp.start()

    def first(e, hi):
        def view(g):
            return ge.at[e, shard_rows(g, hi)]
        return first_copies(hi, fs, f, view, lambda i: re_ref.at[e, hi, i], fss.at[e, hi], fsr.at[e, hi])

    def cross(i, src, dst):
        return remote(src, dst, ss.at[i], sr.at[i], ctx=o)
    for zz in range(nz):
        load_out(zz).wait()

    def project(side):
        total = dot(o_ref[0, side], wb[0, :, out_:end], NT)
        for zz in range(1, nz):
            total += dot(o_ref[zz, side], wb[zz, :, out_:end], NT)
        return total
    snd[0] = project(o).astype(BF16)
    cross(0, snd.at[0], rcv.at[0]).start()
    own = project(c)
    loads(lambda cp: cp.wait())

    @pl.loop(0, nz)
    def _(zz):
        dgu[zz, :, :hidden] = dot(dy_ref[...].reshape(nc * rows, width), wb[zz, :, down_:out_], NN).astype(BF16)
    late_arrive(0)
    cross(0, snd.at[0], rcv.at[0]).wait_recv()
    h = x_ref[...].astype(F32) + own + rcv[0].astype(F32)
    hs[...] = h
    b_ref[c] = (h * lax.rsqrt(jnp.mean(h * h, axis=-1, keepdims=True) + EPS) * gain_ref[...]).astype(BF16)
    cross(1, b_ref.at[c], b_ref.at[c]).start()
    yt[...] = dy_ref[...].reshape(nc * rows, width).T
    late_spread(0, 0)
    late_arrive(1)
    cross(1, b_ref.at[c], b_ref.at[o]).wait_recv()

    @pl.loop(0, nz)
    def _(i):
        zz = jnp.where(low, i, nz - 1 - i)

        @pl.when(i == 1)
        def _():
            late_spread(0, 1)

        @pl.when(i == nz - 1)
        def _():
            for stage in range(1, stages):
                for k in range(2):
                    late_spread(stage, k)
        both = b_ref[...].reshape(nc * rows, width)
        gu = dot(both, wb[zz, :, gate:down_], NN)
        du = dgu[zz, :, :hidden].astype(F32)
        gt, uv = gu[:, :hidden], gu[:, hidden:]
        sig = 1.0 / (1.0 + jnp.exp(-gt))
        silu = gt * sig
        hid = (silu * uv).astype(BF16)
        u_ref[zz] = hid
        dgu[zz, :, :hidden] = (du * uv * sig * (1.0 + gt * (1.0 - sig))).astype(BF16)
        dgu[zz, :, hidden:] = (du * silu).astype(BF16)

    def side_rows(side):
        return pl.ds(pl.multiple_of(side * rows, 128), rows)

    def feed_sum(side, left, start, stop):
        total = dot(left[0, side_rows(side)], wb[0, :, start:stop], NT)
        for zz in range(1, nz):
            total += dot(left[zz, side_rows(side)], wb[zz, :, start:stop], NT)
        return total
    snd[1] = feed_sum(o, dgu, gate, down_).astype(BF16)
    cross(2, snd.at[1], rcv.at[1]).start()
    acc[...] = feed_sum(c, dgu, gate, down_)
    bt[...] = b_ref[...].reshape(nc * rows, width).T

    def feed_grads(zz, into):
        into[:, gate:down_] = dot(bt[...], dgu[zz], NN).astype(BF16)
        into[:, down_:out_] = dot(yt[...], u_ref[zz], NN).astype(BF16)

    def early_grads(e):
        feed_grads(early[e], ge.at[e])
        for hi in range(2):
            for cp in first(e, hi):
                cp.start()
    early_grads(0)
    cross(2, snd.at[1], rcv.at[1]).wait_recv()
    db = acc[...] + rcv[1].astype(F32)
    h = hs[...]
    inv = lax.rsqrt(jnp.mean(h * h, axis=-1, keepdims=True) + EPS)
    n = h * inv
    sc = db * gain_ref[...]
    dh = dy_ref[c].astype(F32) + inv * (sc - n * jnp.mean(sc * n, axis=-1, keepdims=True))
    fg_ref[...] = jnp.sum(db * n, axis=0, keepdims=True)
    dh_ref[...] = dh
    da_ref[c] = dh.astype(BF16)
    cross(4, da_ref.at[c], da_ref.at[c]).start()
    for e in range(1, len(early)):
        early_grads(e)
    snd[2] = feed_sum(o, u_ref, down_, out_).astype(BF16)
    cross(3, snd.at[2], rcv.at[2]).start()
    acc[...] = feed_sum(c, u_ref, down_, out_)
    cross(4, da_ref.at[c], da_ref.at[o]).wait_recv()

    def stores(zz):
        if zz not in early:
            return [pltpu.make_async_copy(wb.at[zz], g_ref.at[zz], gs.at[0, zz])]
        lead, tail = pl.ds(0, out_), pl.ds(out_, end - out_)
        return [pltpu.make_async_copy(ge.at[early.index(zz)], g_ref.at[zz, :, lead], gs.at[0, zz]),
                pltpu.make_async_copy(wb.at[zz, :, tail], g_ref.at[zz, :, tail], gs.at[1, zz])]

    @pl.loop(1, nz + 1)
    def _(dz):
        to = lax.rem(z + dz, nz)
        both = dot(da_ref[...].reshape(nc * rows, width), wb[to, :, out_:end], NN).astype(BF16).reshape(nc, rows, q_cols)
        dos[to] = both[:, :, :HEAD]
        dr_ref[to] = both[:, :, HEAD:]

        @pl.when(dz < nz)
        def _():
            for side in range(nc):
                remote(dos.at[to, side], do_ref.at[side, z], xs.at[dz, side], xr.at[z, side], tp=to).start()
    for side in range(nc):
        do_ref[side, z] = dos[z, side]
    cross(3, snd.at[2], rcv.at[2]).wait_recv()
    out_ref[...] = (hs[...] + acc[...] + rcv[2].astype(F32)).astype(BF16)
    at[...] = da_ref[...].reshape(nc * rows, width).T
    for zz in early + late_parts(nz):
        wb[zz, :, out_:end] = dot(at[...], o_ref[zz].reshape(nc * rows, q_cols), NN).astype(BF16)
        if zz not in early:
            feed_grads(zz, wb.at[zz])
        for cp in stores(zz):
            cp.start()
    for zz in range(nz):
        for cp in stores(zz):
            cp.wait()

    for hi in range(2):
        for stage in range(stages):
            for k in range(2):
                for cp in late_plane(hi, stage, k):
                    cp.wait_send()
    for dz in range(1, nz):
        src = lax.rem(z + dz, nz)
        for side in range(nc):
            cp = remote(dos.at[0, side], do_ref.at[side, src], xs.at[dz, side], xr.at[src, side], tp=src)
            cp.wait_recv()
            cp.wait_send()
    out_copies(lambda cp: cp.wait_send())
    for e in range(len(early)):
        for hi in range(2):
            for cp in first(e, hi):
                cp.wait_recv()
                cp.wait_send()
    for i, part in enumerate((snd.at[0], b_ref.at[c], snd.at[1], snd.at[2], da_ref.at[c])):
        cross(i, part, part).wait_send()


def feed_call(dims, x, dyp, o, w, gain):
    fs, nc, nz = dims
    rows, width = x.shape
    q_cols = o.shape[3]
    cols = w.shape[2]
    hidden = (cols - q_cols) // 3
    early = len(early_parts(nz))
    DMA = pltpu.SemaphoreType.DMA
    V = pltpu.VMEM
    return pl.pallas_call(
        lambda *refs: feed_kernel(dims, *refs),
        out_shape=(
            jax.ShapeDtypeStruct((rows, width), BF16),
            jax.ShapeDtypeStruct((rows, width), F32),
            jax.ShapeDtypeStruct((1, width), F32),
            jax.ShapeDtypeStruct((nc, nz, rows, HEAD), BF16),
            jax.ShapeDtypeStruct((nz, nc, rows, q_cols - HEAD), BF16),
            jax.ShapeDtypeStruct(w.shape, BF16),
            jax.ShapeDtypeStruct((early, 2, fs // 2, width // (fs * nc), 3 * hidden), BF16),
        ),
        in_specs=[VMEM_SPEC] * 3 + [ANY_SPEC, VMEM_SPEC],
        out_specs=(VMEM_SPEC,) * 5 + (ANY_SPEC, ANY_SPEC),
        scratch_shapes=[
            V(w.shape, BF16), V((early, width, 3 * hidden), BF16), V((rows, width), F32), V((nc, rows, width), BF16), V((nc, rows, width), BF16),
            V((nz, nc * rows, 2 * hidden), BF16), V((nz, nc * rows, hidden), BF16),
            V((rows, width), F32),
            V((3, rows, width), BF16), V((3, rows, width), BF16), V((nz, nc, rows, HEAD), BF16),
            V((width, nc * rows), BF16), V((width, nc * rows), BF16), V((width, nc * rows), BF16),
            DMA((2, nz)), DMA((2, nz)), DMA((5,)), DMA((5,)), DMA((nz, nc)), DMA((nz, nc)),
            DMA((early, 2, fs // 2)), DMA((early, 2, fs // 2)),
            DMA((2, 2)), DMA((2,)), DMA((2, 2, fs - 1)), DMA((2, 2, fs - 1)), DMA((2,)),
        ],
        compiler_params=pltpu.CompilerParams(collective_id=2, has_side_effects=True, vmem_limit_bytes=VMEM_LIMIT),
        cost_estimate=pl.CostEstimate(flops=2 * 13 * 2**30, bytes_accessed=40 * 2**20, transcendentals=0),
    )(x, dyp, o, w, gain)
def line_events(nz):
    out = []
    for z in range(nz):
        events = [(z + nz - 1 - t, 0, t) for t in range(z + 1, nz)] + [(nz - 1 - z + t, 1, t) for t in range(z)]
        out.append([(way, t) for _, way, t in sorted(events)])
    return out


def at_place(z, rows):
    return pick(z, rows)


def finish_kernel(dims, cut, d_ref, wall_ref, a_hbm, x_hbm, dh_hbm, gain_ref, te_hbm, to_hbm, tl_hbm, ch_hbm, fg_ref, qgg_ref, kgg_ref, g_ref,
                  ig_ref, dwq_ref, dwz_ref, gains_ref,
                  a_ref, x_ref, dh_ref, te_ref, to_ref, tl_ref, ch_ref, pa, sib, ru, snd, rq, wq, rw, tw, hx, rx, rno, rn, fin, share, sc_, gx, gy,
                  la, lx, xs, xr, os, orr, bs, br, us, ur, qs, qr, vs, vr, ns, nr, cs, cr, hs, hr):
    fs, nc, nz = dims
    f, c, z = lax.axis_index("fsdp"), lax.axis_index("ctx"), lax.axis_index("tp")
    o = 1 - c
    me = f * nc + c
    rows, width = ig_ref.shape
    shard = dwq_ref.shape[1]
    early, late, final = early_parts(nz), late_parts(nz)[:-1], late_parts(nz)[-1]
    stages = fs.bit_length() - 1
    rest = pl.ds(cut, tw.shape[-1] - cut)
    others = [(df, dc) for df in range(fs) for dc in range(nc) if (df, dc) != (0, 0)]
    barrier = pltpu.get_barrier_semaphore()
    for df, dc in others:
        pl.semaphore_signal(barrier, inc=1, device_id={"fsdp": lax.rem(f + df, fs), "ctx": lax.rem(c + dc, nc)}, device_id_type=MESH)
    for dz in range(1, nz):
        pl.semaphore_signal(barrier, inc=1, device_id={"tp": lax.rem(z + dz, nz)}, device_id_type=MESH)
    pairs = ((to_hbm, to_ref), (tl_hbm, tl_ref), (te_hbm, te_ref), (ch_hbm, ch_ref), (x_hbm, x_ref), (dh_hbm, dh_ref), (a_hbm, a_ref))
    fills = [pltpu.make_async_copy(src, dst, la.at[i]) for i, (src, dst) in enumerate(pairs)]
    for cp in fills:
        cp.start()
    own = []
    for hi in range(2):
        for i, m in enumerate(reduce_masks(fs, hi)):
            own.append(pltpu.make_async_copy(g_ref.at[final, flip(f, m), hi], hx.at[hi, i], lx.at[hi, i]))
    for cp in own:
        cp.start()
    pl.semaphore_wait(barrier, len(others) + nz - 1)

    def last(hi):
        return first_copies(hi, fs, f, lambda g: g_ref.at[final, g, hi], lambda i: rx.at[hi, i], xs.at[hi], xr.at[hi])

    def later_rest(e, hi, stage):
        return later_copies(hi, stage, fs, f, lambda i: to_ref.at[e, hi, i], lambda i: rno.at[e, hi, i], os.at[e, hi], orr.at[e, hi])

    def later(j, hi, stage):
        held = (lambda i: tl_ref.at[j, hi, i]) if j < len(late) else (lambda i: hx.at[hi, i])
        return later_copies(hi, stage, fs, f, held, lambda i: rn.at[j, hi, i], ns.at[j, hi], nr.at[j, hi])

    def begin(copies):
        for cp in copies:
            cp.start()
    def reduce_last():
        for cp in own:
            cp.wait()
        for hi in range(2):
            for cp in last(hi):
                cp.wait_recv()
            hx[hi] = add_low(hx[hi], rx[hi])
            if stages > 1:
                begin(later(len(late), hi, 1))

    def reduce_more(copies, held, got, done):
        for stage in range(1, stages):
            keep = fs >> (stage + 1)
            base = fs // 2 - (fs >> stage)
            for cp in copies(stage):
                cp.wait_recv()
            if stage + 1 == stages:
                done(add_low(held[0], got[base]))
            else:
                held[:keep] = add_low(held[:keep], got[base:base + keep])
                begin(copies(stage + 1))
        if stages == 1:
            done(held[0])

    def put(t, hi, where):
        def done(value):
            tw[t, hi, :, where] = value
        return done

    def reduce_rest():
        for hi in range(2):
            for e in range(len(early)):
                reduce_more(lambda stage: later_rest(e, hi, stage), to_ref.at[e, hi], rno.at[e, hi], put(early[e], hi, rest))
            for j, t in enumerate(late + (final,)):
                held = tl_ref.at[j, hi] if j < len(late) else hx.at[hi]
                reduce_more(lambda stage: later(j, hi, stage), held, rn.at[j, hi], put(t, hi, slice(None)))

    def cross(t):
        return remote(snd.at[t], sib.at[t], bs.at[t], br.at[t], ctx=o)
    events = line_events(nz)

    def event(i):
        way = at_place(z, [events[zz][i][0] for zz in range(nz)])
        t = at_place(z, [events[zz][i][1] for zz in range(nz)])
        arrives = jnp.where(way == 0, z > 0, z < nz - 1)
        to = jnp.where(way == 0, jnp.minimum(z + 1, nz - 1), jnp.maximum(z - 1, 0))
        slot = jnp.where((way == 1) & (t == to), nz, t)
        return t, arrives, to, slot

    def rows_copy(i):
        t, _, to, slot = event(i)
        return remote(snd.at[t], ru.at[slot], us.at[i], ur.at[slot], tp=to)

    def rows_event(i):
        t, arrives, _, _ = event(i)
        cross(t).wait()

        @pl.when(arrives)
        def _():
            remote(snd.at[t], ru.at[t], us.at[i], ur.at[t], ctx=o).wait_recv()
            snd[t] = (pa[t] + sib[t].astype(F32) + ru[t].astype(F32)).astype(BF16)

        @pl.when(jnp.logical_not(arrives))
        def _():
            snd[t] = (pa[t] + sib[t].astype(F32)).astype(BF16)
        rows_copy(i).start()

    def weights(r):
        return pl.ds(pl.multiple_of(r * shard, shard), shard)

    def project(t):
        snd[t] = dot(d_ref[o * nz + t], wall_ref[...], NT).astype(BF16)
        cross(t).start()
        pa[t] = dot(d_ref[c * nz + t], wall_ref[...], NT)

    @pl.loop(0, nz)
    def _(i):
        t = z
        for k in range(nz - 1):
            t = jnp.where(i == k, event(k)[0], t)
        project(t)

        @pl.when(i == 0)
        def _():
            for cp in fills[:2]:
                cp.wait()
            for hi in range(2):
                begin(last(hi))
                if stages > 1:
                    for e in range(len(early)):
                        begin(later_rest(e, hi, 1))
                    for j in range(len(late)):
                        begin(later(j, hi, 1))

        @pl.when((i == 1) & jnp.logical_not(event(0)[1]))
        def _():
            rows_event(0)
    for cp in fills[2:]:
        cp.wait()
    wq[...] = jnp.zeros_like(wq)

    @pl.loop(0, nc * nz)
    def _(s):
        wq[...] += dot(a_ref[s], d_ref[s], TN)
    rq[me] = wq[weights(me)].astype(BF16)
    for i, (df, dc) in enumerate(others):
        tf, tc = lax.rem(f + df, fs), lax.rem(c + dc, nc)
        sc_[i] = wq[weights(tf * nc + tc)].astype(BF16)
        remote(sc_.at[i], rq.at[me], qs.at[i], qr.at[me], fsdp=tf, ctx=tc).start()
    pl.when(event(0)[1])(lambda: rows_event(0))
    for e in range(len(early)):
        tw[early[e], :, :, :cut] = te_ref[e]

    @pl.when(z == 1)
    def _():
        rw[nz - 1, :, :, :cut] = ch_ref[...]

    @pl.when(z == nz - 2)
    def _():
        rw[0, :, :, :cut] = ch_ref[...]
    reduce_last()
    for i in range(1, nz - 1):
        rows_event(i)

    reduce_rest()
    firsts = ((z == 0), (z == nz - 1))

    def grads_copy(i, part=None):
        t, _, to, slot = event(i)
        src, dst = (tw.at[t], rw.at[slot]) if part is None else (tw.at[t, :, :, part], rw.at[slot, :, :, part])
        return remote(src, dst, vs.at[i], vr.at[slot], tp=to)

    def grads_came(i, t, part=None):
        src, dst = (tw.at[t], rw.at[t]) if part is None else (tw.at[t, :, :, part], rw.at[t, :, :, part])
        remote(src, dst, vs.at[i], vr.at[t], ctx=o).wait_recv()

    def leads(i):
        t = event(i)[0]
        return ((z == 0) & (t == nz - 1)) | ((z == nz - 1) & (t == 0))

    def follows(i):
        t = event(i)[0]
        return ((z == 1) & (t == nz - 1)) | ((z == nz - 2) & (t == 0))

    def grads_event(i):
        t, arrives, _, _ = event(i)

        @pl.when(arrives)
        def _():
            pl.when(follows(i))(lambda: grads_came(i, t, rest))
            pl.when(jnp.logical_not(follows(i)))(lambda: grads_came(i, t))
            tw[t] = add_low(tw[t], rw[t])
        pl.when(leads(i))(lambda: grads_copy(i, rest).start())
        pl.when(jnp.logical_not(leads(i)))(lambda: grads_copy(i).start())
    grads_event(0)

    def rows_arrival(way):
        slot = nz if way else z
        return remote(snd.at[0], ru.at[slot], us.at[0], ur.at[slot], ctx=o)

    cross(z).wait()
    pa[z] += sib[z].astype(F32)

    @pl.when(z > 0)
    def _():
        rows_arrival(0).wait_recv()
        pa[z] += ru[z].astype(F32)

    @pl.when(z < nz - 1)
    def _():
        rows_arrival(1).wait_recv()
        pa[z] += ru[nz].astype(F32)
    da = pa[z]
    x = x_ref[...].astype(F32)
    inv = lax.rsqrt(jnp.mean(x * x, axis=-1, keepdims=True) + EPS)
    n = x * inv
    sc = da * gain_ref[...]
    ig_ref[...] = dh_ref[...] + inv * (sc - n * jnp.mean(sc * n, axis=-1, keepdims=True))
    gx[z, 0:1] = jnp.sum(da * n, axis=0, keepdims=True)
    gx[z, 1:2] = fg_ref[...]
    gx[z, 2:3] = jnp.concatenate([qgg_ref[...], kgg_ref[...]] + [jnp.zeros((1, width - 2 * HEAD), F32)], axis=1)
    gx[z, 3:] = jnp.zeros_like(gx[z, 3:])
    for dz in range(1, nz):
        to = lax.rem(z + dz, nz)
        remote(gx.at[z], gx.at[z], hs.at[dz - 1], hr.at[z], tp=to).start()
    for i in range(1, nz - 1):
        grads_event(i)

    for i, (df, dc) in enumerate(others):
        src = lax.rem(f + df, fs) * nc + lax.rem(c + dc, nc)
        remote(sc_.at[0], rq.at[src], qs.at[i], qr.at[src], ctx=o).wait_recv()
    for cc in range(nc):
        total = rq[cc].astype(F32)
        for ff in range(1, fs):
            total += rq[ff * nc + cc].astype(F32)
        dwq_ref[cc] = total

    def grads_arrival(way):
        slot = nz if way else z
        return remote(tw.at[0], rw.at[slot], vs.at[0], vr.at[slot], ctx=o)

    for dz in range(1, nz):
        src = lax.rem(z + dz, nz)
        remote(gx.at[src], gx.at[src], hs.at[dz - 1], hr.at[src], tp=src).wait_recv()
    total = gx[0]
    for zz in range(1, nz):
        total += gx[zz]
    gy[me] = total
    for i, (df, dc) in enumerate(others):
        remote(gy.at[me], gy.at[me], hs.at[nz - 1 + i], hr.at[nz + me], fsdp=lax.rem(f + df, fs), ctx=lax.rem(c + dc, nc)).start()

    fin[...] = tw[z].astype(F32)

    @pl.when(z > 0)
    def _():
        grads_arrival(0).wait_recv()
        fin[...] += rw[z].astype(F32)

    @pl.when(z < nz - 1)
    def _():
        grads_arrival(1).wait_recv()
        fin[...] += rw[nz].astype(F32)
    share[0] = fin[o].astype(BF16)
    swap = remote(share.at[0], share.at[1], cs.at[0], cr.at[0], ctx=o)
    swap.start()
    dwz_ref[c] = fin[c]

    for i, (df, dc) in enumerate(others):
        src = lax.rem(f + df, fs) * nc + lax.rem(c + dc, nc)
        remote(gy.at[src], gy.at[src], hs.at[nz - 1 + i], hr.at[nz + src], ctx=o).wait_recv()
    total = gy[0]
    for r in range(1, fs * nc):
        total += gy[r]
    gains_ref[...] = total
    swap.wait_recv()
    dwz_ref[o] = share[1].astype(F32)

    swap.wait_send()
    for i in range(nz - 1):
        rows_copy(i).wait_send()
        pl.when(leads(i))(lambda: grads_copy(i, rest).wait_send())
        pl.when(jnp.logical_not(leads(i)))(lambda: grads_copy(i).wait_send())
    for i in range(nz - 1):
        remote(gx.at[0], gx.at[0], hs.at[i], hr.at[0], ctx=o).wait_send()
    for i in range(len(others)):
        remote(sc_.at[0], rq.at[0], qs.at[i], qr.at[0], ctx=o).wait_send()
        remote(gy.at[0], gy.at[0], hs.at[nz - 1 + i], hr.at[nz], ctx=o).wait_send()
    for hi in range(2):
        for cp in last(hi):
            cp.wait_send()
        for stage in range(1, stages):
            for e in range(len(early)):
                for cp in later_rest(e, hi, stage):
                    cp.wait_send()
            for j in range(len(late) + 1):
                for cp in later(j, hi, stage):
                    cp.wait_send()


def finish_call(dims, d, wall, a, x, dh, gain, te, to, tl, ch, fg, qgg, kgg, g):
    fs, nc, nz = dims
    rows, width = x.shape
    shard, cols = g.shape[3:]
    cut = te.shape[3]
    early = te.shape[0]
    half, more = fs // 2, max(fs // 2 - 1, 1)
    proj = wall.shape[1]
    late = len(late_parts(nz))
    n = fs * nc
    DMA = pltpu.SemaphoreType.DMA
    V = pltpu.VMEM
    return pl.pallas_call(
        lambda *refs: finish_kernel(dims, cut, *refs),
        out_shape=(
            jax.ShapeDtypeStruct((rows, width), F32),
            jax.ShapeDtypeStruct((nc, width // n, proj), F32),
            jax.ShapeDtypeStruct((nc, shard, cols), F32),
            jax.ShapeDtypeStruct((8, width), F32),
        ),
        in_specs=[VMEM_SPEC] * 2 + [ANY_SPEC] * 3 + [VMEM_SPEC] + [ANY_SPEC] * 4 + [VMEM_SPEC] * 3 + [ANY_SPEC],
        out_specs=(VMEM_SPEC,) * 4,
        scratch_shapes=[
            V(a.shape, BF16), V(x.shape, BF16), V(dh.shape, F32), V(te.shape, BF16), V(to.shape, BF16), V(tl.shape, BF16), V(ch.shape, BF16),
            V((nz, rows, width), F32), V((nz, rows, width), BF16), V((nz + 1, rows, width), BF16),
            V((nz, rows, width), BF16),
            V((n, width // n, proj), BF16), V((width, proj), F32),
            V((nz + 1, 2, shard, cols), BF16), V((nz, 2, shard, cols), BF16),
            V((2, half, shard, cols), BF16), V((2, half, shard, cols), BF16),
            V((early, 2, more, shard, cols - cut), BF16), V((late, 2, more, shard, cols), BF16),
            V((2, shard, cols), F32), V((2, shard, cols), BF16),
            V((n - 1, width // n, proj), BF16), V((nz, 8, width), F32), V((n, 8, width), F32),
            DMA((7,)), DMA((2, half)), DMA((2, half)), DMA((2, half)), DMA((early, 2, more)), DMA((early, 2, more)),
            DMA((nz,)), DMA((nz,)), DMA((nz - 1,)), DMA((nz + 1,)),
            DMA((n - 1,)), DMA((n,)), DMA((nz - 1,)), DMA((nz + 1,)),
            DMA((late, 2, max(fs // 2 - 1, 1))), DMA((late, 2, max(fs // 2 - 1, 1))),
            DMA((1,)), DMA((1,)), DMA((nz - 1 + n - 1,)), DMA((nz + n,)),
        ],
        compiler_params=pltpu.CompilerParams(collective_id=4, has_side_effects=True, vmem_limit_bytes=VMEM_LIMIT),
        cost_estimate=pl.CostEstimate(flops=2 * 4 * 2**30, bytes_accessed=40 * 2**20, transcendentals=0),
    )(d, wall, a, x, dh, gain, te, to, tl, ch, fg, qgg, kgg, g)
def unpack_kernel(parts, result_ref, ig_ref, gains_ref, dwq_ref, dwz_ref, *outs):
    outs[0][...] = result_ref[...]
    outs[1][...] = ig_ref[...]
    outs[2][...] = gains_ref[0:1]
    outs[3][...] = gains_ref[1:2]
    outs[4][...] = gains_ref[2:3, :HEAD]
    outs[5][...] = gains_ref[2:3, HEAD:2 * HEAD]
    for (which, at, step, turned), out in zip(parts, outs[6:]):
        ref = (dwq_ref, dwz_ref)[which]
        value = jnp.concatenate([ref[cc, :, at:at + step] for cc in range(ref.shape[0])], axis=1)
        out[...] = value.T if turned else value


def unpack_call(result, ig, gains, dwq, dwz, hidden, q_cols):
    nc, shard, _ = dwq.shape
    parts = ((0, 0, q_cols, False), (0, q_cols, HEAD, False), (0, q_cols + HEAD, HEAD, False),
             (1, 3 * hidden, q_cols, True), (1, 0, hidden, False), (1, hidden, hidden, False), (1, 2 * hidden, hidden, True))
    width = gains.shape[1]
    shapes = [(shard, nc * step)[::-1] if turned else (shard, nc * step) for _, _, step, turned in parts]
    return pl.pallas_call(
        lambda *refs: unpack_kernel(parts, *refs),
        out_shape=[jax.ShapeDtypeStruct(result.shape, BF16), jax.ShapeDtypeStruct(ig.shape, F32)]
        + [jax.ShapeDtypeStruct((1, n), F32) for n in (width, width, HEAD, HEAD)]
        + [jax.ShapeDtypeStruct(shape, F32) for shape in shapes],
        in_specs=[VMEM_SPEC] * 5,
        out_specs=[VMEM_SPEC] * 13,
        compiler_params=pltpu.CompilerParams(vmem_limit_bytes=VMEM_LIMIT),
    )(result, ig, gains, dwq, dwz)


def on_device(dims, tokens, out_grad, block_slot, attn_gain, ffn_gain, query_gain, key_norm_gain,
              w_query, key_weight, value_weight, w_out, w_gate, w_up, w_down):
    fs, nc, nz = dims
    rows, width = tokens.shape
    shard = w_query.shape[0]
    block_ids = block_slot[0]
    cos, sins = rope_tables()
    hidden, q_cols = w_gate.shape[1] // nc, w_query.shape[1] // nc
    ag, fg = attn_gain[None], ffn_gain[None]
    qg, kg = query_gain[None], key_norm_gain[None]
    weights = (w_query, key_weight, value_weight, w_gate, w_up, w_down, w_out)
    a, q, k, v, pre, wall, w, dyp = gather_call(dims, block_ids, tokens, out_grad, ag, weights, cos, sins, qg, kg)
    blocks = lambda t: t.reshape(BLOCKS, BLOCK, -1)
    q, k, v, pre = blocks(q), blocks(k), blocks(v), blocks(pre)
    w, mixed, o, logs = attend_call(dims, 2 * hidden, block_ids, q, k, v, w, rows)
    cols = w.shape[4]
    result, dh, ffn_part, do, dr, g, re = feed_call(dims, tokens, dyp, mixed, w.reshape(nz, width, cols), fg)
    g = g.reshape(nz, fs, nc, shard, cols)
    dr = dr.reshape(nz, nc, rows // UNIT, UNIT, q_cols - HEAD)
    d, te, to, tl, ch, q_part, k_part = attend_back_call(
        dims, block_ids, q, k, v, blocks(o), logs, blocks(do), pre, cos, sins, qg, kg, re, dr, g)
    input_grad, dwq, dwz, gains = finish_call(
        dims, d.reshape(nc * nz, rows, -1), wall.reshape(width, -1), a, tokens, dh, ag, te, to, tl, ch, ffn_part, q_part, k_part, g)
    outs = unpack_call(result, input_grad, gains, dwq, dwz, hidden, q_cols)
    return tuple(t[0] if 2 <= i < 6 else t for i, t in enumerate(outs))


def solution(mesh):
    dims = (mesh.shape["fsdp"], mesh.shape["ctx"], mesh.shape["tp"])
    everything, weights = ("fsdp", "ctx", "tp"), ("fsdp", "ctx")
    split, turned = P(weights, "tp"), P("tp", weights)
    return jax.shard_map(
        lambda *args: on_device(dims, *args),
        mesh=mesh,
        in_specs=(P(everything, None), P(everything, None), P("fsdp", None), P(), P(), P(), P(), split, split, split, turned, split, split, turned),
        out_specs=(P(everything, None), P(everything, None), P(), P(), P(), P(), split, split, split, turned, split, split, turned),
        check_vma=False,
    )
```
